128 devices in a mesh: em: 8 (over z, core), th: 16 (over y, x).
Axes of the slice: x: 4, y: 4, z: 4, core: 2. Of those that a mesh axis runs over, the one named last changes fastest.
Arguments:
- e_real: float32 [131072, 128], P(('em', 'th')), may hold values from -6 to 6
- e_imag: float32 [131072, 128], P(('em', 'th')), may hold values from -6 to 6
- sigma_em: float32 [131072, 128], P(('em', 'th')), may hold values from 0.5 to 2
- temp_coef: float32 [131072, 128], P(('em', 'th')), may hold values from 0.05 to 0.5
- dest_dev: int32 [131072, 1], P(('em', 'th')), may hold values from 0 to 127; in each aligned block of 1024 rows (0 to 1023, 1024 to 2047, ...) at most 16 rows name the same one
- dest_tile: int32 [131072, 1], P(('em', 'th')), may hold values from 0 to 1023
- t_old: float32 [4096, 4096], P('th', 'em'), may hold values from 0.5 to 2
- heat_cap: float32 [4096, 4096], P('th', 'em'), may hold values from 0.05 to 0.5
- conduct: float32 [4096, 4096], P('th', 'em'), may hold values from 0.5 to 2
Outputs:
- temperature: float32 [4096, 4096], P('th', 'em')
- sigma_new: float32 [131072, 128], P(('em', 'th'))
The draws below stay inside these ranges and needn't reach their ends.
Inputs may be any that keep to these rules, and one draw needn't show every extreme that they name: `dest_dev`: in the rows of one device (aligned blocks of 1024 rows), no owner is named by more than 16 rows, a bound that some block reaches.
All inputs are finite; a program needn't handle non-finite values.
Results may differ from the reference program's by a relative error of at most 0.00002.
Values sent between devices are 32-bit elements; how exact they have to be, the bound alone decides.
No kernel may reach another device: no remote copies, remote signals or barrier semaphores. Data moves between devices by JAX's collectives and lax.ppermute only.
A program may use at most 64 MiB of HBM per device.

```python
import math
import jax
import jax.numpy as jnp
import numpy as np

SRC_DEV = 1024
CX = 256
CY = 512
SWEEPS = 3
CAP = 16
TILES = 1024
SRC_ALL = 131072
GX = 4096
GY = 4096
N_EM = 8
N_TH = 16
DEVICES = 128


def set_ends(array, stream_key, smallest, top_value):
    dims = array.shape
    spot = [jax.random.randint(jax.random.fold_in(stream_key, axis), (), 0, dims[axis]) for axis in range(len(dims))]
    array = array.at[tuple(spot)].set(smallest)
    longest = dims.index(max(dims))
    spot[longest] = (spot[longest] + 1) % dims[longest]
    return array.at[tuple(spot)].set(top_value)


def block_levels(key, extent, shards, smallest, high):
    loudness, own = 1.0, jax.random.fold_in(key, 6)
    for position, blocks in shards:
        draws = jnp.exp(jax.random.uniform(jax.random.fold_in(own, position), (blocks,), jnp.float32, smallest / len(shards), high / len(shards)))
        loudness = loudness * jnp.repeat(draws, extent[position] // blocks).reshape([-1 if axis == position else 1 for axis in range(len(extent))])
    return loudness


def assign_block(stream_key, own, number, rows, number_of, top, bound, lean):
    sequence = jax.random.permutation(stream_key, number_of)
    heavy_load, ordinary = portions_of(number_of, rows * top, bound, lean, True), portions_of(number_of, rows * top, bound, lean, False)
    places = jnp.arange(number_of)

    def named(lengths, offset_by):
        used = int((lengths > 0).sum())
        fixed = max(1, used // 4)
        shifted = fixed + (places - fixed + offset_by * (used - fixed)) % max(1, number_of - fixed)
        return jnp.zeros((number_of,), jnp.int32).at[sequence[jnp.where(places < fixed, places, shifted)]].set(jnp.asarray(lengths, jnp.int32))

    lengths = jnp.where(number % 4 == 0, named(heavy_load, number // 4), named(ordinary, number - number // 4 - 1))
    mixed = jax.random.permutation(jax.random.fold_in(own, 3), number_of)
    giver, receiver = mixed[0:number_of // 2 * 2:2], mixed[1:number_of // 2 * 2:2]
    slack = jnp.minimum(lengths[giver] - 1, bound - lengths[receiver]) // 2
    slack = jnp.where((giver == sequence[0]) | (receiver == sequence[0]) | (lengths[receiver] == 0), 0, jnp.maximum(slack, 0))
    shifted = jax.random.randint(jax.random.fold_in(own, 4), (number_of // 2,), 0, 1 << 20) % (slack + 1)
    lengths = lengths.at[giver].add(-shifted).at[receiver].add(shifted)
    members = jnp.searchsorted(jnp.cumsum(lengths), jnp.arange(rows * top), side="right").astype(jnp.int32)
    listing = members.reshape(top, rows).T
    listing = listing[jax.random.permutation(jax.random.fold_in(own, 1), rows)]
    offset_by = jax.random.randint(jax.random.fold_in(own, 2), (rows, 1), 0, top)
    return jnp.take_along_axis(listing, (jnp.arange(top)[None, :] + offset_by) % top, axis=1)


def portions_of(count, total, reach, lean, full):
    loads = [(1 << 20) // math.isqrt(standing ** lean) + 1 for standing in range(1, count + 1)]
    largest = reach if full else min(reach, max(-(-total // count), total * loads[0] // sum(loads)))
    least = 1 if total - largest >= count - 1 else 0
    holding, surplus = [largest] + [least] * (count - 1), total - largest - least * (count - 1)
    while surplus > 0:
        free = [i for i in range(1, count) if holding[i] < largest] or [i for i in range(1, count) if holding[i] < reach]
        whole, left = sum([loads[i] for i in free]), surplus
        for i in free:
            extra = min(reach - holding[i], max(1, left * loads[i] // whole), surplus)
            holding[i] = holding[i] + extra
            surplus = surplus - extra
    return np.array(holding)


def gaussian(key, extent, scale, reach, shards=(), dtype=jnp.bfloat16):
    entries = jax.random.normal(key, extent, jnp.float32) * scale
    if len(shards) > 0:
        entries = block_levels(key, extent, shards, -0.22, 0.18) * entries
    return jnp.clip(entries, min=-reach, max=reach).astype(dtype)


def setup_inputs(seed: int = 0) -> dict:
    streams_of = jax.random.split(jax.random.key(seed), 10)
    e_real = gaussian(streams_of[0], (SRC_ALL, 128), 1.0, 6.0, ((0, 128),), jnp.float32)
    e_imag = gaussian(streams_of[1], (SRC_ALL, 128), 1.0, 6.0, ((0, 128),), jnp.float32)
    sigma_em = jnp.clip(jnp.exp(math.log(2.0) - 1.3862944 * jax.random.uniform(streams_of[2], (SRC_ALL, 128), jnp.float32) ** block_levels(streams_of[2], (SRC_ALL, 128), ((0, 128),), -0.2, 0.2)), 0.5, 2.0)
    temp_coef = jnp.clip(jnp.exp(math.log(0.5) - 2.3025851 * jax.random.uniform(streams_of[3], (SRC_ALL, 128), jnp.float32) ** block_levels(streams_of[3], (SRC_ALL, 128), ((0, 128),), -0.2, 0.2)), 0.05, 0.5)
    dest_dev_keys = jax.random.split(jax.random.fold_in(streams_of[4], 1), SRC_ALL // SRC_DEV)
    dest_dev_turns = jax.random.permutation(jax.random.fold_in(streams_of[4], 3), SRC_ALL // SRC_DEV)
    dest_dev = jax.vmap(lambda own, number: assign_block(jax.random.fold_in(streams_of[4], 2), own, number, SRC_DEV, DEVICES, 1, CAP, 1))(dest_dev_keys, dest_dev_turns).reshape((SRC_ALL, 1))
    dest_tile = set_ends(jax.random.randint(streams_of[5], (SRC_ALL, 1), 0, TILES), jax.random.fold_in(streams_of[5], 1), 0, TILES - 1).astype(jnp.int32)
    t_old = jnp.clip(0.5 + 1.5 * jax.random.uniform(streams_of[6], (GX, GY), jnp.float32) ** block_levels(streams_of[6], (GX, GY), ((0, 16), (1, 8)), -0.2, 0.2), 0.5, 2.0)
    heat_cap = jnp.clip(jnp.exp(math.log(0.5) - 2.3025851 * jax.random.uniform(streams_of[7], (GX, GY), jnp.float32) ** block_levels(streams_of[7], (GX, GY), ((0, 16), (1, 8)), -0.2, 0.2)), 0.05, 0.5)
    conduct = jnp.clip(jnp.exp(math.log(2.0) - 1.3862944 * jax.random.uniform(streams_of[8], (GX, GY), jnp.float32) ** block_levels(streams_of[8], (GX, GY), ((0, 16), (1, 8)), -0.2, 0.2)), 0.5, 2.0)
    return dict(e_real=e_real, e_imag=e_imag, sigma_em=sigma_em, temp_coef=temp_coef, dest_dev=dest_dev, dest_tile=dest_tile, t_old=t_old, heat_cap=heat_cap, conduct=conduct)


def reference(e_real, e_imag, sigma_em, temp_coef, dest_dev, dest_tile, t_old, heat_cap, conduct):
    devices = N_EM * N_TH
    tiles = CX * CY // 128
    loss = sigma_em * (e_real * e_real + e_imag * e_imag)
    target = (dest_dev[:, 0] * tiles + dest_tile[:, 0]).astype(jnp.int32)
    heat_tiles = jax.ops.segment_sum(loss, target, num_segments=devices * tiles)
    heat = heat_tiles.reshape(N_EM, N_TH, CX, CY).transpose(1, 2, 0, 3).reshape(N_TH * CX, N_EM * CY)
    rhs = heat_cap * t_old + heat
    diag = heat_cap + 4.0 * conduct
    temp = t_old
    for sweep in range(SWEEPS):
        padded = jnp.pad(temp, 1)
        beside_all = padded[2:, 1:-1] + padded[:-2, 1:-1] + padded[1:-1, 2:] + padded[1:-1, :-2]
        temp = (rhs + conduct * beside_all) / diag
    back = temp.reshape(N_TH, CX, N_EM, CY).transpose(2, 0, 1, 3).reshape(devices * tiles, 128)
    hot = back[target]
    return temp, sigma_em / (1.0 + temp_coef * hot)
```

```python
import functools
import jax
import jax.numpy as jnp
from jax import lax
from jax.experimental import pallas as pl
from jax.experimental.pallas import tpu as pltpu
from jax.sharding import PartitionSpec as P

F32 = jnp.float32
BF16 = jnp.bfloat16
I32 = jnp.int32
RIM = 8
SIDE = 128


def iota(shape, dim):
    return lax.broadcasted_iota(I32, shape, dim)


def halves(x):
    high = x.astype(BF16)
    low = (x - high.astype(F32)).astype(BF16)
    return high, low


def select(mask):
    return jnp.where(mask, 1.0, 0.0).astype(BF16)


def joined(y):
    return y[:, :128] + y[:, 128:]


def route_kernel(owners, slots, rows, dev_ref, tile_ref, er_ref, ei_ref, sg_ref, send_ref, slot_ref, pair_ref):
    count = er_ref.shape[0]
    blocks = count // 128
    er = er_ref[...]
    ei = ei_ref[...]
    high, low = halves(sg_ref[...] * (er * er + ei * ei))
    pair_ref[:, :128] = high
    pair_ref[:, 128:] = low
    dev = dev_ref[...]
    tile = tile_ref[...]
    tile = (tile & 3) * rows + (tile >> 2)
    hits = [jnp.broadcast_to(dev[b : b + 1], (owners, 128)) == iota((owners, 128), 0) for b in range(blocks)]
    ahead = select(iota((128, 256), 0) < iota((128, 256), 1))
    sums = jnp.dot(
        jnp.concatenate([select(h) for h in hits], axis=0), ahead, preferred_element_type=F32
    )
    carry = jnp.zeros((owners, 128), F32)
    ranks = []
    for b in range(blocks):
        part = sums[b * owners : (b + 1) * owners]
        ranks.append(
            jnp.sum(jnp.where(hits[b], part[:, :128] + carry, 0.0), axis=0, keepdims=True)
        )
        carry = carry + part[:, 128:]
    rank = jnp.concatenate(ranks, axis=0).astype(I32)
    slot_ref[...] = dev * slots + rank
    line = lambda x: jnp.concatenate([x[b : b + 1] for b in range(blocks)], axis=1)
    place = line(dev * (slots + 1) + rank)
    step = 4 * 136
    for start in range(0, owners * (slots + 1), step):
        mask = jnp.broadcast_to(place, (step, count)) == iota((step, count), 0) + start
        send_ref[start : start + step, :] = joined(
            jnp.dot(select(mask), pair_ref[...], preferred_element_type=F32)
        )
    hit = jnp.concatenate(hits, axis=1)
    tiles = line(tile)
    upper = jnp.where(hit, jnp.broadcast_to(tiles >> 5, (owners, count)), 0)
    lower = jnp.where(hit, jnp.broadcast_to(tiles & 31, (owners, count)), 0)
    numbers = jnp.concatenate([upper, lower], axis=0).astype(F32).astype(BF16)
    which = select(jnp.broadcast_to(line(rank), (128, count)) == iota((128, count), 0))
    ids = lax.dot_general(
        numbers, which, (((1,), (1,)), ((), ())), preferred_element_type=F32
    )
    send_ref[pl.ds(slots, owners, stride=slots + 1), :] = ids[:owners] * 32.0 + ids[owners:]


def route(dev, tile, er, ei, sg, owners, slots, rows):
    count = er.shape[0]
    return pl.pallas_call(
        functools.partial(route_kernel, owners, slots, rows),
        out_shape=(
            jax.ShapeDtypeStruct((owners * (slots + 1), 128), F32),
            jax.ShapeDtypeStruct((count // 128, 128), I32),
        ),
        scratch_shapes=[pltpu.VMEM((count, 256), BF16)],
        compiler_params=pltpu.CompilerParams(vmem_limit_bytes=32 << 20),
        name="route",
    )(dev.reshape(count // 128, 128), tile.reshape(count // 128, 128), er, ei, sg)


def heat_kernel(owners, slots, got_ref, heat_ref, ids_ref, pair_ref):
    rows = heat_ref.shape[0]
    groups = heat_ref.shape[1] // 128
    ids = got_ref[pl.ds(slots, owners, stride=slots + 1), :].astype(I32)
    ids_ref[...] = ids
    flat = ids.T
    for r in range(slots):
        high, low = halves(got_ref[pl.ds(r, owners, stride=slots + 1), :])
        pair_ref[r * owners : (r + 1) * owners, :128] = high
        pair_ref[r * owners : (r + 1) * owners, 128:] = low
    line = jnp.concatenate([flat[r : r + 1] for r in range(slots)], axis=1)
    for q in range(groups):
        shape = (rows, owners * slots)
        mask = jnp.broadcast_to(line, shape) == iota(shape, 0) + q * rows
        heat_ref[:, q * 128 : (q + 1) * 128] = joined(
            jnp.dot(select(mask), pair_ref[...], preferred_element_type=F32)
        )


def gather_heat(got, owners, slots, rows, cols):
    return pl.pallas_call(
        functools.partial(heat_kernel, owners, slots),
        out_shape=(
            jax.ShapeDtypeStruct((rows, cols), F32),
            jax.ShapeDtypeStruct((owners, 128), I32),
        ),
        scratch_shapes=[pltpu.VMEM((owners * slots, 256), BF16)],
        compiler_params=pltpu.CompilerParams(vmem_limit_bytes=32 << 20),
        name="heat",
    )(got)


def around(x):
    rows, cols = x.shape
    return (
        pltpu.roll(x, 1, 0) + pltpu.roll(x, rows - 1, 0)
    ) + (pltpu.roll(x, 1, 1) + pltpu.roll(x, cols - 1, 1))


def base_kernel(sweeps, t_ref, hc_ref, c_ref, base_ref, a_ref, g_ref):
    hc = hc_ref[...]
    c = c_ref[...]
    diag = hc + 4.0 * c
    g = jnp.where(diag > 0.0, 1.0 / jnp.where(diag > 0.0, diag, 1.0), 0.0)
    g_ref[...] = g
    a_ref[...] = c * g
    r0 = hc * t_ref[...] * g
    temp = t_ref[...]
    for _ in range(sweeps):
        temp = r0 + a_ref[...] * around(temp)
    base_ref[...] = temp


def base(t, hc, c, sweeps):
    shape = jax.ShapeDtypeStruct(t.shape, F32)
    return pl.pallas_call(
        functools.partial(base_kernel, sweeps),
        out_shape=(shape, shape, shape),
        compiler_params=pltpu.CompilerParams(vmem_limit_bytes=32 << 20),
        name="base",
    )(t, hc, c)


def solve_kernel(sweeps, owners, slots, heat_ref, base_ref, a_ref, g_ref, ids_ref, temp_ref, reply_ref, pair_ref):
    rows, cols = temp_ref.shape
    h = heat_ref[...] * g_ref[...]
    u = h
    for _ in range(sweeps - 1):
        u = h + a_ref[...] * around(u)
    temp = (base_ref[...] + u)[RIM : RIM + rows, SIDE : SIDE + cols]
    temp_ref[...] = temp
    groups = cols // 128
    for q in range(groups):
        high, low = halves(temp[:, q * 128 : (q + 1) * 128])
        pair_ref[q * rows : (q + 1) * rows, :128] = high
        pair_ref[q * rows : (q + 1) * rows, 128:] = low
    tiles = groups * rows
    ids = ids_ref[...]
    for r in range(0, slots, 4):
        column = jnp.concatenate(
            [jnp.broadcast_to(ids[:, k : k + 1], (owners, 128)) for k in range(r, r + 4)], axis=0
        )
        mask = jnp.concatenate(
            [column == iota((4 * owners, 128), 1) + 128 * k for k in range(tiles // 128)], axis=1
        )
        got = joined(jnp.dot(select(mask), pair_ref[...], preferred_element_type=F32))
        for k in range(4):
            reply_ref[pl.ds(r + k, owners, stride=slots), :] = got[k * owners : (k + 1) * owners]


def solve(heat, base_t, a, g, ids, sweeps, owners, slots, rows, cols):
    return pl.pallas_call(
        functools.partial(solve_kernel, sweeps, owners, slots),
        out_shape=(
            jax.ShapeDtypeStruct((rows, cols), F32),
            jax.ShapeDtypeStruct((owners * slots, 128), F32),
        ),
        scratch_shapes=[pltpu.VMEM((rows * cols // 128, 256), BF16)],
        compiler_params=pltpu.CompilerParams(vmem_limit_bytes=32 << 20),
        name="solve",
    )(heat, base_t, a, g, ids)


def final_kernel(slot_ref, back_ref, sg_ref, tc_ref, out_ref, pair_ref):
    total = back_ref.shape[0]
    blocks = slot_ref.shape[0]
    high, low = halves(back_ref[...])
    pair_ref[:, :128] = high
    pair_ref[:, 128:] = low
    slot = slot_ref[...].T
    for b in range(0, blocks, 4):
        column = jnp.concatenate(
            [jnp.broadcast_to(slot[:, k : k + 1], (128, 128)) for k in range(b, b + 4)], axis=0
        )
        mask = jnp.concatenate(
            [column == iota((512, 128), 1) + 128 * k for k in range(total // 128)], axis=1
        )
        hot = joined(jnp.dot(select(mask), pair_ref[...], preferred_element_type=F32))
        span = slice(b * 128, b * 128 + 512)
        out_ref[span, :] = sg_ref[span, :] / (1.0 + tc_ref[span, :] * hot)


def final(slot, back, sg, tc):
    return pl.pallas_call(
        final_kernel,
        out_shape=jax.ShapeDtypeStruct(sg.shape, F32),
        scratch_shapes=[pltpu.VMEM((back.shape[0], 256), BF16)],
        compiler_params=pltpu.CompilerParams(vmem_limit_bytes=32 << 20),
        name="final",
    )(slot, back, sg, tc)


def swap(low_part, high_part, axis):
    count = lax.axis_size(axis)
    up = [(i, i + 1) for i in range(count - 1)]
    down = [(i + 1, i) for i in range(count - 1)]
    return lax.ppermute(high_part, axis, up), lax.ppermute(low_part, axis, down)


def widened(blocks, width):
    n = len(blocks)
    rows, cols = blocks[0].shape
    pack = lambda f: jnp.concatenate([f(x).T for x in blocks], axis=0)
    left, right = swap(pack(lambda x: x[:, :width]), pack(lambda x: x[:, cols - width :]), "em")
    wide = []
    for k, x in enumerate(blocks):
        lo = jnp.pad(left[k * width : (k + 1) * width].T, ((0, 0), (SIDE - width, 0)))
        hi = jnp.pad(right[k * width : (k + 1) * width].T, ((0, 0), (0, SIDE - width)))
        wide.append(jnp.concatenate([lo, x, hi], axis=1))
    pack = lambda f: jnp.concatenate([f(x) for x in wide], axis=0)
    above, below = swap(pack(lambda x: x[:width]), pack(lambda x: x[rows - width :]), "th")
    out = []
    for k, x in enumerate(wide):
        lo = jnp.pad(above[k * width : (k + 1) * width], ((RIM - width, 0), (0, 0)))
        hi = jnp.pad(below[k * width : (k + 1) * width], ((0, RIM - width), (0, 0)))
        out.append(jnp.concatenate([lo, x, hi], axis=0))
    return out


def exchanged(x, owners):
    rows = x.shape[0]
    x = x.reshape(owners, 1, rows // owners * 128)
    x = lax.all_to_all(x, ("em", "th"), split_axis=0, concat_axis=0, tiled=True)
    return x.reshape(rows, 128)


SWEEPS = 3


def local(e_real, e_imag, sigma_em, temp_coef, dest_dev, dest_tile, t_old, heat_cap, conduct):
    owners = lax.axis_size("em") * lax.axis_size("th")
    slots = 2 * e_real.shape[0] // owners
    rows, cols = t_old.shape
    send, slot = route(dest_dev, dest_tile, e_real, e_imag, sigma_em, owners, slots, rows)
    got = exchanged(send, owners)
    base_t, a, g = base(*widened([t_old, heat_cap, conduct], SWEEPS), SWEEPS)
    heat, ids = gather_heat(got, owners, slots, rows, cols)
    (heat,) = widened([heat], SWEEPS - 1)
    temp, reply = solve(heat, base_t, a, g, ids, SWEEPS, owners, slots, rows, cols)
    back = exchanged(reply, owners)
    return temp, final(slot, back, sigma_em, temp_coef)


def solution(mesh):
    tiles = P(("em", "th"), None)
    grid = P("th", "em")
    return jax.shard_map(
        local,
        mesh=mesh,
        in_specs=(tiles,) * 6 + (grid,) * 3,
        out_specs=(grid, tiles),
        check_vma=False,
    )
```

```python
import functools
import jax
import jax.numpy as jnp
from jax import lax
from jax.experimental import pallas as pl
from jax.experimental.pallas import tpu as pltpu
from jax.sharding import PartitionSpec as P

F32 = jnp.float32
BF16 = jnp.bfloat16
I32 = jnp.int32
RIM = 8
SIDE = 128


def iota(shape, dim):
    return lax.broadcasted_iota(I32, shape, dim)


def halves(x):
    high = x.astype(BF16)
    low = (x - high.astype(F32)).astype(BF16)
    return high, low


def select(mask):
    return jnp.where(mask, 1.0, 0.0).astype(BF16)


def joined(y):
    return y[:, :128] + y[:, 128:]


def route_kernel(owners, slots, rows, near, dev_hbm, tile_hbm, er_hbm, ei_hbm, sg_hbm, out_ref, slot_ref, dev_ref, tile_ref, er_ref, ei_ref, sg_ref, pair_ref, send_ref, ids_ref, rims_ref, sems, out_sems):
    count = er_ref.shape[0]
    blocks = count // 128
    copies = [
        pltpu.make_async_copy(source, target, sems.at[k])
        for k, (source, target) in enumerate(
            (
                (dev_hbm, dev_ref),
                (tile_hbm, tile_ref),
                (er_hbm, er_ref),
                (ei_hbm, ei_ref),
                (sg_hbm, sg_ref),
            )
        )
    ]
    for copy in copies:
        copy.start()
    copies[0].wait()
    copies[1].wait()
    dev = dev_ref[...]
    tile = tile_ref[...]
    tile = (tile & 3) * rows + (tile >> 2)
    hits = [jnp.broadcast_to(dev[b : b + 1], (owners, 128)) == iota((owners, 128), 0) for b in range(blocks)]
    ahead = select(iota((128, 256), 0) < iota((128, 256), 1))
    sums = jnp.dot(
        jnp.concatenate([select(h) for h in hits], axis=0), ahead, preferred_element_type=F32
    )
    carry = jnp.zeros((owners, 128), F32)
    ranks = []
    for b in range(blocks):
        part = sums[b * owners : (b + 1) * owners]
        ranks.append(
            jnp.sum(jnp.where(hits[b], part[:, :128] + carry, 0.0), axis=0, keepdims=True)
        )
        carry = carry + part[:, 128:]
    rank = jnp.concatenate(ranks, axis=0).astype(I32)
    slot_ref[...] = dev * slots + rank
    line = lambda x: jnp.concatenate([x[b : b + 1] for b in range(blocks)], axis=1)
    place = line(dev * (slots + 1) + rank)
    hit = jnp.concatenate(hits, axis=1)
    tiles = line(tile)
    upper = jnp.where(hit, jnp.broadcast_to(tiles >> 5, (owners, count)), 0)
    lower = jnp.where(hit, jnp.broadcast_to(tiles & 31, (owners, count)), 0)
    numbers = jnp.concatenate([upper, lower], axis=0).astype(F32).astype(BF16)
    which = select(jnp.broadcast_to(line(rank), (128, count)) == iota((128, count), 0))
    ids = lax.dot_general(
        numbers, which, (((1,), (1,)), ((), ())), preferred_element_type=F32
    )
    none = jnp.zeros((near, 128), F32)
    for ref in (ids_ref, rims_ref):
        ref[:near] = none
        ref[near + owners :] = none
    ids_ref[near : near + owners] = ids[:owners] * 32.0 + ids[owners:]
    for copy in copies[2:]:
        copy.wait()
    er = er_ref[...]
    ei = ei_ref[...]
    high, low = halves(sg_ref[...] * (er * er + ei * ei))
    pair_ref[:, :128] = high
    pair_ref[:, 128:] = low
    part = 2 * near
    step = part * (slots + 1)
    lane = iota((part, 128), 1)
    own_at, left_at, right_at = (4 * slots + k * slots for k in range(3))
    writes = []
    for c in range(owners // part + 1):
        if c < owners // part:
            mask = jnp.broadcast_to(place, (step, count)) == iota((step, count), 0) + c * step
            send_ref[c * step : (c + 1) * step, :] = joined(
                jnp.dot(select(mask), pair_ref[...], preferred_element_type=F32)
            )
            rims = jnp.zeros((part, 128), F32)
            for r in range(slots):
                values = send_ref[pl.ds(c * step + r, part, stride=slots + 1), :]
                rims = jnp.where(lane >> 2 == r, pltpu.roll(values, 2 + 4 * r, 1), rims)
            rims_ref[near + c * part : near + (c + 1) * part] = rims
        if c > 0:
            at = (c - 1) * part
            left, own, right = (slice(at + k * near, at + k * near + part) for k in range(3))
            info = jnp.where(lane & 3 < 2, rims_ref[left], rims_ref[right])
            info = jnp.where(lane >= own_at, pltpu.roll(ids_ref[own], own_at, 1), info)
            info = jnp.where(lane >= left_at, pltpu.roll(ids_ref[left], left_at, 1), info)
            info = jnp.where(lane >= right_at, pltpu.roll(ids_ref[right], right_at, 1), info)
            send_ref[pl.ds((c - 1) * step + slots, part, stride=slots + 1), :] = info
            span = pl.ds((c - 1) * step, step)
            write = pltpu.make_async_copy(send_ref.at[span], out_ref.at[span], out_sems.at[c - 1])
            write.start()
            writes.append(write)
    for write in writes:
        write.wait()


def route(dev, tile, er, ei, sg, owners, slots, rows, near):
    count = er.shape[0]
    return pl.pallas_call(
        functools.partial(route_kernel, owners, slots, rows, near),
        out_shape=(
            jax.ShapeDtypeStruct((owners * (slots + 1), 128), F32),
            jax.ShapeDtypeStruct((count // 128, 128), I32),
        ),
        in_specs=[pl.BlockSpec(memory_space=pltpu.HBM)] * 5,
        out_specs=(pl.BlockSpec(memory_space=pltpu.HBM), pl.BlockSpec(memory_space=pltpu.VMEM)),
        scratch_shapes=[
            pltpu.VMEM((count // 128, 128), I32),
            pltpu.VMEM((count // 128, 128), I32),
            pltpu.VMEM((count, 128), F32),
            pltpu.VMEM((count, 128), F32),
            pltpu.VMEM((count, 128), F32),
            pltpu.VMEM((count, 256), BF16),
            pltpu.VMEM((owners * (slots + 1), 128), F32),
            pltpu.VMEM((owners + 2 * near, 128), F32),
            pltpu.VMEM((owners + 2 * near, 128), F32),
            pltpu.SemaphoreType.DMA((5,)),
            pltpu.SemaphoreType.DMA((owners // (2 * near),)),
        ],
        compiler_params=pltpu.CompilerParams(vmem_limit_bytes=16 << 20),
        name="route",
    )(*pinned(dev.reshape(count // 128, 128), tile.reshape(count // 128, 128), er, ei, sg))


def places(flat, first, slots):
    return jnp.concatenate([flat[first + r : first + r + 1] for r in range(slots)], axis=1)


def side_columns(x):
    lane = iota(x.shape, 1)
    x = pltpu.roll(x + pltpu.roll(x, 124, 1), 126, 1)
    return jnp.where(lane >= 126, x, 0.0), jnp.where(lane < 2, x, 0.0)


def rims_kernel(owners, slots, rows, got_ref, low_ref, high_ref, pair_ref, rims_ref, flat_ref, ids_ref, top_ref, bottom_ref):
    groups = top_ref.shape[1] // 128 - 2
    info = got_ref[pl.ds(slots, owners, stride=slots + 1), :]
    ids_ref[...] = info.astype(I32)
    flat = info.T.astype(I32)
    flat_ref[...] = flat
    lane = iota((owners, 128), 1)
    for r in range(slots):
        span = slice(r * owners, (r + 1) * owners)
        high, low = halves(got_ref[pl.ds(r, owners, stride=slots + 1), :])
        pair_ref[span, :128] = high
        pair_ref[span, 128:] = low
        values = pltpu.roll(info, (128 - 4 * r) % 128, 1)
        high = values.astype(BF16).astype(F32)
        low = pltpu.roll(values - high, 4, 1)
        rims_ref[span, :] = jnp.where(lane < 4, high, low).astype(BF16)
    own, left, right = (places(flat, 4 * slots + k * slots, slots) for k in range(3))
    shape = (8 * groups, owners * slots)
    line = iota(shape, 0)
    row = line & 7
    row = row + jnp.where(row < 4, 0, rows - 8)
    mask = jnp.broadcast_to(own, shape) == (line >> 3) * rows + row
    heat = joined(jnp.dot(select(mask), pair_ref[...], preferred_element_type=F32))
    shape = (16, owners * slots)
    line = iota(shape, 0)
    row = line & 7
    row = row + jnp.where(row < 4, 0, rows - 8)
    mask = jnp.where(
        line < 8,
        jnp.broadcast_to(left, shape) - (groups - 1) * rows,
        jnp.broadcast_to(right, shape),
    ) == row
    lows, highs = side_columns(jnp.dot(select(mask), rims_ref[...], preferred_element_type=F32))
    for ref, edge, at in ((top_ref, low_ref, 0), (bottom_ref, high_ref, 4)):
        ref[:8] = edge[:8]
        ref[12:] = edge[12:]
        for q in range(groups + 2):
            span = slice(128 * q, 128 * (q + 1))
            if q == 0:
                loss = lows[at : at + 4]
            elif q == groups + 1:
                loss = highs[8 + at : 12 + at]
            else:
                loss = heat[8 * (q - 1) + at : 8 * (q - 1) + at + 4]
            ref[8:12, span] = edge[8:12, span] + edge[12:, span] * loss


def rims(got, low, high, owners, slots, rows):
    strip = jax.ShapeDtypeStruct(low.shape, F32)
    numbers = jax.ShapeDtypeStruct((128, owners), I32)
    return pl.pallas_call(
        functools.partial(rims_kernel, owners, slots, rows),
        out_shape=(
            jax.ShapeDtypeStruct((owners * slots, 256), BF16),
            jax.ShapeDtypeStruct((owners * slots, 128), BF16),
            numbers,
            jax.ShapeDtypeStruct((owners, 128), I32),
            strip,
            strip,
        ),
        compiler_params=pltpu.CompilerParams(vmem_limit_bytes=16 << 20),
        name="rims",
    )(got, low, high)


def around(x):
    rows, cols = x.shape
    return (
        pltpu.roll(x, 1, 0) + pltpu.roll(x, rows - 1, 0)
    ) + (pltpu.roll(x, 1, 1) + pltpu.roll(x, cols - 1, 1))


def strips_kernel(width, t_hbm, hc_hbm, c_hbm, low_ref, high_ref, parts_ref, sems):
    cols = t_hbm.shape[1]
    copies = []
    for k, ref in enumerate((t_hbm, hc_hbm, c_hbm)):
        for side, at in enumerate((0, cols - 128)):
            copies.append(
                pltpu.make_async_copy(
                    ref.at[:, pl.ds(at, 128)], parts_ref.at[2 * k + side], sems.at[2 * k + side]
                )
            )
    for copy in copies:
        copy.start()
    low_ref[...] = jnp.zeros_like(low_ref)
    high_ref[...] = jnp.zeros_like(high_ref)
    for k in range(3):
        span = slice(RIM * k, RIM * k + width)
        copies[2 * k].wait()
        copies[2 * k + 1].wait()
        low_ref[span] = parts_ref[2 * k].T[:width]
        high_ref[span] = parts_ref[2 * k + 1].T[128 - width :]


def strips(t, hc, c, width):
    shape = jax.ShapeDtypeStruct((3 * RIM, t.shape[0]), F32)
    return pl.pallas_call(
        functools.partial(strips_kernel, width),
        out_shape=(shape, shape),
        in_specs=[pl.BlockSpec(memory_space=pltpu.HBM)] * 3,
        scratch_shapes=[pltpu.VMEM((6, t.shape[0], 128), F32), pltpu.SemaphoreType.DMA((6,))],
        compiler_params=pltpu.CompilerParams(vmem_limit_bytes=16 << 20),
        name="strips",
    )(t, hc, c)


def sides(part, width, rows):
    lane = iota((rows, 128), 1)
    x = jnp.concatenate([part, jnp.zeros((128 - RIM, rows), F32)], axis=0).T
    return x, pltpu.roll(x, 128 - width, 1)


def prepare_kernel(width, t_ref, hc_ref, c_ref, left_ref, right_ref, t_out, a_out, r_out, g_out, top_ref, bottom_ref):
    rows, cols = t_ref.shape
    for k, (ref, out) in enumerate(((t_ref, t_out), (hc_ref, r_out), (c_ref, a_out))):
        span = slice(RIM * k, RIM * k + RIM)
        right, _ = sides(right_ref[span], width, rows)
        _, left = sides(left_ref[span], width, rows)
        out[:, :SIDE] = left
        out[:, SIDE : SIDE + cols] = ref[...]
        out[:, SIDE + cols :] = right
    hc = r_out[...]
    c = a_out[...]
    diag = hc + 4.0 * c
    g = jnp.where(diag > 0.0, 1.0 / jnp.where(diag > 0.0, diag, 1.0), 0.0)
    g_out[...] = g
    a_out[...] = c * g
    r_out[...] = hc * t_out[...] * g
    for k, out in enumerate((t_out, a_out, r_out, g_out)):
        top_ref[4 * k : 4 * k + 4] = out[:4]
        bottom_ref[4 * k : 4 * k + 4] = out[rows - 4 :]


def prepare(t, hc, c, left, right, width):
    rows, cols = t.shape
    wide = cols + 2 * SIDE
    ext = jax.ShapeDtypeStruct((rows, wide), F32)
    strip = jax.ShapeDtypeStruct((16, wide), F32)
    return pl.pallas_call(
        functools.partial(prepare_kernel, width),
        out_shape=(ext, ext, ext, ext, strip, strip),
        compiler_params=pltpu.CompilerParams(vmem_limit_bytes=16 << 20),
        name="prepare",
    )(t, hc, c, left, right)


def middle_kernel(sweeps, slots, pair_ref, rims_ref, flat_ref, t_ref, a_ref, r_ref, g_ref, temp_ref, top_ref, bottom_ref, rhs_ref):
    rows, cols = temp_ref.shape
    groups = cols // 128
    flat = flat_ref[...]
    own, left, right = (places(flat, 4 * slots + k * slots, slots) for k in range(3))
    shape = (rows, own.shape[1])
    row = iota(shape, 0)
    match = lambda x, first: select(jnp.broadcast_to(x - first, shape) == row)
    for q in range(groups + 2):
        span = slice(q * 128, (q + 1) * 128)
        if q == 0:
            heat = jnp.dot(match(left, (groups - 1) * rows), rims_ref[...], preferred_element_type=F32)
            heat = side_columns(heat)[0]
        elif q == groups + 1:
            heat = jnp.dot(match(right, 0), rims_ref[...], preferred_element_type=F32)
            heat = side_columns(heat)[1]
        else:
            heat = joined(
                jnp.dot(match(own, (q - 1) * rows), pair_ref[...], preferred_element_type=F32)
            )
        rhs_ref[:, span] = r_ref[:, span] + g_ref[:, span] * heat
    for k, ref in enumerate((t_ref, a_ref, rhs_ref)):
        top_ref[k] = ref[: 2 * RIM]
        bottom_ref[k] = ref[rows - 2 * RIM :]
    temp = t_ref[...]
    for _ in range(sweeps):
        temp = rhs_ref[...] + a_ref[...] * around(temp)
    temp_ref[...] = temp[:, SIDE : SIDE + cols]


def middle(pair, rim, flat, t, a, r, g, cols, sweeps, slots):
    rows, wide = t.shape
    strip = jax.ShapeDtypeStruct((3, 2 * RIM, wide), F32)
    return pl.pallas_call(
        functools.partial(middle_kernel, sweeps, slots),
        out_shape=(jax.ShapeDtypeStruct((rows, cols), F32), strip, strip),
        scratch_shapes=[pltpu.VMEM((rows, wide), F32)],
        compiler_params=pltpu.CompilerParams(vmem_limit_bytes=16 << 20),
        name="middle",
    )(pair, rim, flat, t, a, r, g)


def solve_kernel(sweeps, owners, slots, above_ref, below_ref, inner_ref, top_ref, bottom_ref, ids_ref, out_ref, reply_ref, temp_ref, pair_ref, sems):
    rows, cols = inner_ref.shape
    inside = pl.ds(RIM, rows - 2 * RIM)
    writes = [pltpu.make_async_copy(inner_ref.at[inside], out_ref.at[inside], sems.at[0])]
    writes[0].start()
    none = jnp.zeros((4, top_ref.shape[2]), F32)
    groups = cols // 128
    for q in range(groups):
        high, low = halves(inner_ref[:, q * 128 : (q + 1) * 128])
        pair_ref[q * rows : (q + 1) * rows, :128] = high
        pair_ref[q * rows : (q + 1) * rows, 128:] = low
    for k, (strip, ref) in enumerate(((above_ref, top_ref), (below_ref, bottom_ref))):
        t, a, r = (
            jnp.concatenate(
                [none, strip[4 * j : 4 * j + 4], ref[j]] if k == 0 else [ref[j], strip[4 * j : 4 * j + 4], none],
                axis=0,
            )
            for j in range(3)
        )
        for _ in range(sweeps):
            t = r + a * around(t)
        t = t[RIM : 2 * RIM, SIDE : SIDE + cols]
        temp_ref[k] = t
        at = k * (rows - RIM)
        write = pltpu.make_async_copy(temp_ref.at[k], out_ref.at[pl.ds(at, RIM)], sems.at[k + 1])
        write.start()
        writes.append(write)
        for q in range(groups):
            span = slice(q * 128, (q + 1) * 128)
            both = [t[:, span], inner_ref[RIM : 2 * RIM, span]]
            if k == 1:
                both = [inner_ref[rows - 2 * RIM : rows - RIM, span], t[:, span]]
            high, low = halves(jnp.concatenate(both, axis=0))
            at = q * rows + k * (rows - 2 * RIM)
            pair_ref[at : at + 2 * RIM, :128] = high
            pair_ref[at : at + 2 * RIM, 128:] = low
    ids = ids_ref[...]
    for r in range(0, slots, 4):
        column = jnp.concatenate(
            [
                jnp.broadcast_to(ids[:, 4 * slots + k : 4 * slots + k + 1], (owners, 128))
                for k in range(r, r + 4)
            ],
            axis=0,
        )
        mask = jnp.concatenate(
            [column == iota((4 * owners, 128), 1) + 128 * k for k in range(rows * groups // 128)], axis=1
        )
        got = joined(jnp.dot(select(mask), pair_ref[...], preferred_element_type=F32))
        for k in range(4):
            reply_ref[pl.ds(r + k, owners, stride=slots), :] = got[k * owners : (k + 1) * owners]
    for write in writes:
        write.wait()


def solve(above, below, inner, top, bottom, ids, sweeps, owners, slots):
    rows, cols = inner.shape
    return pl.pallas_call(
        functools.partial(solve_kernel, sweeps, owners, slots),
        out_shape=(
            jax.ShapeDtypeStruct((rows, cols), F32),
            jax.ShapeDtypeStruct((owners * slots, 128), F32),
        ),
        out_specs=(pl.BlockSpec(memory_space=pltpu.HBM), pl.BlockSpec(memory_space=pltpu.VMEM)),
        scratch_shapes=[
            pltpu.VMEM((2, RIM, cols), F32),
            pltpu.VMEM((rows * cols // 128, 256), BF16),
            pltpu.SemaphoreType.DMA((3,)),
        ],
        compiler_params=pltpu.CompilerParams(vmem_limit_bytes=16 << 20),
        name="solve",
    )(above, below, inner, top, bottom, ids)


def final_kernel(slot_ref, back_ref, sg_ref, tc_ref, out_ref, pair_ref, new_ref, sems):
    total = back_ref.shape[0]
    blocks = slot_ref.shape[0]
    high, low = halves(back_ref[...])
    pair_ref[:, :128] = high
    pair_ref[:, 128:] = low
    slot = slot_ref[...].T
    writes = []
    for b in range(0, blocks, 4):
        column = jnp.concatenate(
            [jnp.broadcast_to(slot[:, k : k + 1], (128, 128)) for k in range(b, b + 4)], axis=0
        )
        mask = jnp.concatenate(
            [column == iota((512, 128), 1) + 128 * k for k in range(total // 128)], axis=1
        )
        hot = joined(jnp.dot(select(mask), pair_ref[...], preferred_element_type=F32))
        span = pl.ds(b * 128, 512)
        new_ref[span, :] = sg_ref[span, :] / (1.0 + tc_ref[span, :] * hot)
        write = pltpu.make_async_copy(new_ref.at[span], out_ref.at[span], sems.at[b // 4])
        write.start()
        writes.append(write)
    for write in writes:
        write.wait()


def final(slot, back, sg, tc):
    return pl.pallas_call(
        final_kernel,
        out_shape=jax.ShapeDtypeStruct(sg.shape, F32),
        out_specs=pl.BlockSpec(memory_space=pltpu.HBM),
        scratch_shapes=[
            pltpu.VMEM((back.shape[0], 256), BF16),
            pltpu.VMEM(sg.shape, F32),
            pltpu.SemaphoreType.DMA((slot.shape[0] // 4,)),
        ],
        compiler_params=pltpu.CompilerParams(vmem_limit_bytes=16 << 20),
        name="final",
    )(slot, back, sg, tc)


def swap(low_part, high_part, axis):
    count = lax.axis_size(axis)
    up = [(i, i + 1) for i in range(count - 1)]
    down = [(i + 1, i) for i in range(count - 1)]
    return lax.ppermute(high_part, axis, up), lax.ppermute(low_part, axis, down)


def exchanged(x, owners):
    rows = x.shape[0]
    x = x.reshape(owners, 1, rows // owners * 128)
    x = lax.all_to_all(x, ("em", "th"), split_axis=0, concat_axis=0, tiled=True)
    return x.reshape(rows, 128)


SWEEPS = 3


def pinned(*arrays):
    return [pltpu.with_memory_space_constraint(x, pltpu.HBM) for x in arrays]


def local(e_real, e_imag, sigma_em, temp_coef, dest_dev, dest_tile, t_old, heat_cap, conduct):
    owners = lax.axis_size("em") * lax.axis_size("th")
    slots = 2 * e_real.shape[0] // owners
    rows, cols = t_old.shape
    near = lax.axis_size("th")
    send, slot = route(dest_dev, dest_tile, e_real, e_imag, sigma_em, owners, slots, rows, near)
    got = exchanged(send, owners)
    grid = pinned(*lax.optimization_barrier((t_old, heat_cap, conduct, slot))[:3])
    low, high = strips(*grid, SWEEPS)
    left, right = swap(low, high, "em")
    t, a, r, g, low, high = prepare(*grid, left, right, SWEEPS)
    pair, rim, flat, ids, low, high = rims(got, low, high, owners, slots, rows)
    above, below = swap(low, high, "th")
    inner, top, bottom = middle(pair, rim, flat, t, a, r, g, cols, SWEEPS, slots)
    temp, reply = solve(above, below, inner, top, bottom, ids, SWEEPS, owners, slots)
    back = exchanged(reply, owners)
    return temp, final(slot, back, sigma_em, temp_coef)


def solution(mesh):
    tiles = P(("em", "th"), None)
    grid = P("th", "em")
    return jax.shard_map(
        local,
        mesh=mesh,
        in_specs=(tiles,) * 6 + (grid,) * 3,
        out_specs=(grid, tiles),
        check_vma=False,
    )
```

```python
import functools
import jax
import jax.numpy as jnp
from jax import lax
from jax.experimental import pallas as pl
from jax.experimental.pallas import tpu as pltpu
from jax.sharding import PartitionSpec as P

F32 = jnp.float32
BF16 = jnp.bfloat16
I32 = jnp.int32
RIM = 8
SIDE = 128


def iota(shape, dim):
    return lax.broadcasted_iota(I32, shape, dim)


def to_send(low, high, axis):
    even = lax.axis_index(axis) % 2 == 0
    return jnp.where(even, high, low), jnp.where(even, low, high)


def received(first, second, axis, count):
    me = lax.axis_index(axis)
    even = me % 2 == 0
    low = jnp.where(me > 0, jnp.where(even, second, first), 0.0)
    high = jnp.where(me < count - 1, jnp.where(even, first, second), 0.0)
    return low, high


def halves(x):
    high = x.astype(BF16)
    low = (x - high.astype(F32)).astype(BF16)
    return high, low


def select(mask):
    return jnp.where(mask, 1.0, 0.0).astype(BF16)


def joined(y):
    return y[:, :128] + y[:, 128:]


def route_kernel(owners, slots, rows, near, dev_hbm, tile_hbm, er_hbm, ei_hbm, sg_hbm, out_ref, slot_ref, dev_ref, tile_ref, er_ref, ei_ref, sg_ref, pair_ref, send_ref, ids_ref, rims_ref, sems, out_sems):
    count = er_ref.shape[0]
    blocks = count // 128
    copies = [
        pltpu.make_async_copy(source, target, sems.at[k])
        for k, (source, target) in enumerate(
            (
                (dev_hbm, dev_ref),
                (tile_hbm, tile_ref),
                (er_hbm, er_ref),
                (ei_hbm, ei_ref),
                (sg_hbm, sg_ref),
            )
        )
    ]
    for copy in copies:
        copy.start()
    copies[0].wait()
    copies[1].wait()
    dev = dev_ref[...]
    tile = tile_ref[...]
    tile = (tile & 3) * rows + (tile >> 2)
    hits = [jnp.broadcast_to(dev[b : b + 1], (owners, 128)) == iota((owners, 128), 0) for b in range(blocks)]
    ahead = select(iota((128, 256), 0) < iota((128, 256), 1))
    sums = jnp.dot(
        jnp.concatenate([select(h) for h in hits], axis=0), ahead, preferred_element_type=F32
    )
    carry = jnp.zeros((owners, 128), F32)
    ranks = []
    for b in range(blocks):
        part = sums[b * owners : (b + 1) * owners]
        ranks.append(
            jnp.sum(jnp.where(hits[b], part[:, :128] + carry, 0.0), axis=0, keepdims=True)
        )
        carry = carry + part[:, 128:]
    rank = jnp.concatenate(ranks, axis=0).astype(I32)
    slot_ref[...] = dev * slots + rank
    line = lambda x: jnp.concatenate([x[b : b + 1] for b in range(blocks)], axis=1)
    place = line(dev * (slots + 1) + rank)
    hit = jnp.concatenate(hits, axis=1)
    tiles = line(tile)
    upper = jnp.where(hit, jnp.broadcast_to(tiles >> 5, (owners, count)), 0)
    lower = jnp.where(hit, jnp.broadcast_to(tiles & 31, (owners, count)), 0)
    numbers = jnp.concatenate([upper, lower], axis=0).astype(F32).astype(BF16)
    which = select(jnp.broadcast_to(line(rank), (128, count)) == iota((128, count), 0))
    ids = lax.dot_general(
        numbers, which, (((1,), (1,)), ((), ())), preferred_element_type=F32
    )
    none = jnp.zeros((near, 128), F32)
    for ref in (ids_ref, rims_ref):
        ref[:near] = none
        ref[near + owners :] = none
    ids_ref[near : near + owners] = ids[:owners] * 32.0 + ids[owners:]
    for copy in copies[2:]:
        copy.wait()
    er = er_ref[...]
    ei = ei_ref[...]
    high, low = halves(sg_ref[...] * (er * er + ei * ei))
    pair_ref[:, :128] = high
    pair_ref[:, 128:] = low
    part = 2 * near
    step = part * (slots + 1)
    lane = iota((part, 128), 1)
    own_at, left_at, right_at = (4 * slots + k * slots for k in range(3))
    writes = []
    for c in range(owners // part + 1):
        if c < owners // part:
            mask = jnp.broadcast_to(place, (step, count)) == iota((step, count), 0) + c * step
            send_ref[c * step : (c + 1) * step, :] = joined(
                jnp.dot(select(mask), pair_ref[...], preferred_element_type=F32)
            )
            rims = jnp.zeros((part, 128), F32)
            for r in range(slots):
                values = send_ref[pl.ds(c * step + r, part, stride=slots + 1), :]
                rims = jnp.where(lane >> 2 == r, pltpu.roll(values, 2 + 4 * r, 1), rims)
            rims_ref[near + c * part : near + (c + 1) * part] = rims
        if c > 0:
            at = (c - 1) * part
            left, own, right = (slice(at + k * near, at + k * near + part) for k in range(3))
            info = jnp.where(lane & 3 < 2, rims_ref[left], rims_ref[right])
            info = jnp.where(lane >= own_at, pltpu.roll(ids_ref[own], own_at, 1), info)
            info = jnp.where(lane >= left_at, pltpu.roll(ids_ref[left], left_at, 1), info)
            info = jnp.where(lane >= right_at, pltpu.roll(ids_ref[right], right_at, 1), info)
            send_ref[pl.ds((c - 1) * step + slots, part, stride=slots + 1), :] = info
            span = pl.ds((c - 1) * step, step)
            write = pltpu.make_async_copy(send_ref.at[span], out_ref.at[span], out_sems.at[c - 1])
            write.start()
            writes.append(write)
    for write in writes:
        write.wait()


def route(dev, tile, er, ei, sg, owners, slots, rows, near):
    count = er.shape[0]
    return pl.pallas_call(
        functools.partial(route_kernel, owners, slots, rows, near),
        out_shape=(
            jax.ShapeDtypeStruct((owners * (slots + 1), 128), F32),
            jax.ShapeDtypeStruct((count // 128, 128), I32),
        ),
        in_specs=[pl.BlockSpec(memory_space=pltpu.HBM)] * 5,
        out_specs=(pl.BlockSpec(memory_space=pltpu.HBM), pl.BlockSpec(memory_space=pltpu.VMEM)),
        scratch_shapes=[
            pltpu.VMEM((count // 128, 128), I32),
            pltpu.VMEM((count // 128, 128), I32),
            pltpu.VMEM((count, 128), F32),
            pltpu.VMEM((count, 128), F32),
            pltpu.VMEM((count, 128), F32),
            pltpu.VMEM((count, 256), BF16),
            pltpu.VMEM((owners * (slots + 1), 128), F32),
            pltpu.VMEM((owners + 2 * near, 128), F32),
            pltpu.VMEM((owners + 2 * near, 128), F32),
            pltpu.SemaphoreType.DMA((5,)),
            pltpu.SemaphoreType.DMA((owners // (2 * near),)),
        ],
        compiler_params=pltpu.CompilerParams(vmem_limit_bytes=16 << 20),
        name="route",
    )(*pinned(dev.reshape(count // 128, 128), tile.reshape(count // 128, 128), er, ei, sg))


def places(flat, first, slots):
    return jnp.concatenate([flat[first + r : first + r + 1] for r in range(slots)], axis=1)


def side_columns(x):
    lane = iota(x.shape, 1)
    x = pltpu.roll(x + pltpu.roll(x, 124, 1), 126, 1)
    return jnp.where(lane >= 126, x, 0.0), jnp.where(lane < 2, x, 0.0)


def rims_kernel(owners, slots, got_ref, ext_ref, pair_ref, rims_ref, flat_ref, ids_ref, first_ref, second_ref):
    rows = ext_ref.shape[1]
    groups = ext_ref.shape[2] // 128 - 2
    info = got_ref[pl.ds(slots, owners, stride=slots + 1), :]
    ids_ref[...] = info.astype(I32)
    flat = info.T.astype(I32)
    flat_ref[...] = flat
    lane = iota((owners, 128), 1)
    for r in range(slots):
        span = slice(r * owners, (r + 1) * owners)
        high, low = halves(got_ref[pl.ds(r, owners, stride=slots + 1), :])
        pair_ref[span, :128] = high
        pair_ref[span, 128:] = low
        values = pltpu.roll(info, (128 - 4 * r) % 128, 1)
        high = values.astype(BF16).astype(F32)
        low = pltpu.roll(values - high, 4, 1)
        rims_ref[span, :] = jnp.where(lane < 4, high, low).astype(BF16)
    own, left, right = (places(flat, 4 * slots + k * slots, slots) for k in range(3))
    shape = (8 * groups, owners * slots)
    line = iota(shape, 0)
    row = line & 7
    row = row + jnp.where(row < 4, 0, rows - 8)
    mask = jnp.broadcast_to(own, shape) == (line >> 3) * rows + row
    heat = joined(jnp.dot(select(mask), pair_ref[...], preferred_element_type=F32))
    shape = (16, owners * slots)
    line = iota(shape, 0)
    row = line & 7
    row = row + jnp.where(row < 4, 0, rows - 8)
    mask = jnp.where(
        line < 8,
        jnp.broadcast_to(left, shape) - (groups - 1) * rows,
        jnp.broadcast_to(right, shape),
    ) == row
    lows, highs = side_columns(jnp.dot(select(mask), rims_ref[...], preferred_element_type=F32))
    edges = []
    for at, rim in ((0, slice(0, 4)), (4, slice(rows - 4, rows))):
        loss = [lows[at : at + 4]]
        loss += [heat[8 * q + at : 8 * q + at + 4] for q in range(groups)]
        loss += [highs[8 + at : 12 + at]]
        rhs = ext_ref[2, rim] + ext_ref[3, rim] * jnp.concatenate(loss, axis=1)
        edges.append((ext_ref[0, rim], ext_ref[1, rim], rhs))
    for k in range(3):
        span = slice(4 * k, 4 * k + 4)
        first_ref[span], second_ref[span] = to_send(edges[0][k], edges[1][k], "th")


def rims(got, ext, owners, slots):
    strip = jax.ShapeDtypeStruct((12, ext.shape[2]), F32)
    return pl.pallas_call(
        functools.partial(rims_kernel, owners, slots),
        out_shape=(
            jax.ShapeDtypeStruct((owners * slots, 256), BF16),
            jax.ShapeDtypeStruct((owners * slots, 128), BF16),
            jax.ShapeDtypeStruct((128, owners), I32),
            jax.ShapeDtypeStruct((owners, 128), I32),
            strip,
            strip,
        ),
        compiler_params=pltpu.CompilerParams(vmem_limit_bytes=16 << 20),
        name="rims",
    )(got, ext)


def around(x):
    rows, cols = x.shape
    return (
        pltpu.roll(x, 1, 0) + pltpu.roll(x, rows - 1, 0)
    ) + (pltpu.roll(x, 1, 1) + pltpu.roll(x, cols - 1, 1))


def strips_kernel(width, t_hbm, hc_hbm, c_hbm, first_ref, second_ref, parts_ref, sems):
    cols = t_hbm.shape[1]
    copies = []
    for k, ref in enumerate((t_hbm, hc_hbm, c_hbm)):
        for side, at in enumerate((0, cols - 128)):
            copies.append(
                pltpu.make_async_copy(
                    ref.at[:, pl.ds(at, 128)], parts_ref.at[2 * k + side], sems.at[2 * k + side]
                )
            )
    for copy in copies:
        copy.start()
    for k in range(3):
        span = slice(RIM * k, RIM * k + RIM)
        copies[2 * k].wait()
        copies[2 * k + 1].wait()
        low = parts_ref[2 * k].T[:RIM]
        high = pltpu.roll(parts_ref[2 * k + 1].T[128 - RIM :], width, 0)
        first_ref[span], second_ref[span] = to_send(low, high, "em")


def strips(t, hc, c, width):
    shape = jax.ShapeDtypeStruct((3 * RIM, t.shape[0]), F32)
    return pl.pallas_call(
        functools.partial(strips_kernel, width),
        out_shape=(shape, shape),
        in_specs=[pl.BlockSpec(memory_space=pltpu.HBM)] * 3,
        scratch_shapes=[pltpu.VMEM((6, t.shape[0], 128), F32), pltpu.SemaphoreType.DMA((6,))],
        compiler_params=pltpu.CompilerParams(vmem_limit_bytes=16 << 20),
        name="strips",
    )(t, hc, c)


def sides(part, width, rows):
    lane = iota((rows, 128), 1)
    x = jnp.concatenate([part, jnp.zeros((128 - RIM, rows), F32)], axis=0).T
    return x, pltpu.roll(x, 128 - width, 1)


def prepare_kernel(width, count, t_ref, hc_ref, c_ref, first_ref, second_ref, ext_ref):
    rows, cols = t_ref.shape
    left, right = received(first_ref[...], second_ref[...], "em", count)
    for k, ref in enumerate((t_ref, hc_ref, c_ref)):
        span = slice(RIM * k, RIM * k + RIM)
        ext_ref[k, :, :SIDE] = sides(left[span], width, rows)[1]
        ext_ref[k, :, SIDE : SIDE + cols] = ref[...]
        ext_ref[k, :, SIDE + cols :] = sides(right[span], width, rows)[0]
    hc = ext_ref[1]
    c = ext_ref[2]
    diag = hc + 4.0 * c
    g = jnp.where(diag > 0.0, 1.0 / jnp.where(diag > 0.0, diag, 1.0), 0.0)
    ext_ref[1] = c * g
    ext_ref[2] = hc * ext_ref[0] * g
    ext_ref[3] = g


def prepare(t, hc, c, first, second, width):
    rows, cols = t.shape
    return pl.pallas_call(
        functools.partial(prepare_kernel, width, lax.axis_size("em")),
        out_shape=jax.ShapeDtypeStruct((4, rows, cols + 2 * SIDE), F32),
        compiler_params=pltpu.CompilerParams(vmem_limit_bytes=16 << 20),
        name="prepare",
    )(t, hc, c, first, second)


def middle_kernel(sweeps, slots, pair_ref, rims_ref, flat_ref, ext_ref, temp_ref, top_ref, bottom_ref, rhs_ref):
    rows, cols = temp_ref.shape
    groups = cols // 128
    flat = flat_ref[...]
    own, left, right = (places(flat, 4 * slots + k * slots, slots) for k in range(3))
    shape = (rows, own.shape[1])
    row = iota(shape, 0)
    match = lambda x, first: select(jnp.broadcast_to(x - first, shape) == row)
    for q in range(groups + 2):
        span = slice(q * 128, (q + 1) * 128)
        if q == 0:
            heat = jnp.dot(match(left, (groups - 1) * rows), rims_ref[...], preferred_element_type=F32)
            heat = side_columns(heat)[0]
        elif q == groups + 1:
            heat = jnp.dot(match(right, 0), rims_ref[...], preferred_element_type=F32)
            heat = side_columns(heat)[1]
        else:
            heat = joined(
                jnp.dot(match(own, (q - 1) * rows), pair_ref[...], preferred_element_type=F32)
            )
        rhs_ref[:, span] = ext_ref[2, :, span] + ext_ref[3, :, span] * heat
    for k, ref in enumerate((ext_ref.at[0], ext_ref.at[1], rhs_ref)):
        top_ref[k] = ref[: 2 * RIM]
        bottom_ref[k] = ref[rows - 2 * RIM :]
    temp = ext_ref[0]
    for _ in range(sweeps):
        temp = rhs_ref[...] + ext_ref[1] * around(temp)
    temp_ref[...] = temp[:, SIDE : SIDE + cols]


def middle(pair, rim, flat, ext, cols, sweeps, slots):
    _, rows, wide = ext.shape
    strip = jax.ShapeDtypeStruct((3, 2 * RIM, wide), F32)
    return pl.pallas_call(
        functools.partial(middle_kernel, sweeps, slots),
        out_shape=(jax.ShapeDtypeStruct((rows, cols), F32), strip, strip),
        scratch_shapes=[pltpu.VMEM((rows, wide), F32)],
        compiler_params=pltpu.CompilerParams(vmem_limit_bytes=16 << 20),
        name="middle",
    )(pair, rim, flat, ext)


def solve_kernel(sweeps, owners, slots, count, first_ref, second_ref, inner_ref, top_ref, bottom_ref, ids_ref, out_ref, reply_ref, temp_ref, pair_ref, sems):
    rows, cols = inner_ref.shape
    inside = pl.ds(RIM, rows - 2 * RIM)
    writes = [pltpu.make_async_copy(inner_ref.at[inside], out_ref.at[inside], sems.at[0])]
    writes[0].start()
    none = jnp.zeros((4, top_ref.shape[2]), F32)
    groups = cols // 128
    for q in range(groups):
        high, low = halves(inner_ref[:, q * 128 : (q + 1) * 128])
        pair_ref[q * rows : (q + 1) * rows, :128] = high
        pair_ref[q * rows : (q + 1) * rows, 128:] = low
    above, below = received(first_ref[...], second_ref[...], "th", count)
    for k, (strip, ref) in enumerate(((above, top_ref), (below, bottom_ref))):
        t, a, r = (
            jnp.concatenate(
                [none, strip[4 * j : 4 * j + 4], ref[j]] if k == 0 else [ref[j], strip[4 * j : 4 * j + 4], none],
                axis=0,
            )
            for j in range(3)
        )
        for _ in range(sweeps):
            t = r + a * around(t)
        t = t[RIM : 2 * RIM, SIDE : SIDE + cols]
        temp_ref[k] = t
        at = k * (rows - RIM)
        write = pltpu.make_async_copy(temp_ref.at[k], out_ref.at[pl.ds(at, RIM)], sems.at[k + 1])
        write.start()
        writes.append(write)
        for q in range(groups):
            span = slice(q * 128, (q + 1) * 128)
            both = [t[:, span], inner_ref[RIM : 2 * RIM, span]]
            if k == 1:
                both = [inner_ref[rows - 2 * RIM : rows - RIM, span], t[:, span]]
            high, low = halves(jnp.concatenate(both, axis=0))
            at = q * rows + k * (rows - 2 * RIM)
            pair_ref[at : at + 2 * RIM, :128] = high
            pair_ref[at : at + 2 * RIM, 128:] = low
    ids = ids_ref[...]
    for r in range(0, slots, 4):
        column = jnp.concatenate(
            [
                jnp.broadcast_to(ids[:, 4 * slots + k : 4 * slots + k + 1], (owners, 128))
                for k in range(r, r + 4)
            ],
            axis=0,
        )
        mask = jnp.concatenate(
            [column == iota((4 * owners, 128), 1) + 128 * k for k in range(rows * groups // 128)], axis=1
        )
        got = joined(jnp.dot(select(mask), pair_ref[...], preferred_element_type=F32))
        for k in range(4):
            reply_ref[pl.ds(r + k, owners, stride=slots), :] = got[k * owners : (k + 1) * owners]
    for write in writes:
        write.wait()


def solve(first, second, inner, top, bottom, ids, sweeps, owners, slots):
    rows, cols = inner.shape
    return pl.pallas_call(
        functools.partial(solve_kernel, sweeps, owners, slots, lax.axis_size("th")),
        out_shape=(
            jax.ShapeDtypeStruct((rows, cols), F32),
            jax.ShapeDtypeStruct((owners * slots, 128), F32),
        ),
        out_specs=(pl.BlockSpec(memory_space=pltpu.HBM), pl.BlockSpec(memory_space=pltpu.VMEM)),
        scratch_shapes=[
            pltpu.VMEM((2, RIM, cols), F32),
            pltpu.VMEM((rows * cols // 128, 256), BF16),
            pltpu.SemaphoreType.DMA((3,)),
        ],
        compiler_params=pltpu.CompilerParams(vmem_limit_bytes=16 << 20),
        name="solve",
    )(first, second, inner, top, bottom, ids)


def final_kernel(slot_ref, back_ref, sg_ref, tc_ref, out_ref, pair_ref, new_ref, sems):
    total = back_ref.shape[0]
    blocks = slot_ref.shape[0]
    high, low = halves(back_ref[...])
    pair_ref[:, :128] = high
    pair_ref[:, 128:] = low
    slot = slot_ref[...].T
    writes = []
    for b in range(0, blocks, 4):
        column = jnp.concatenate(
            [jnp.broadcast_to(slot[:, k : k + 1], (128, 128)) for k in range(b, b + 4)], axis=0
        )
        mask = jnp.concatenate(
            [column == iota((512, 128), 1) + 128 * k for k in range(total // 128)], axis=1
        )
        hot = joined(jnp.dot(select(mask), pair_ref[...], preferred_element_type=F32))
        span = pl.ds(b * 128, 512)
        new_ref[span, :] = sg_ref[span, :] / (1.0 + tc_ref[span, :] * hot)
        write = pltpu.make_async_copy(new_ref.at[span], out_ref.at[span], sems.at[b // 4])
        write.start()
        writes.append(write)
    for write in writes:
        write.wait()


def final(slot, back, sg, tc):
    return pl.pallas_call(
        final_kernel,
        out_shape=jax.ShapeDtypeStruct(sg.shape, F32),
        out_specs=pl.BlockSpec(memory_space=pltpu.HBM),
        scratch_shapes=[
            pltpu.VMEM((back.shape[0], 256), BF16),
            pltpu.VMEM(sg.shape, F32),
            pltpu.SemaphoreType.DMA((slot.shape[0] // 4,)),
        ],
        compiler_params=pltpu.CompilerParams(vmem_limit_bytes=16 << 20),
        name="final",
    )(slot, back, sg, tc)


def traded(first, second, axis):
    n_em, n_th = lax.axis_size("em"), lax.axis_size("th")
    near, far = [], []
    for e in range(n_em):
        for t in range(n_th):
            if axis == "em":
                mate = (e + 1 if e % 2 else e - 1) % n_em, t
                close = e ^ 1, t
            else:
                mate = e, t + 1 if t % 2 else t - 1
                mate = mate if 0 <= mate[1] < n_th else (e ^ 1, t)
                close = e, t ^ 1
            near.append((e * n_th + t, close[0] * n_th + close[1]))
            far.append((e * n_th + t, mate[0] * n_th + mate[1]))
    return lax.ppermute(first, ("em", "th"), near), lax.ppermute(second, ("em", "th"), far)


def exchanged(x, owners):
    rows = x.shape[0]
    x = x.reshape(owners, 1, rows // owners * 128)
    x = lax.all_to_all(x, ("em", "th"), split_axis=0, concat_axis=0, tiled=True)
    return x.reshape(rows, 128)


SWEEPS = 3


def pinned(*arrays):
    return [pltpu.with_memory_space_constraint(x, pltpu.HBM) for x in arrays]


def local(e_real, e_imag, sigma_em, temp_coef, dest_dev, dest_tile, t_old, heat_cap, conduct):
    owners = lax.axis_size("em") * lax.axis_size("th")
    slots = 2 * e_real.shape[0] // owners
    rows, cols = t_old.shape
    near = lax.axis_size("th")
    send, slot = route(dest_dev, dest_tile, e_real, e_imag, sigma_em, owners, slots, rows, near)
    got = exchanged(send, owners)
    grid = pinned(*lax.optimization_barrier((t_old, heat_cap, conduct, slot))[:3])
    ext = prepare(*grid, *traded(*strips(*grid, SWEEPS), "em"), SWEEPS)
    pair, rim, flat, ids, first, second = rims(got, ext, owners, slots)
    first, second = traded(first, second, "th")
    inner, top, bottom = middle(pair, rim, flat, ext, cols, SWEEPS, slots)
    temp, reply = solve(first, second, inner, top, bottom, ids, SWEEPS, owners, slots)
    back = exchanged(reply, owners)
    return temp, final(slot, back, sigma_em, temp_coef)


def solution(mesh):
    tiles = P(("em", "th"), None)
    grid = P("th", "em")
    return jax.shard_map(
        local,
        mesh=mesh,
        in_specs=(tiles,) * 6 + (grid,) * 3,
        out_specs=(grid, tiles),
        check_vma=False,
    )
```

```python
import functools
import jax
import jax.numpy as jnp
from jax import lax
from jax.experimental import pallas as pl
from jax.experimental.pallas import tpu as pltpu
from jax.sharding import PartitionSpec as P

F32 = jnp.float32
BF16 = jnp.bfloat16
I32 = jnp.int32
RIM = 8
SIDE = 128


def iota(shape, dim):
    return lax.broadcasted_iota(I32, shape, dim)


def to_send(low, high, axis):
    even = lax.axis_index(axis) % 2 == 0
    return jnp.where(even, high, low), jnp.where(even, low, high)


def received(first, second, axis, count):
    me = lax.axis_index(axis)
    even = me % 2 == 0
    low = jnp.where(me > 0, jnp.where(even, second, first), 0.0)
    high = jnp.where(me < count - 1, jnp.where(even, first, second), 0.0)
    return low, high


def halves(x):
    high = x.astype(BF16)
    low = (x - high.astype(F32)).astype(BF16)
    return high, low


def select(mask):
    return jnp.where(mask, 1.0, 0.0).astype(BF16)


def joined(y):
    return y[:, :128] + y[:, 128:]


def route_kernel(owners, slots, rows, near, dev_hbm, tile_hbm, er_hbm, ei_hbm, sg_hbm, out_ref, slot_ref, dev_ref, tile_ref, er_ref, ei_ref, sg_ref, pair_ref, send_ref, ids_ref, rims_ref, sems, out_sems):
    count = er_ref.shape[0]
    blocks = count // 128
    copies = [
        pltpu.make_async_copy(source, target, sems.at[k])
        for k, (source, target) in enumerate(
            (
                (dev_hbm, dev_ref),
                (tile_hbm, tile_ref),
                (er_hbm, er_ref),
                (ei_hbm, ei_ref),
                (sg_hbm, sg_ref),
            )
        )
    ]
    for copy in copies:
        copy.start()
    copies[0].wait()
    copies[1].wait()
    dev = dev_ref[...]
    tile = tile_ref[...]
    tile = (tile & 3) * rows + (tile >> 2)
    hits = [jnp.broadcast_to(dev[b : b + 1], (owners, 128)) == iota((owners, 128), 0) for b in range(blocks)]
    ahead = select(iota((128, 256), 0) < iota((128, 256), 1))
    sums = jnp.dot(
        jnp.concatenate([select(h) for h in hits], axis=0), ahead, preferred_element_type=F32
    )
    carry = jnp.zeros((owners, 128), F32)
    ranks = []
    for b in range(blocks):
        part = sums[b * owners : (b + 1) * owners]
        ranks.append(
            jnp.sum(jnp.where(hits[b], part[:, :128] + carry, 0.0), axis=0, keepdims=True)
        )
        carry = carry + part[:, 128:]
    rank = jnp.concatenate(ranks, axis=0).astype(I32)
    slot_ref[...] = dev * slots + rank
    line = lambda x: jnp.concatenate([x[b : b + 1] for b in range(blocks)], axis=1)
    place = line(dev * (slots + 1) + rank)
    hit = jnp.concatenate(hits, axis=1)
    tiles = line(tile)
    upper = jnp.where(hit, jnp.broadcast_to(tiles >> 5, (owners, count)), 0)
    lower = jnp.where(hit, jnp.broadcast_to(tiles & 31, (owners, count)), 0)
    numbers = jnp.concatenate([upper, lower], axis=0).astype(F32).astype(BF16)
    which = select(jnp.broadcast_to(line(rank), (128, count)) == iota((128, count), 0))
    ids = lax.dot_general(
        numbers, which, (((1,), (1,)), ((), ())), preferred_element_type=F32
    )
    none = jnp.zeros((near, 128), F32)
    for ref in (ids_ref, rims_ref):
        ref[:near] = none
        ref[near + owners :] = none
    ids_ref[near : near + owners] = ids[:owners] * 32.0 + ids[owners:]
    for copy in copies[2:]:
        copy.wait()
    er = er_ref[...]
    ei = ei_ref[...]
    high, low = halves(sg_ref[...] * (er * er + ei * ei))
    pair_ref[:, :128] = high
    pair_ref[:, 128:] = low
    part = 2 * near
    step = part * (slots + 1)
    lane = iota((part, 128), 1)
    own_at, left_at, right_at = (4 * slots + k * slots for k in range(3))
    writes = []
    for c in range(owners // part + 1):
        if c < owners // part:
            mask = jnp.broadcast_to(place, (step, count)) == iota((step, count), 0) + c * step
            send_ref[c * step : (c + 1) * step, :] = joined(
                jnp.dot(select(mask), pair_ref[...], preferred_element_type=F32)
            )
            rims = jnp.zeros((part, 128), F32)
            for r in range(slots):
                values = send_ref[pl.ds(c * step + r, part, stride=slots + 1), :]
                rims = jnp.where(lane >> 2 == r, pltpu.roll(values, 2 + 4 * r, 1), rims)
            rims_ref[near + c * part : near + (c + 1) * part] = rims
        if c > 0:
            at = (c - 1) * part
            left, own, right = (slice(at + k * near, at + k * near + part) for k in range(3))
            info = jnp.where(lane & 3 < 2, rims_ref[left], rims_ref[right])
            info = jnp.where(lane >= own_at, pltpu.roll(ids_ref[own], own_at, 1), info)
            info = jnp.where(lane >= left_at, pltpu.roll(ids_ref[left], left_at, 1), info)
            info = jnp.where(lane >= right_at, pltpu.roll(ids_ref[right], right_at, 1), info)
            send_ref[pl.ds((c - 1) * step + slots, part, stride=slots + 1), :] = info
            span = pl.ds((c - 1) * step, step)
            write = pltpu.make_async_copy(send_ref.at[span], out_ref.at[span], out_sems.at[c - 1])
            write.start()
            writes.append(write)
    for write in writes:
        write.wait()


def route(dev, tile, er, ei, sg, owners, slots, rows, near):
    count = er.shape[0]
    return pl.pallas_call(
        functools.partial(route_kernel, owners, slots, rows, near),
        out_shape=(
            jax.ShapeDtypeStruct((owners * (slots + 1), 128), F32),
            jax.ShapeDtypeStruct((count // 128, 128), I32),
        ),
        in_specs=[pl.BlockSpec(memory_space=pltpu.HBM)] * 5,
        out_specs=(pl.BlockSpec(memory_space=pltpu.HBM), pl.BlockSpec(memory_space=pltpu.VMEM)),
        scratch_shapes=[
            pltpu.VMEM((count // 128, 128), I32),
            pltpu.VMEM((count // 128, 128), I32),
            pltpu.VMEM((count, 128), F32),
            pltpu.VMEM((count, 128), F32),
            pltpu.VMEM((count, 128), F32),
            pltpu.VMEM((count, 256), BF16),
            pltpu.VMEM((owners * (slots + 1), 128), F32),
            pltpu.VMEM((owners + 2 * near, 128), F32),
            pltpu.VMEM((owners + 2 * near, 128), F32),
            pltpu.SemaphoreType.DMA((5,)),
            pltpu.SemaphoreType.DMA((owners // (2 * near),)),
        ],
        compiler_params=pltpu.CompilerParams(vmem_limit_bytes=16 << 20),
        name="route",
    )(*pinned(dev.reshape(count // 128, 128), tile.reshape(count // 128, 128), er, ei, sg))


def source(t, a, g, heat):
    return t * (1.0 - 4.0 * a) + g * heat


def places(flat, first, slots):
    return jnp.concatenate([flat[first + r : first + r + 1] for r in range(slots)], axis=1)


def side_columns(low, high):
    lane = iota(low.shape, 1)
    low, high = (pltpu.roll(x + pltpu.roll(x, 124, 1), 126, 1) for x in (low, high))
    return jnp.where(lane >= 126, low, jnp.where(lane < 2, high, 0.0))


def rims_kernel(owners, slots, got_ref, ext_ref, pair_ref, rims_ref, flat_ref, ids_ref, first_ref, second_ref):
    rows = ext_ref.shape[1]
    groups = ext_ref.shape[2] // 128 - 1
    info = got_ref[pl.ds(slots, owners, stride=slots + 1), :]
    ids_ref[...] = info.astype(I32)
    flat = info.T.astype(I32)
    flat_ref[...] = flat
    lane = iota((owners, 128), 1)
    for r in range(slots):
        span = slice(r * owners, (r + 1) * owners)
        high, low = halves(got_ref[pl.ds(r, owners, stride=slots + 1), :])
        pair_ref[span, :128] = high
        pair_ref[span, 128:] = low
        values = pltpu.roll(info, (128 - 4 * r) % 128, 1)
        high = values.astype(BF16).astype(F32)
        low = pltpu.roll(values - high, 4, 1)
        rims_ref[span, :] = jnp.where(lane < 4, high, low).astype(BF16)
    own, left, right = (places(flat, 4 * slots + k * slots, slots) for k in range(3))
    shape = (8 * groups, owners * slots)
    line = iota(shape, 0)
    row = line & 7
    row = row + jnp.where(row < 4, 0, rows - 8)
    mask = jnp.broadcast_to(own, shape) == (line >> 3) * rows + row
    heat = joined(jnp.dot(select(mask), pair_ref[...], preferred_element_type=F32))
    shape = (16, owners * slots)
    line = iota(shape, 0)
    row = line & 7
    row = row + jnp.where(row < 4, 0, rows - 8)
    mask = jnp.where(
        line < 8,
        jnp.broadcast_to(left, shape) - (groups - 1) * rows,
        jnp.broadcast_to(right, shape),
    ) == row
    side = jnp.dot(select(mask), rims_ref[...], preferred_element_type=F32)
    side = side_columns(side[:8], side[8:])
    edges = []
    for at, rim in ((0, slice(0, 4)), (4, slice(rows - 4, rows))):
        loss = [heat[8 * q + at : 8 * q + at + 4] for q in range(groups)] + [side[at : at + 4]]
        t, a = ext_ref[0, rim], ext_ref[1, rim]
        edges.append((t, a, source(t, a, ext_ref[2, rim], jnp.concatenate(loss, axis=1))))
    for k in range(3):
        span = slice(4 * k, 4 * k + 4)
        first_ref[span], second_ref[span] = to_send(edges[0][k], edges[1][k], "th")


def rims(got, ext, owners, slots):
    strip = jax.ShapeDtypeStruct((12, ext.shape[2]), F32)
    return pl.pallas_call(
        functools.partial(rims_kernel, owners, slots),
        out_shape=(
            jax.ShapeDtypeStruct((owners * slots, 256), BF16),
            jax.ShapeDtypeStruct((owners * slots, 128), BF16),
            jax.ShapeDtypeStruct((128, owners), I32),
            jax.ShapeDtypeStruct((owners, 128), I32),
            strip,
            strip,
        ),
        compiler_params=pltpu.CompilerParams(vmem_limit_bytes=16 << 20),
        name="rims",
    )(got, ext)


def around(x):
    rows, cols = x.shape
    return (
        pltpu.roll(x, 1, 0) + pltpu.roll(x, rows - 1, 0)
    ) + (pltpu.roll(x, 1, 1) + pltpu.roll(x, cols - 1, 1))


def strips_kernel(width, t_hbm, hc_hbm, c_hbm, first_ref, second_ref, parts_ref, sems):
    cols = t_hbm.shape[1]
    copies = []
    for k, ref in enumerate((t_hbm, hc_hbm, c_hbm)):
        for side, at in enumerate((0, cols - 128)):
            copies.append(
                pltpu.make_async_copy(
                    ref.at[:, pl.ds(at, 128)], parts_ref.at[2 * k + side], sems.at[2 * k + side]
                )
            )
    for copy in copies:
        copy.start()
    for k in range(3):
        span = slice(RIM * k, RIM * k + RIM)
        copies[2 * k].wait()
        copies[2 * k + 1].wait()
        low = parts_ref[2 * k].T[:RIM]
        high = pltpu.roll(parts_ref[2 * k + 1].T[128 - RIM :], width, 0)
        first_ref[span], second_ref[span] = to_send(low, high, "em")


def strips(t, hc, c, width):
    shape = jax.ShapeDtypeStruct((3 * RIM, t.shape[0]), F32)
    return pl.pallas_call(
        functools.partial(strips_kernel, width),
        out_shape=(shape, shape),
        in_specs=[pl.BlockSpec(memory_space=pltpu.HBM)] * 3,
        scratch_shapes=[pltpu.VMEM((6, t.shape[0], 128), F32), pltpu.SemaphoreType.DMA((6,))],
        compiler_params=pltpu.CompilerParams(vmem_limit_bytes=16 << 20),
        name="strips",
    )(t, hc, c)


def sides(left, right, width, rows):
    lane = iota((rows, 128), 1)
    none = jnp.zeros((128 - RIM, rows), F32)
    left, right = (jnp.concatenate([x, none], axis=0).T for x in (left, right))
    left = pltpu.roll(left, 128 - width, 1)
    return jnp.where(lane >= 128 - width, left, jnp.where(lane < width, right, 0.0))


def prepare_kernel(width, count, t_ref, hc_ref, c_ref, first_ref, second_ref, ext_ref):
    rows, cols = t_ref.shape
    left, right = received(first_ref[...], second_ref[...], "em", count)
    for k, ref in enumerate((t_ref, hc_ref, c_ref)):
        span = slice(RIM * k, RIM * k + RIM)
        ext_ref[k, :, :cols] = ref[...]
        ext_ref[k, :, cols:] = sides(left[span], right[span], width, rows)
    hc = ext_ref[1]
    c = ext_ref[2]
    diag = hc + 4.0 * c
    g = jnp.where(diag > 0.0, 1.0 / jnp.where(diag > 0.0, diag, 1.0), 0.0)
    ext_ref[1] = c * g
    ext_ref[2] = g


def prepare(t, hc, c, first, second, width):
    rows, cols = t.shape
    return pl.pallas_call(
        functools.partial(prepare_kernel, width, lax.axis_size("em")),
        out_shape=jax.ShapeDtypeStruct((3, rows, cols + SIDE), F32),
        compiler_params=pltpu.CompilerParams(vmem_limit_bytes=16 << 20),
        name="prepare",
    )(t, hc, c, first, second)


def middle_kernel(sweeps, slots, pair_ref, rims_ref, flat_ref, ext_ref, temp_ref, top_ref, bottom_ref, rhs_ref):
    rows, cols = temp_ref.shape
    groups = cols // 128
    flat = flat_ref[...]
    own, left, right = (places(flat, 4 * slots + k * slots, slots) for k in range(3))
    shape = (rows, own.shape[1])
    row = iota(shape, 0)
    match = lambda x, first: select(jnp.broadcast_to(x - first, shape) == row)
    for q in range(groups + 1):
        span = slice(q * 128, (q + 1) * 128)
        if q == groups:
            heat = side_columns(
                *(
                    jnp.dot(match(*x), rims_ref[...], preferred_element_type=F32)
                    for x in ((left, (groups - 1) * rows), (right, 0))
                )
            )
        else:
            heat = joined(jnp.dot(match(own, q * rows), pair_ref[...], preferred_element_type=F32))
        rhs_ref[:, span] = source(ext_ref[0, :, span], ext_ref[1, :, span], ext_ref[2, :, span], heat)
    for k, ref in enumerate((ext_ref.at[0], ext_ref.at[1], rhs_ref)):
        top_ref[k] = ref[: 2 * RIM]
        bottom_ref[k] = ref[rows - 2 * RIM :]
    temp = ext_ref[0]
    for _ in range(sweeps):
        temp = rhs_ref[...] + ext_ref[1] * around(temp)
    temp_ref[...] = temp[:, :cols]


def middle(pair, rim, flat, ext, cols, sweeps, slots):
    _, rows, wide = ext.shape
    strip = jax.ShapeDtypeStruct((3, 2 * RIM, wide), F32)
    return pl.pallas_call(
        functools.partial(middle_kernel, sweeps, slots),
        out_shape=(jax.ShapeDtypeStruct((rows, cols), F32), strip, strip),
        scratch_shapes=[pltpu.VMEM((rows, wide), F32)],
        compiler_params=pltpu.CompilerParams(vmem_limit_bytes=16 << 20),
        name="middle",
    )(pair, rim, flat, ext)


def solve_kernel(sweeps, owners, slots, count, first_ref, second_ref, inner_ref, top_ref, bottom_ref, ids_ref, out_ref, reply_ref, temp_ref, pair_ref, sems):
    rows, cols = inner_ref.shape
    inside = pl.ds(RIM, rows - 2 * RIM)
    writes = [pltpu.make_async_copy(inner_ref.at[inside], out_ref.at[inside], sems.at[0])]
    writes[0].start()
    none = jnp.zeros((4, top_ref.shape[2]), F32)
    groups = cols // 128
    for q in range(groups):
        high, low = halves(inner_ref[:, q * 128 : (q + 1) * 128])
        pair_ref[q * rows : (q + 1) * rows, :128] = high
        pair_ref[q * rows : (q + 1) * rows, 128:] = low
    above, below = received(first_ref[...], second_ref[...], "th", count)
    for k, (strip, ref) in enumerate(((above, top_ref), (below, bottom_ref))):
        t, a, r = (
            jnp.concatenate(
                [none, strip[4 * j : 4 * j + 4], ref[j]] if k == 0 else [ref[j], strip[4 * j : 4 * j + 4], none],
                axis=0,
            )
            for j in range(3)
        )
        for _ in range(sweeps):
            t = r + a * around(t)
        t = t[RIM : 2 * RIM, :cols]
        temp_ref[k] = t
        at = k * (rows - RIM)
        write = pltpu.make_async_copy(temp_ref.at[k], out_ref.at[pl.ds(at, RIM)], sems.at[k + 1])
        write.start()
        writes.append(write)
        for q in range(groups):
            span = slice(q * 128, (q + 1) * 128)
            both = [t[:, span], inner_ref[RIM : 2 * RIM, span]]
            if k == 1:
                both = [inner_ref[rows - 2 * RIM : rows - RIM, span], t[:, span]]
            high, low = halves(jnp.concatenate(both, axis=0))
            at = q * rows + k * (rows - 2 * RIM)
            pair_ref[at : at + 2 * RIM, :128] = high
            pair_ref[at : at + 2 * RIM, 128:] = low
    ids = ids_ref[...]
    for r in range(0, slots, 4):
        column = jnp.concatenate(
            [
                jnp.broadcast_to(ids[:, 4 * slots + k : 4 * slots + k + 1], (owners, 128))
                for k in range(r, r + 4)
            ],
            axis=0,
        )
        mask = jnp.concatenate(
            [column == iota((4 * owners, 128), 1) + 128 * k for k in range(rows * groups // 128)], axis=1
        )
        got = joined(jnp.dot(select(mask), pair_ref[...], preferred_element_type=F32))
        for k in range(4):
            reply_ref[pl.ds(r + k, owners, stride=slots), :] = got[k * owners : (k + 1) * owners]
    for write in writes:
        write.wait()


def solve(first, second, inner, top, bottom, ids, sweeps, owners, slots):
    rows, cols = inner.shape
    return pl.pallas_call(
        functools.partial(solve_kernel, sweeps, owners, slots, lax.axis_size("th")),
        out_shape=(
            jax.ShapeDtypeStruct((rows, cols), F32),
            jax.ShapeDtypeStruct((owners * slots, 128), F32),
        ),
        out_specs=(pl.BlockSpec(memory_space=pltpu.HBM), pl.BlockSpec(memory_space=pltpu.VMEM)),
        scratch_shapes=[
            pltpu.VMEM((2, RIM, cols), F32),
            pltpu.VMEM((rows * cols // 128, 256), BF16),
            pltpu.SemaphoreType.DMA((3,)),
        ],
        compiler_params=pltpu.CompilerParams(vmem_limit_bytes=16 << 20),
        name="solve",
    )(first, second, inner, top, bottom, ids)


def final_kernel(slot_ref, back_ref, sg_ref, tc_ref, out_ref, pair_ref, new_ref, sems):
    total = back_ref.shape[0]
    blocks = slot_ref.shape[0]
    high, low = halves(back_ref[...])
    pair_ref[:, :128] = high
    pair_ref[:, 128:] = low
    slot = slot_ref[...].T
    writes = []
    for b in range(0, blocks, 4):
        column = jnp.concatenate(
            [jnp.broadcast_to(slot[:, k : k + 1], (128, 128)) for k in range(b, b + 4)], axis=0
        )
        mask = jnp.concatenate(
            [column == iota((512, 128), 1) + 128 * k for k in range(total // 128)], axis=1
        )
        hot = joined(jnp.dot(select(mask), pair_ref[...], preferred_element_type=F32))
        span = pl.ds(b * 128, 512)
        new_ref[span, :] = sg_ref[span, :] / (1.0 + tc_ref[span, :] * hot)
        write = pltpu.make_async_copy(new_ref.at[span], out_ref.at[span], sems.at[b // 4])
        write.start()
        writes.append(write)
    for write in writes:
        write.wait()


def final(slot, back, sg, tc):
    return pl.pallas_call(
        final_kernel,
        out_shape=jax.ShapeDtypeStruct(sg.shape, F32),
        out_specs=pl.BlockSpec(memory_space=pltpu.HBM),
        scratch_shapes=[
            pltpu.VMEM((back.shape[0], 256), BF16),
            pltpu.VMEM(sg.shape, F32),
            pltpu.SemaphoreType.DMA((slot.shape[0] // 4,)),
        ],
        compiler_params=pltpu.CompilerParams(vmem_limit_bytes=16 << 20),
        name="final",
    )(slot, back, sg, tc)


def traded(first, second, axis):
    n_em, n_th = lax.axis_size("em"), lax.axis_size("th")
    near, far = [], []
    for e in range(n_em):
        for t in range(n_th):
            if axis == "em":
                mate = (e + 1 if e % 2 else e - 1) % n_em, t
                close = e ^ 1, t
            else:
                mate = e, t + 1 if t % 2 else t - 1
                mate = mate if 0 <= mate[1] < n_th else (e ^ 1, t)
                close = e, t ^ 1
            near.append((e * n_th + t, close[0] * n_th + close[1]))
            far.append((e * n_th + t, mate[0] * n_th + mate[1]))
    return lax.ppermute(first, ("em", "th"), near), lax.ppermute(second, ("em", "th"), far)


def exchanged(x, owners):
    rows = x.shape[0]
    x = x.reshape(owners, 1, rows // owners * 128)
    x = lax.all_to_all(x, ("em", "th"), split_axis=0, concat_axis=0, tiled=True)
    return x.reshape(rows, 128)


SWEEPS = 3


def pinned(*arrays):
    return [pltpu.with_memory_space_constraint(x, pltpu.HBM) for x in arrays]


def local(e_real, e_imag, sigma_em, temp_coef, dest_dev, dest_tile, t_old, heat_cap, conduct):
    owners = lax.axis_size("em") * lax.axis_size("th")
    slots = 2 * e_real.shape[0] // owners
    rows, cols = t_old.shape
    near = lax.axis_size("th")
    send, slot = route(dest_dev, dest_tile, e_real, e_imag, sigma_em, owners, slots, rows, near)
    got = exchanged(send, owners)
    grid = pinned(*lax.optimization_barrier((t_old, heat_cap, conduct, slot))[:3])
    ext = prepare(*grid, *traded(*strips(*grid, SWEEPS), "em"), SWEEPS)
    pair, rim, flat, ids, first, second = rims(got, ext, owners, slots)
    first, second = traded(first, second, "th")
    inner, top, bottom = middle(pair, rim, flat, ext, cols, SWEEPS, slots)
    temp, reply = solve(first, second, inner, top, bottom, ids, SWEEPS, owners, slots)
    back = exchanged(reply, owners)
    return temp, final(slot, back, sigma_em, temp_coef)


def solution(mesh):
    tiles = P(("em", "th"), None)
    grid = P("th", "em")
    return jax.shard_map(
        local,
        mesh=mesh,
        in_specs=(tiles,) * 6 + (grid,) * 3,
        out_specs=(grid, tiles),
        check_vma=False,
    )
```

```python
import functools
import jax
import jax.numpy as jnp
from jax import lax
from jax.experimental import pallas as pl
from jax.experimental.pallas import tpu as pltpu
from jax.sharding import PartitionSpec as P

F32 = jnp.float32
BF16 = jnp.bfloat16
I32 = jnp.int32
RIM = 8
SIDE = 128


def iota(shape, dim):
    return lax.broadcasted_iota(I32, shape, dim)


def to_send(low, high, axis):
    even = lax.axis_index(axis) % 2 == 0
    return jnp.where(even, high, low), jnp.where(even, low, high)


def received(first, second, axis, count):
    me = lax.axis_index(axis)
    even = me % 2 == 0
    low = jnp.where(me > 0, jnp.where(even, second, first), 0.0)
    high = jnp.where(me < count - 1, jnp.where(even, first, second), 0.0)
    return low, high


def halves(x):
    high = x.astype(BF16)
    low = (x - high.astype(F32)).astype(BF16)
    return high, low


def select(mask):
    return jnp.where(mask, 1.0, 0.0).astype(BF16)


def joined(y):
    return y[:, :128] + y[:, 128:]


def route_kernel(owners, slots, rows, near, dev_hbm, tile_hbm, er_hbm, ei_hbm, sg_hbm, out_ref, slot_ref, dev_ref, tile_ref, er_ref, ei_ref, sg_ref, pair_ref, send_ref, ids_ref, rims_ref, sems, out_sems):
    count = er_ref.shape[0]
    blocks = count // 128
    copies = [
        pltpu.make_async_copy(source, target, sems.at[k])
        for k, (source, target) in enumerate(
            (
                (dev_hbm, dev_ref),
                (tile_hbm, tile_ref),
                (er_hbm, er_ref),
                (ei_hbm, ei_ref),
                (sg_hbm, sg_ref),
            )
        )
    ]
    for copy in copies:
        copy.start()
    copies[0].wait()
    copies[1].wait()
    dev = dev_ref[...]
    tile = tile_ref[...]
    tile = (tile & 3) * rows + (tile >> 2)
    hits = [jnp.broadcast_to(dev[b : b + 1], (owners, 128)) == iota((owners, 128), 0) for b in range(blocks)]
    ahead = select(iota((128, 256), 0) < iota((128, 256), 1))
    sums = jnp.dot(
        jnp.concatenate([select(h) for h in hits], axis=0), ahead, preferred_element_type=F32
    )
    carry = jnp.zeros((owners, 128), F32)
    ranks = []
    for b in range(blocks):
        part = sums[b * owners : (b + 1) * owners]
        ranks.append(
            jnp.sum(jnp.where(hits[b], part[:, :128] + carry, 0.0), axis=0, keepdims=True)
        )
        carry = carry + part[:, 128:]
    rank = jnp.concatenate(ranks, axis=0).astype(I32)
    slot_ref[...] = dev * slots + rank
    line = lambda x: jnp.concatenate([x[b : b + 1] for b in range(blocks)], axis=1)
    place = line(dev * (slots + 1) + rank)
    hit = jnp.concatenate(hits, axis=1)
    tiles = line(tile)
    upper = jnp.where(hit, jnp.broadcast_to(tiles >> 5, (owners, count)), 0)
    lower = jnp.where(hit, jnp.broadcast_to(tiles & 31, (owners, count)), 0)
    numbers = jnp.concatenate([upper, lower], axis=0).astype(F32).astype(BF16)
    which = select(jnp.broadcast_to(line(rank), (128, count)) == iota((128, count), 0))
    ids = lax.dot_general(
        numbers, which, (((1,), (1,)), ((), ())), preferred_element_type=F32
    )
    none = jnp.zeros((near, 128), F32)
    for ref in (ids_ref, rims_ref):
        ref[:near] = none
        ref[near + owners :] = none
    ids_ref[near : near + owners] = ids[:owners] * 32.0 + ids[owners:]
    for copy in copies[2:]:
        copy.wait()
    er = er_ref[...]
    ei = ei_ref[...]
    high, low = halves(sg_ref[...] * (er * er + ei * ei))
    pair_ref[:, :128] = high
    pair_ref[:, 128:] = low
    part = 2 * near
    step = part * (slots + 1)
    lane = iota((part, 128), 1)
    own_at, left_at, right_at = (4 * slots + k * slots for k in range(3))
    writes = []
    for c in range(owners // part + 1):
        if c < owners // part:
            mask = jnp.broadcast_to(place, (step, count)) == iota((step, count), 0) + c * step
            send_ref[c * step : (c + 1) * step, :] = joined(
                jnp.dot(select(mask), pair_ref[...], preferred_element_type=F32)
            )
            rims = jnp.zeros((part, 128), F32)
            for r in range(slots):
                values = send_ref[pl.ds(c * step + r, part, stride=slots + 1), :]
                rims = jnp.where(lane >> 2 == r, pltpu.roll(values, 2 + 4 * r, 1), rims)
            rims_ref[near + c * part : near + (c + 1) * part] = rims
        if c > 0:
            at = (c - 1) * part
            left, own, right = (slice(at + k * near, at + k * near + part) for k in range(3))
            info = jnp.where(lane & 3 < 2, rims_ref[left], rims_ref[right])
            info = jnp.where(lane >= own_at, pltpu.roll(ids_ref[own], own_at, 1), info)
            info = jnp.where(lane >= left_at, pltpu.roll(ids_ref[left], left_at, 1), info)
            info = jnp.where(lane >= right_at, pltpu.roll(ids_ref[right], right_at, 1), info)
            send_ref[pl.ds((c - 1) * step + slots, part, stride=slots + 1), :] = info
            span = pl.ds((c - 1) * step, step)
            write = pltpu.make_async_copy(send_ref.at[span], out_ref.at[span], out_sems.at[c - 1])
            write.start()
            writes.append(write)
    for write in writes:
        write.wait()


def route(dev, tile, er, ei, sg, owners, slots, rows, near):
    count = er.shape[0]
    return pl.pallas_call(
        functools.partial(route_kernel, owners, slots, rows, near),
        out_shape=(
            jax.ShapeDtypeStruct((owners * (slots + 1), 128), F32),
            jax.ShapeDtypeStruct((count // 128, 128), I32),
        ),
        in_specs=[pl.BlockSpec(memory_space=pltpu.HBM)] * 5,
        out_specs=(pl.BlockSpec(memory_space=pltpu.HBM), pl.BlockSpec(memory_space=pltpu.VMEM)),
        scratch_shapes=[
            pltpu.VMEM((count // 128, 128), I32),
            pltpu.VMEM((count // 128, 128), I32),
            pltpu.VMEM((count, 128), F32),
            pltpu.VMEM((count, 128), F32),
            pltpu.VMEM((count, 128), F32),
            pltpu.VMEM((count, 256), BF16),
            pltpu.VMEM((owners * (slots + 1), 128), F32),
            pltpu.VMEM((owners + 2 * near, 128), F32),
            pltpu.VMEM((owners + 2 * near, 128), F32),
            pltpu.SemaphoreType.DMA((5,)),
            pltpu.SemaphoreType.DMA((owners // (2 * near),)),
        ],
        compiler_params=pltpu.CompilerParams(vmem_limit_bytes=16 << 20),
        name="route",
    )(*pinned(dev.reshape(count // 128, 128), tile.reshape(count // 128, 128), er, ei, sg))


def source(t, a, g, heat):
    return t * (1.0 - 4.0 * a) + g * heat


def places(flat, first, slots):
    return jnp.concatenate([flat[first + r : first + r + 1] for r in range(slots)], axis=1)


def side_columns(low, high):
    lane = iota(low.shape, 1)
    low, high = (pltpu.roll(x + pltpu.roll(x, 124, 1), 126, 1) for x in (low, high))
    return jnp.where(lane >= 126, low, jnp.where(lane < 2, high, 0.0))


def rims_kernel(owners, slots, got_ref, ext_ref, pair_ref, rims_ref, flat_ref, ids_ref, first_ref, second_ref):
    rows = ext_ref.shape[1]
    groups = ext_ref.shape[2] // 128 - 1
    info = got_ref[pl.ds(slots, owners, stride=slots + 1), :]
    ids_ref[...] = info.astype(I32)
    flat = info.T.astype(I32)
    flat_ref[...] = flat
    lane = iota((owners, 128), 1)
    for r in range(slots):
        span = slice(r * owners, (r + 1) * owners)
        high, low = halves(got_ref[pl.ds(r, owners, stride=slots + 1), :])
        pair_ref[span, :128] = high
        pair_ref[span, 128:] = low
        values = pltpu.roll(info, (128 - 4 * r) % 128, 1)
        high = values.astype(BF16).astype(F32)
        low = pltpu.roll(values - high, 4, 1)
        rims_ref[span, :] = jnp.where(lane < 4, high, low).astype(BF16)
    own, left, right = (places(flat, 4 * slots + k * slots, slots) for k in range(3))
    shape = (8 * groups, owners * slots)
    line = iota(shape, 0)
    row = line & 7
    row = row + jnp.where(row < 4, 0, rows - 8)
    mask = jnp.broadcast_to(own, shape) == (line >> 3) * rows + row
    heat = joined(jnp.dot(select(mask), pair_ref[...], preferred_element_type=F32))
    shape = (16, owners * slots)
    line = iota(shape, 0)
    row = line & 7
    row = row + jnp.where(row < 4, 0, rows - 8)
    mask = jnp.where(
        line < 8,
        jnp.broadcast_to(left, shape) - (groups - 1) * rows,
        jnp.broadcast_to(right, shape),
    ) == row
    side = jnp.dot(select(mask), rims_ref[...], preferred_element_type=F32)
    side = side_columns(side[:8], side[8:])
    edges = []
    for at, rim in ((0, slice(0, 4)), (4, slice(rows - 4, rows))):
        loss = [heat[8 * q + at : 8 * q + at + 4] for q in range(groups)] + [side[at : at + 4]]
        t, a = ext_ref[0, rim], ext_ref[1, rim]
        edges.append((t, a, source(t, a, ext_ref[2, rim], jnp.concatenate(loss, axis=1))))
    for k in range(3):
        span = slice(4 * k, 4 * k + 4)
        first_ref[span], second_ref[span] = to_send(edges[0][k], edges[1][k], "th")


def rims(got, ext, owners, slots):
    strip = jax.ShapeDtypeStruct((12, ext.shape[2]), F32)
    return pl.pallas_call(
        functools.partial(rims_kernel, owners, slots),
        out_shape=(
            jax.ShapeDtypeStruct((owners * slots, 256), BF16),
            jax.ShapeDtypeStruct((owners * slots, 128), BF16),
            jax.ShapeDtypeStruct((128, owners), I32),
            jax.ShapeDtypeStruct((owners, 128), I32),
            strip,
            strip,
        ),
        compiler_params=pltpu.CompilerParams(vmem_limit_bytes=16 << 20),
        name="rims",
    )(got, ext)


def around(x):
    rows, cols = x.shape
    return (
        pltpu.roll(x, 1, 0) + pltpu.roll(x, rows - 1, 0)
    ) + (pltpu.roll(x, 1, 1) + pltpu.roll(x, cols - 1, 1))


def strips_kernel(width, t_hbm, hc_hbm, c_hbm, first_ref, second_ref, parts_ref, sems):
    cols = t_hbm.shape[1]
    copies = []
    for k, ref in enumerate((t_hbm, hc_hbm, c_hbm)):
        for side, at in enumerate((0, cols - 128)):
            copies.append(
                pltpu.make_async_copy(
                    ref.at[:, pl.ds(at, 128)], parts_ref.at[2 * k + side], sems.at[2 * k + side]
                )
            )
    for copy in copies:
        copy.start()
    for k in range(3):
        span = slice(RIM * k, RIM * k + RIM)
        copies[2 * k].wait()
        copies[2 * k + 1].wait()
        low = parts_ref[2 * k].T[:RIM]
        high = pltpu.roll(parts_ref[2 * k + 1].T[128 - RIM :], width, 0)
        first_ref[span], second_ref[span] = to_send(low, high, "em")


def strips(t, hc, c, width):
    shape = jax.ShapeDtypeStruct((3 * RIM, t.shape[0]), F32)
    return pl.pallas_call(
        functools.partial(strips_kernel, width),
        out_shape=(shape, shape),
        in_specs=[pl.BlockSpec(memory_space=pltpu.HBM)] * 3,
        scratch_shapes=[pltpu.VMEM((6, t.shape[0], 128), F32), pltpu.SemaphoreType.DMA((6,))],
        compiler_params=pltpu.CompilerParams(vmem_limit_bytes=16 << 20),
        name="strips",
    )(t, hc, c)


def sides(left, right, width, rows):
    lane = iota((rows, 128), 1)
    none = jnp.zeros((128 - RIM, rows), F32)
    left, right = (jnp.concatenate([x, none], axis=0).T for x in (left, right))
    left = pltpu.roll(left, 128 - width, 1)
    return jnp.where(lane >= 128 - width, left, jnp.where(lane < width, right, 0.0))


def prepare_kernel(width, count, t_ref, hc_ref, c_ref, first_ref, second_ref, ext_ref):
    rows, cols = t_ref.shape
    left, right = received(first_ref[...], second_ref[...], "em", count)
    for k, ref in enumerate((t_ref, hc_ref, c_ref)):
        span = slice(RIM * k, RIM * k + RIM)
        ext_ref[k, :, :cols] = ref[...]
        ext_ref[k, :, cols:] = sides(left[span], right[span], width, rows)
    hc = ext_ref[1]
    c = ext_ref[2]
    diag = hc + 4.0 * c
    g = jnp.where(diag > 0.0, 1.0 / jnp.where(diag > 0.0, diag, 1.0), 0.0)
    ext_ref[1] = c * g
    ext_ref[2] = g


def prepare(t, hc, c, first, second, width):
    rows, cols = t.shape
    return pl.pallas_call(
        functools.partial(prepare_kernel, width, lax.axis_size("em")),
        out_shape=jax.ShapeDtypeStruct((3, rows, cols + SIDE), F32),
        compiler_params=pltpu.CompilerParams(vmem_limit_bytes=16 << 20),
        name="prepare",
    )(t, hc, c, first, second)


def middle_kernel(sweeps, slots, pair_ref, rims_ref, flat_ref, ids_ref, ext_ref, out_ref, top_ref, bottom_ref, reply_ref, rhs_ref, temp_ref, tiles_ref, sems):
    rows, cols = out_ref.shape
    owners = ids_ref.shape[0]
    groups = cols // 128
    flat = flat_ref[...]
    own, left, right = (places(flat, 4 * slots + k * slots, slots) for k in range(3))
    shape = (rows, own.shape[1])
    row = iota(shape, 0)
    match = lambda x, first: select(jnp.broadcast_to(x - first, shape) == row)
    for q in range(groups + 1):
        span = slice(q * 128, (q + 1) * 128)
        if q == groups:
            heat = side_columns(
                *(
                    jnp.dot(match(*x), rims_ref[...], preferred_element_type=F32)
                    for x in ((left, (groups - 1) * rows), (right, 0))
                )
            )
        else:
            heat = joined(jnp.dot(match(own, q * rows), pair_ref[...], preferred_element_type=F32))
        rhs_ref[:, span] = source(ext_ref[0, :, span], ext_ref[1, :, span], ext_ref[2, :, span], heat)
    for k, ref in enumerate((ext_ref.at[0], ext_ref.at[1], rhs_ref)):
        top_ref[k] = ref[: 2 * RIM]
        bottom_ref[k] = ref[rows - 2 * RIM :]
    temp = ext_ref[0]
    for _ in range(sweeps):
        temp = rhs_ref[...] + ext_ref[1] * around(temp)
    temp_ref[...] = temp[:, :cols]
    inside = pl.ds(RIM, rows - 2 * RIM)
    write = pltpu.make_async_copy(temp_ref.at[inside], out_ref.at[inside], sems.at[0])
    write.start()
    row = iota((rows, 128), 0)
    inner = (row >= RIM) & (row < rows - RIM)
    for q in range(groups):
        high, low = halves(jnp.where(inner, temp[:, q * 128 : (q + 1) * 128], 0.0))
        tiles_ref[q * rows : (q + 1) * rows, :128] = high
        tiles_ref[q * rows : (q + 1) * rows, 128:] = low
    for r in range(0, slots, 4):
        column = slot_columns(ids_ref[...], 4 * slots + r, owners)
        mask = jnp.concatenate(
            [column == iota((4 * owners, 128), 1) + 128 * k for k in range(rows * groups // 128)], axis=1
        )
        reply_ref[r * owners : (r + 4) * owners] = joined(
            jnp.dot(select(mask), tiles_ref[...], preferred_element_type=F32)
        )
    write.wait()


def slot_columns(ids, first, owners):
    return jnp.concatenate(
        [jnp.broadcast_to(ids[:, k : k + 1], (owners, 128)) for k in range(first, first + 4)], axis=0
    )


def middle(pair, rim, flat, ids, ext, cols, sweeps, slots):
    _, rows, wide = ext.shape
    strip = jax.ShapeDtypeStruct((3, 2 * RIM, wide), F32)
    onchip = pl.BlockSpec(memory_space=pltpu.VMEM)
    return pl.pallas_call(
        functools.partial(middle_kernel, sweeps, slots),
        out_shape=(
            jax.ShapeDtypeStruct((rows, cols), F32),
            strip,
            strip,
            jax.ShapeDtypeStruct((slots * ids.shape[0], 128), F32),
        ),
        out_specs=(pl.BlockSpec(memory_space=pltpu.HBM), onchip, onchip, onchip),
        scratch_shapes=[
            pltpu.VMEM((rows, wide), F32),
            pltpu.VMEM((rows, cols), F32),
            pltpu.VMEM((rows * cols // 128, 256), BF16),
            pltpu.SemaphoreType.DMA((1,)),
        ],
        compiler_params=pltpu.CompilerParams(vmem_limit_bytes=16 << 20),
        name="middle",
    )(pair, rim, flat, ids, ext)


def solve_kernel(sweeps, slots, count, first_ref, second_ref, top_ref, bottom_ref, ids_ref, part_ref, inner_ref, out_ref, reply_ref, temp_ref, tiles_ref, sems):
    rows, cols = out_ref.shape
    owners = ids_ref.shape[0]
    groups = cols // 128
    none = jnp.zeros((4, top_ref.shape[2]), F32)
    above, below = received(first_ref[...], second_ref[...], "th", count)
    writes, edges = [], []
    for k, (strip, ref) in enumerate(((above, top_ref), (below, bottom_ref))):
        t, a, r = (
            jnp.concatenate(
                [none, strip[4 * j : 4 * j + 4], ref[j]] if k == 0 else [ref[j], strip[4 * j : 4 * j + 4], none],
                axis=0,
            )
            for j in range(3)
        )
        for _ in range(sweeps):
            t = r + a * around(t)
        t = t[RIM : 2 * RIM, :cols]
        edges.append(t)
        temp_ref[k] = t
        write = pltpu.make_async_copy(
            temp_ref.at[k], out_ref.at[pl.ds(k * (rows - RIM), RIM)], sems.at[k]
        )
        write.start()
        writes.append(write)
    for q in range(128 // (2 * RIM)):
        both = jnp.zeros((2 * RIM, 128), F32)
        if q < groups:
            both = jnp.concatenate([t[:, q * 128 : (q + 1) * 128] for t in edges], axis=0)
        high, low = halves(both)
        tiles_ref[2 * RIM * q : 2 * RIM * (q + 1), :128] = high
        tiles_ref[2 * RIM * q : 2 * RIM * (q + 1), 128:] = low
    ids = ids_ref[...]
    bits = rows.bit_length() - 1
    row = ids & (rows - 1)
    line = jnp.where(row < RIM, row, jnp.where(row >= rows - RIM, row - (rows - 2 * RIM), -128))
    code = (ids >> bits) * (2 * RIM) + line
    lane = iota((4 * owners, 128), 1)
    for r in range(0, slots, 4):
        mask = slot_columns(code, 4 * slots + r, owners) == lane
        got = part_ref[r * owners : (r + 4) * owners] + joined(
            jnp.dot(select(mask), tiles_ref[...], preferred_element_type=F32)
        )
        for k in range(4):
            reply_ref[pl.ds(r + k, owners, stride=slots), :] = got[k * owners : (k + 1) * owners]
    for write in writes:
        write.wait()


def solve(first, second, top, bottom, ids, part, inner, sweeps, owners, slots):
    rows, cols = inner.shape
    onchip = pl.BlockSpec(memory_space=pltpu.VMEM)
    return pl.pallas_call(
        functools.partial(solve_kernel, sweeps, slots, lax.axis_size("th")),
        out_shape=(
            jax.ShapeDtypeStruct((rows, cols), F32),
            jax.ShapeDtypeStruct((owners * slots, 128), F32),
        ),
        in_specs=[onchip] * 6 + [pl.BlockSpec(memory_space=pltpu.HBM)],
        out_specs=(pl.BlockSpec(memory_space=pltpu.HBM), onchip),
        scratch_shapes=[
            pltpu.VMEM((2, RIM, cols), F32),
            pltpu.VMEM((128, 256), BF16),
            pltpu.SemaphoreType.DMA((2,)),
        ],
        input_output_aliases={6: 0},
        compiler_params=pltpu.CompilerParams(vmem_limit_bytes=16 << 20),
        name="solve",
    )(first, second, top, bottom, ids, part, inner)


def final_kernel(slot_ref, back_ref, sg_ref, tc_ref, out_ref, pair_ref, new_ref, sems):
    total = back_ref.shape[0]
    blocks = slot_ref.shape[0]
    high, low = halves(back_ref[...])
    pair_ref[:, :128] = high
    pair_ref[:, 128:] = low
    slot = slot_ref[...].T
    writes = []
    for b in range(0, blocks, 4):
        column = jnp.concatenate(
            [jnp.broadcast_to(slot[:, k : k + 1], (128, 128)) for k in range(b, b + 4)], axis=0
        )
        mask = jnp.concatenate(
            [column == iota((512, 128), 1) + 128 * k for k in range(total // 128)], axis=1
        )
        hot = joined(jnp.dot(select(mask), pair_ref[...], preferred_element_type=F32))
        span = pl.ds(b * 128, 512)
        new_ref[span, :] = sg_ref[span, :] / (1.0 + tc_ref[span, :] * hot)
        write = pltpu.make_async_copy(new_ref.at[span], out_ref.at[span], sems.at[b // 4])
        write.start()
        writes.append(write)
    for write in writes:
        write.wait()


def final(slot, back, sg, tc):
    return pl.pallas_call(
        final_kernel,
        out_shape=jax.ShapeDtypeStruct(sg.shape, F32),
        out_specs=pl.BlockSpec(memory_space=pltpu.HBM),
        scratch_shapes=[
            pltpu.VMEM((back.shape[0], 256), BF16),
            pltpu.VMEM(sg.shape, F32),
            pltpu.SemaphoreType.DMA((slot.shape[0] // 4,)),
        ],
        compiler_params=pltpu.CompilerParams(vmem_limit_bytes=16 << 20),
        name="final",
    )(slot, back, sg, tc)


def traded(first, second, axis):
    n_em, n_th = lax.axis_size("em"), lax.axis_size("th")
    near, far = [], []
    for e in range(n_em):
        for t in range(n_th):
            if axis == "em":
                mate = (e + 1 if e % 2 else e - 1) % n_em, t
                close = e ^ 1, t
            else:
                mate = e, t + 1 if t % 2 else t - 1
                mate = mate if 0 <= mate[1] < n_th else (e ^ 1, t)
                close = e, t ^ 1
            near.append((e * n_th + t, close[0] * n_th + close[1]))
            far.append((e * n_th + t, mate[0] * n_th + mate[1]))
    return lax.ppermute(first, ("em", "th"), near), lax.ppermute(second, ("em", "th"), far)


def exchanged(x, owners):
    rows = x.shape[0]
    x = x.reshape(owners, 1, rows // owners * 128)
    x = lax.all_to_all(x, ("em", "th"), split_axis=0, concat_axis=0, tiled=True)
    return x.reshape(rows, 128)


SWEEPS = 3


def pinned(*arrays):
    return [pltpu.with_memory_space_constraint(x, pltpu.HBM) for x in arrays]


def local(e_real, e_imag, sigma_em, temp_coef, dest_dev, dest_tile, t_old, heat_cap, conduct):
    owners = lax.axis_size("em") * lax.axis_size("th")
    slots = 2 * e_real.shape[0] // owners
    rows, cols = t_old.shape
    near = lax.axis_size("th")
    send, slot = route(dest_dev, dest_tile, e_real, e_imag, sigma_em, owners, slots, rows, near)
    got = exchanged(send, owners)
    grid = pinned(*lax.optimization_barrier((t_old, heat_cap, conduct, slot))[:3])
    ext = prepare(*grid, *traded(*strips(*grid, SWEEPS), "em"), SWEEPS)
    pair, rim, flat, ids, first, second = rims(got, ext, owners, slots)
    first, second = traded(first, second, "th")
    inner, top, bottom, part = middle(pair, rim, flat, ids, ext, cols, SWEEPS, slots)
    (inner,) = pinned(inner)
    temp, reply = solve(first, second, top, bottom, ids, part, inner, SWEEPS, owners, slots)
    back = exchanged(reply, owners)
    return temp, final(slot, back, sigma_em, temp_coef)


def solution(mesh):
    tiles = P(("em", "th"), None)
    grid = P("th", "em")
    return jax.shard_map(
        local,
        mesh=mesh,
        in_specs=(tiles,) * 6 + (grid,) * 3,
        out_specs=(grid, tiles),
        check_vma=False,
    )
```

```python
import functools
import jax
import jax.numpy as jnp
from jax import lax
from jax.experimental import pallas as pl
from jax.experimental.pallas import tpu as pltpu
from jax.sharding import PartitionSpec as P

F32 = jnp.float32
BF16 = jnp.bfloat16
I32 = jnp.int32
RIM = 8
SIDE = 128


def iota(shape, dim):
    return lax.broadcasted_iota(I32, shape, dim)


def to_send(low, high, axis):
    even = lax.axis_index(axis) % 2 == 0
    return jnp.where(even, high, low), jnp.where(even, low, high)


def received(first, second, axis, count):
    me = lax.axis_index(axis)
    even = me % 2 == 0
    low = jnp.where(me > 0, jnp.where(even, second, first), 0.0)
    high = jnp.where(me < count - 1, jnp.where(even, first, second), 0.0)
    return low, high


def halves(x):
    high = x.astype(BF16)
    low = (x - high.astype(F32)).astype(BF16)
    return high, low


def select(mask):
    return jnp.where(mask, 1.0, 0.0).astype(BF16)


def joined(y):
    return y[:, :128] + y[:, 128:]


def route_kernel(owners, slots, rows, near, dev_hbm, tile_hbm, er_hbm, ei_hbm, sg_hbm, out_ref, slot_ref, dev_ref, tile_ref, er_ref, ei_ref, sg_ref, pair_ref, send_ref, ids_ref, rims_ref, sems, out_sems):
    count = er_ref.shape[0]
    blocks = count // 128
    copies = [
        pltpu.make_async_copy(source, target, sems.at[k])
        for k, (source, target) in enumerate(
            (
                (dev_hbm, dev_ref),
                (tile_hbm, tile_ref),
                (er_hbm, er_ref),
                (ei_hbm, ei_ref),
                (sg_hbm, sg_ref),
            )
        )
    ]
    for copy in copies:
        copy.start()
    copies[0].wait()
    copies[1].wait()
    dev = dev_ref[...]
    tile = tile_ref[...]
    tile = (tile & 3) * rows + (tile >> 2)
    hits = [jnp.broadcast_to(dev[b : b + 1], (owners, 128)) == iota((owners, 128), 0) for b in range(blocks)]
    ahead = select(iota((128, 256), 0) < iota((128, 256), 1))
    sums = jnp.dot(
        jnp.concatenate([select(h) for h in hits], axis=0), ahead, preferred_element_type=F32
    )
    carry = jnp.zeros((owners, 128), F32)
    ranks = []
    for b in range(blocks):
        part = sums[b * owners : (b + 1) * owners]
        ranks.append(
            jnp.sum(jnp.where(hits[b], part[:, :128] + carry, 0.0), axis=0, keepdims=True)
        )
        carry = carry + part[:, 128:]
    rank = jnp.concatenate(ranks, axis=0).astype(I32)
    slot_ref[...] = dev * slots + rank
    line = lambda x: jnp.concatenate([x[b : b + 1] for b in range(blocks)], axis=1)
    place = line(dev * (slots + 1) + rank)
    hit = jnp.concatenate(hits, axis=1)
    tiles = line(tile)
    upper = jnp.where(hit, jnp.broadcast_to(tiles >> 5, (owners, count)), 0)
    lower = jnp.where(hit, jnp.broadcast_to(tiles & 31, (owners, count)), 0)
    numbers = jnp.concatenate([upper, lower], axis=0).astype(F32).astype(BF16)
    which = select(jnp.broadcast_to(line(rank), (128, count)) == iota((128, count), 0))
    ids = lax.dot_general(
        numbers, which, (((1,), (1,)), ((), ())), preferred_element_type=F32
    )
    none = jnp.zeros((near, 128), F32)
    for ref in (ids_ref, rims_ref):
        ref[:near] = none
        ref[near + owners :] = none
    ids_ref[near : near + owners] = ids[:owners] * 32.0 + ids[owners:]
    for copy in copies[2:]:
        copy.wait()
    er = er_ref[...]
    ei = ei_ref[...]
    high, low = halves(sg_ref[...] * (er * er + ei * ei))
    pair_ref[:, :128] = high
    pair_ref[:, 128:] = low
    part = 2 * near
    step = part * (slots + 1)
    lane = iota((part, 128), 1)
    own_at, left_at, right_at = (4 * slots + k * slots for k in range(3))
    writes = []
    for c in range(owners // part + 1):
        if c < owners // part:
            mask = jnp.broadcast_to(place, (step, count)) == iota((step, count), 0) + c * step
            send_ref[c * step : (c + 1) * step, :] = joined(
                jnp.dot(select(mask), pair_ref[...], preferred_element_type=F32)
            )
            rims = jnp.zeros((part, 128), F32)
            for r in range(slots):
                values = send_ref[pl.ds(c * step + r, part, stride=slots + 1), :]
                rims = jnp.where(lane >> 2 == r, pltpu.roll(values, 2 + 4 * r, 1), rims)
            rims_ref[near + c * part : near + (c + 1) * part] = rims
        if c > 0:
            at = (c - 1) * part
            left, own, right = (slice(at + k * near, at + k * near + part) for k in range(3))
            info = jnp.where(lane & 3 < 2, rims_ref[left], rims_ref[right])
            info = jnp.where(lane >= own_at, pltpu.roll(ids_ref[own], own_at, 1), info)
            info = jnp.where(lane >= left_at, pltpu.roll(ids_ref[left], left_at, 1), info)
            info = jnp.where(lane >= right_at, pltpu.roll(ids_ref[right], right_at, 1), info)
            send_ref[pl.ds((c - 1) * step + slots, part, stride=slots + 1), :] = info
            span = pl.ds((c - 1) * step, step)
            write = pltpu.make_async_copy(send_ref.at[span], out_ref.at[span], out_sems.at[c - 1])
            write.start()
            writes.append(write)
    for write in writes:
        write.wait()


def route(dev, tile, er, ei, sg, owners, slots, rows, near):
    count = er.shape[0]
    return pl.pallas_call(
        functools.partial(route_kernel, owners, slots, rows, near),
        out_shape=(
            jax.ShapeDtypeStruct((owners * (slots + 1), 128), F32),
            jax.ShapeDtypeStruct((count // 128, 128), I32),
        ),
        in_specs=[pl.BlockSpec(memory_space=pltpu.HBM)] * 5,
        out_specs=(pl.BlockSpec(memory_space=pltpu.HBM), pl.BlockSpec(memory_space=pltpu.VMEM)),
        scratch_shapes=[
            pltpu.VMEM((count // 128, 128), I32),
            pltpu.VMEM((count // 128, 128), I32),
            pltpu.VMEM((count, 128), F32),
            pltpu.VMEM((count, 128), F32),
            pltpu.VMEM((count, 128), F32),
            pltpu.VMEM((count, 256), BF16),
            pltpu.VMEM((owners * (slots + 1), 128), F32),
            pltpu.VMEM((owners + 2 * near, 128), F32),
            pltpu.VMEM((owners + 2 * near, 128), F32),
            pltpu.SemaphoreType.DMA((5,)),
            pltpu.SemaphoreType.DMA((owners // (2 * near),)),
        ],
        compiler_params=pltpu.CompilerParams(vmem_limit_bytes=16 << 20),
        name="route",
    )(*pinned(dev.reshape(count // 128, 128), tile.reshape(count // 128, 128), er, ei, sg))


def source(t, a, g, heat):
    return t * (1.0 - 4.0 * a) + g * heat


def places(flat, first, slots):
    return jnp.concatenate([flat[first + r : first + r + 1] for r in range(slots)], axis=1)


def side_columns(flat, slots, row, last):
    rows = row.shape[0]
    left, right = (places(flat, k * slots, slots) for k in (5, 6))
    sums = []
    for k, ids in enumerate((left - last, left - last, right, right)):
        value = jnp.concatenate([flat[4 * r + k : 4 * r + k + 1] for r in range(slots)], axis=1)
        hit = jnp.broadcast_to(ids, row.shape) == row
        sums.append(jnp.sum(jnp.where(hit, jnp.broadcast_to(value, row.shape), 0.0), axis=1, keepdims=True))
    lane = iota((rows, 128), 1)
    out = jnp.zeros((rows, 128), F32)
    for at, x in zip((126, 127, 0, 1), sums):
        out = jnp.where(lane == at, jnp.broadcast_to(x, (rows, 128)), out)
    return out


def rims_kernel(owners, slots, got_ref, ext_ref, pair_ref, flat_ref, ids_ref, first_ref, second_ref):
    rows = ext_ref.shape[1]
    groups = ext_ref.shape[2] // 128 - 1
    info = got_ref[pl.ds(slots, owners, stride=slots + 1), :]
    ids_ref[...] = info.astype(I32)
    flat = info.T
    flat_ref[...] = flat
    for r in range(slots):
        span = slice(r * owners, (r + 1) * owners)
        high, low = halves(got_ref[pl.ds(r, owners, stride=slots + 1), :])
        pair_ref[span, :128] = high
        pair_ref[span, 128:] = low
    own = places(flat, 4 * slots, slots)
    shape = (8 * groups, owners * slots)
    line = iota(shape, 0)
    row = line & 7
    row = row + jnp.where(row < 4, 0, rows - 8)
    mask = jnp.broadcast_to(own, shape) == ((line >> 3) * rows + row).astype(F32)
    heat = joined(jnp.dot(select(mask), pair_ref[...], preferred_element_type=F32))
    side = side_columns(flat, slots, row[:8].astype(F32), (groups - 1) * rows)
    edges = []
    for at, rim in ((0, slice(0, 4)), (4, slice(rows - 4, rows))):
        loss = [heat[8 * q + at : 8 * q + at + 4] for q in range(groups)] + [side[at : at + 4]]
        t, a = ext_ref[0, rim], ext_ref[1, rim]
        edges.append((t, a, source(t, a, ext_ref[2, rim], jnp.concatenate(loss, axis=1))))
    for k in range(3):
        span = slice(4 * k, 4 * k + 4)
        first_ref[span], second_ref[span] = to_send(edges[0][k], edges[1][k], "th")


def rims(got, ext, owners, slots):
    strip = jax.ShapeDtypeStruct((12, ext.shape[2]), F32)
    return pl.pallas_call(
        functools.partial(rims_kernel, owners, slots),
        out_shape=(
            jax.ShapeDtypeStruct((owners * slots, 256), BF16),
            jax.ShapeDtypeStruct((128, owners), F32),
            jax.ShapeDtypeStruct((owners, 128), I32),
            strip,
            strip,
        ),
        compiler_params=pltpu.CompilerParams(vmem_limit_bytes=16 << 20),
        name="rims",
    )(got, ext)


def around(x):
    rows, cols = x.shape
    return (
        pltpu.roll(x, 1, 0) + pltpu.roll(x, rows - 1, 0)
    ) + (pltpu.roll(x, 1, 1) + pltpu.roll(x, cols - 1, 1))


def strips_kernel(width, t_hbm, hc_hbm, c_hbm, first_ref, second_ref, parts_ref, sems):
    cols = t_hbm.shape[1]
    copies = []
    for k, ref in enumerate((t_hbm, hc_hbm, c_hbm)):
        for side, at in enumerate((0, cols - 128)):
            copies.append(
                pltpu.make_async_copy(
                    ref.at[:, pl.ds(at, 128)], parts_ref.at[2 * k + side], sems.at[2 * k + side]
                )
            )
    for copy in copies:
        copy.start()
    for k in range(3):
        span = slice(RIM * k, RIM * k + RIM)
        copies[2 * k].wait()
        copies[2 * k + 1].wait()
        low = parts_ref[2 * k].T[:RIM]
        high = pltpu.roll(parts_ref[2 * k + 1].T[128 - RIM :], width, 0)
        first_ref[span], second_ref[span] = to_send(low, high, "em")


def strips(t, hc, c, width):
    shape = jax.ShapeDtypeStruct((3 * RIM, t.shape[0]), F32)
    return pl.pallas_call(
        functools.partial(strips_kernel, width),
        out_shape=(shape, shape),
        in_specs=[pl.BlockSpec(memory_space=pltpu.HBM)] * 3,
        scratch_shapes=[pltpu.VMEM((6, t.shape[0], 128), F32), pltpu.SemaphoreType.DMA((6,))],
        compiler_params=pltpu.CompilerParams(vmem_limit_bytes=16 << 20),
        name="strips",
    )(t, hc, c)


def sides(left, right, width, rows):
    lane = iota((rows, 128), 1)
    none = jnp.zeros((128 - RIM, rows), F32)
    left, right = (jnp.concatenate([x, none], axis=0).T for x in (left, right))
    left = pltpu.roll(left, 128 - width, 1)
    return jnp.where(lane >= 128 - width, left, jnp.where(lane < width, right, 0.0))


def prepare_kernel(width, count, t_ref, hc_ref, c_ref, first_ref, second_ref, ext_ref):
    rows, cols = t_ref.shape
    left, right = received(first_ref[...], second_ref[...], "em", count)
    for k, ref in enumerate((t_ref, hc_ref, c_ref)):
        span = slice(RIM * k, RIM * k + RIM)
        ext_ref[k, :, :cols] = ref[...]
        ext_ref[k, :, cols:] = sides(left[span], right[span], width, rows)
    hc = ext_ref[1]
    c = ext_ref[2]
    diag = hc + 4.0 * c
    g = jnp.where(diag > 0.0, 1.0 / jnp.where(diag > 0.0, diag, 1.0), 0.0)
    ext_ref[1] = c * g
    ext_ref[2] = g


def prepare(t, hc, c, first, second, width):
    rows, cols = t.shape
    return pl.pallas_call(
        functools.partial(prepare_kernel, width, lax.axis_size("em")),
        out_shape=jax.ShapeDtypeStruct((3, rows, cols + SIDE), F32),
        compiler_params=pltpu.CompilerParams(vmem_limit_bytes=16 << 20),
        name="prepare",
    )(t, hc, c, first, second)


def middle_kernel(sweeps, slots, pair_ref, flat_ref, ids_ref, ext_ref, out_ref, top_ref, bottom_ref, reply_ref, rhs_ref, temp_ref, tiles_ref, sems):
    rows, cols = out_ref.shape
    owners = ids_ref.shape[0]
    groups = cols // 128
    flat = flat_ref[...]
    own = places(flat, 4 * slots, slots)
    shape = (rows, own.shape[1])
    row = iota(shape, 0).astype(F32)
    match = lambda x, first: select(jnp.broadcast_to(x - first, shape) == row)
    for q in range(groups + 1):
        span = slice(q * 128, (q + 1) * 128)
        if q == groups:
            heat = side_columns(flat, slots, row, (groups - 1) * rows)
        else:
            heat = joined(jnp.dot(match(own, q * rows), pair_ref[...], preferred_element_type=F32))
        rhs_ref[:, span] = source(ext_ref[0, :, span], ext_ref[1, :, span], ext_ref[2, :, span], heat)
    for k, ref in enumerate((ext_ref.at[0], ext_ref.at[1], rhs_ref)):
        top_ref[k] = ref[: 2 * RIM]
        bottom_ref[k] = ref[rows - 2 * RIM :]
    temp = ext_ref[0]
    for _ in range(sweeps):
        temp = rhs_ref[...] + ext_ref[1] * around(temp)
    temp_ref[...] = temp[:, :cols]
    inside = pl.ds(RIM, rows - 2 * RIM)
    write = pltpu.make_async_copy(temp_ref.at[inside], out_ref.at[inside], sems.at[0])
    write.start()
    row = iota((rows, 128), 0)
    inner = (row >= RIM) & (row < rows - RIM)
    for q in range(groups):
        high, low = halves(jnp.where(inner, temp[:, q * 128 : (q + 1) * 128], 0.0))
        tiles_ref[q * rows : (q + 1) * rows, :128] = high
        tiles_ref[q * rows : (q + 1) * rows, 128:] = low
    for r in range(0, slots, 4):
        column = slot_columns(ids_ref[...], 4 * slots + r, owners)
        mask = jnp.concatenate(
            [column == iota((4 * owners, 128), 1) + 128 * k for k in range(rows * groups // 128)], axis=1
        )
        reply_ref[r * owners : (r + 4) * owners] = joined(
            jnp.dot(select(mask), tiles_ref[...], preferred_element_type=F32)
        )
    write.wait()


def slot_columns(ids, first, owners):
    return jnp.concatenate(
        [jnp.broadcast_to(ids[:, k : k + 1], (owners, 128)) for k in range(first, first + 4)], axis=0
    )


def middle(pair, flat, ids, ext, cols, sweeps, slots):
    _, rows, wide = ext.shape
    strip = jax.ShapeDtypeStruct((3, 2 * RIM, wide), F32)
    onchip = pl.BlockSpec(memory_space=pltpu.VMEM)
    return pl.pallas_call(
        functools.partial(middle_kernel, sweeps, slots),
        out_shape=(
            jax.ShapeDtypeStruct((rows, cols), F32),
            strip,
            strip,
            jax.ShapeDtypeStruct((slots * ids.shape[0], 128), F32),
        ),
        out_specs=(pl.BlockSpec(memory_space=pltpu.HBM), onchip, onchip, onchip),
        scratch_shapes=[
            pltpu.VMEM((rows, wide), F32),
            pltpu.VMEM((rows, cols), F32),
            pltpu.VMEM((rows * cols // 128, 256), BF16),
            pltpu.SemaphoreType.DMA((1,)),
        ],
        compiler_params=pltpu.CompilerParams(vmem_limit_bytes=16 << 20),
        name="middle",
    )(pair, flat, ids, ext)


def solve_kernel(sweeps, slots, count, first_ref, second_ref, top_ref, bottom_ref, ids_ref, part_ref, inner_ref, out_ref, reply_ref, temp_ref, tiles_ref, sems):
    rows, cols = out_ref.shape
    owners = ids_ref.shape[0]
    groups = cols // 128
    none = jnp.zeros((4, top_ref.shape[2]), F32)
    above, below = received(first_ref[...], second_ref[...], "th", count)
    writes, edges = [], []
    for k, (strip, ref) in enumerate(((above, top_ref), (below, bottom_ref))):
        t, a, r = (
            jnp.concatenate(
                [none, strip[4 * j : 4 * j + 4], ref[j]] if k == 0 else [ref[j], strip[4 * j : 4 * j + 4], none],
                axis=0,
            )
            for j in range(3)
        )
        for _ in range(sweeps):
            t = r + a * around(t)
        t = t[RIM : 2 * RIM, :cols]
        edges.append(t)
        temp_ref[k] = t
        write = pltpu.make_async_copy(
            temp_ref.at[k], out_ref.at[pl.ds(k * (rows - RIM), RIM)], sems.at[k]
        )
        write.start()
        writes.append(write)
    for q in range(128 // (2 * RIM)):
        both = jnp.zeros((2 * RIM, 128), F32)
        if q < groups:
            both = jnp.concatenate([t[:, q * 128 : (q + 1) * 128] for t in edges], axis=0)
        high, low = halves(both)
        tiles_ref[2 * RIM * q : 2 * RIM * (q + 1), :128] = high
        tiles_ref[2 * RIM * q : 2 * RIM * (q + 1), 128:] = low
    ids = ids_ref[...]
    bits = rows.bit_length() - 1
    row = ids & (rows - 1)
    line = jnp.where(row < RIM, row, jnp.where(row >= rows - RIM, row - (rows - 2 * RIM), -128))
    code = (ids >> bits) * (2 * RIM) + line
    lane = iota((4 * owners, 128), 1)
    for r in range(0, slots, 4):
        mask = slot_columns(code, 4 * slots + r, owners) == lane
        got = part_ref[r * owners : (r + 4) * owners] + joined(
            jnp.dot(select(mask), tiles_ref[...], preferred_element_type=F32)
        )
        for k in range(4):
            reply_ref[pl.ds(r + k, owners, stride=slots), :] = got[k * owners : (k + 1) * owners]
    for write in writes:
        write.wait()


def solve(first, second, top, bottom, ids, part, inner, sweeps, owners, slots):
    rows, cols = inner.shape
    onchip = pl.BlockSpec(memory_space=pltpu.VMEM)
    return pl.pallas_call(
        functools.partial(solve_kernel, sweeps, slots, lax.axis_size("th")),
        out_shape=(
            jax.ShapeDtypeStruct((rows, cols), F32),
            jax.ShapeDtypeStruct((owners * slots, 128), F32),
        ),
        in_specs=[onchip] * 6 + [pl.BlockSpec(memory_space=pltpu.HBM)],
        out_specs=(pl.BlockSpec(memory_space=pltpu.HBM), onchip),
        scratch_shapes=[
            pltpu.VMEM((2, RIM, cols), F32),
            pltpu.VMEM((128, 256), BF16),
            pltpu.SemaphoreType.DMA((2,)),
        ],
        input_output_aliases={6: 0},
        compiler_params=pltpu.CompilerParams(vmem_limit_bytes=16 << 20),
        name="solve",
    )(first, second, top, bottom, ids, part, inner)


def final_kernel(slot_ref, back_ref, sg_ref, tc_ref, out_ref, pair_ref, new_ref, sems):
    total = back_ref.shape[0]
    blocks = slot_ref.shape[0]
    high, low = halves(back_ref[...])
    pair_ref[:, :128] = high
    pair_ref[:, 128:] = low
    slot = slot_ref[...].T
    writes = []
    for b in range(0, blocks, 2):
        column = jnp.concatenate(
            [jnp.broadcast_to(slot[:, k : k + 1], (128, 128)) for k in range(b, b + 2)], axis=0
        )
        mask = jnp.concatenate(
            [column == iota((256, 128), 1) + 128 * k for k in range(total // 128)], axis=1
        )
        hot = joined(jnp.dot(select(mask), pair_ref[...], preferred_element_type=F32))
        span = pl.ds(b * 128, 256)
        new_ref[span, :] = sg_ref[span, :] / (1.0 + tc_ref[span, :] * hot)
        write = pltpu.make_async_copy(new_ref.at[span], out_ref.at[span], sems.at[b // 2])
        write.start()
        writes.append(write)
    for write in writes:
        write.wait()


def final(slot, back, sg, tc):
    return pl.pallas_call(
        final_kernel,
        out_shape=jax.ShapeDtypeStruct(sg.shape, F32),
        out_specs=pl.BlockSpec(memory_space=pltpu.HBM),
        scratch_shapes=[
            pltpu.VMEM((back.shape[0], 256), BF16),
            pltpu.VMEM(sg.shape, F32),
            pltpu.SemaphoreType.DMA((slot.shape[0] // 2,)),
        ],
        compiler_params=pltpu.CompilerParams(vmem_limit_bytes=16 << 20),
        name="final",
    )(slot, back, sg, tc)


def traded(first, second, axis):
    n_em, n_th = lax.axis_size("em"), lax.axis_size("th")
    near, far = [], []
    for e in range(n_em):
        for t in range(n_th):
            if axis == "em":
                mate = (e + 1 if e % 2 else e - 1) % n_em, t
                close = e ^ 1, t
            else:
                mate = e, t + 1 if t % 2 else t - 1
                mate = mate if 0 <= mate[1] < n_th else (e ^ 1, t)
                close = e, t ^ 1
            near.append((e * n_th + t, close[0] * n_th + close[1]))
            far.append((e * n_th + t, mate[0] * n_th + mate[1]))
    return lax.ppermute(first, ("em", "th"), near), lax.ppermute(second, ("em", "th"), far)


def exchanged(x, owners):
    rows = x.shape[0]
    x = x.reshape(owners, 1, rows // owners * 128)
    x = lax.all_to_all(x, ("em", "th"), split_axis=0, concat_axis=0, tiled=True)
    return x.reshape(rows, 128)


SWEEPS = 3


def pinned(*arrays):
    return [pltpu.with_memory_space_constraint(x, pltpu.HBM) for x in arrays]


def local(e_real, e_imag, sigma_em, temp_coef, dest_dev, dest_tile, t_old, heat_cap, conduct):
    owners = lax.axis_size("em") * lax.axis_size("th")
    slots = 2 * e_real.shape[0] // owners
    rows, cols = t_old.shape
    near = lax.axis_size("th")
    send, slot = route(dest_dev, dest_tile, e_real, e_imag, sigma_em, owners, slots, rows, near)
    got = exchanged(send, owners)
    grid = pinned(*lax.optimization_barrier((t_old, heat_cap, conduct, slot))[:3])
    ext = prepare(*grid, *traded(*strips(*grid, SWEEPS), "em"), SWEEPS)
    pair, flat, ids, first, second = rims(got, ext, owners, slots)
    first, second = traded(first, second, "th")
    inner, top, bottom, part = middle(pair, flat, ids, ext, cols, SWEEPS, slots)
    (inner,) = pinned(inner)
    temp, reply = solve(first, second, top, bottom, ids, part, inner, SWEEPS, owners, slots)
    back = exchanged(reply, owners)
    return temp, final(slot, back, sigma_em, temp_coef)


def solution(mesh):
    tiles = P(("em", "th"), None)
    grid = P("th", "em")
    return jax.shard_map(
        local,
        mesh=mesh,
        in_specs=(tiles,) * 6 + (grid,) * 3,
        out_specs=(grid, tiles),
        check_vma=False,
    )
```

```python
import functools
import jax
import jax.numpy as jnp
from jax import lax
from jax.experimental import pallas as pl
from jax.experimental.pallas import tpu as pltpu
from jax.sharding import PartitionSpec as P

F32 = jnp.float32
BF16 = jnp.bfloat16
I32 = jnp.int32
RIM = 8
SIDE = 128


def iota(shape, dim):
    return lax.broadcasted_iota(I32, shape, dim)


def to_send(low, high, axis):
    even = lax.axis_index(axis) % 2 == 0
    return jnp.where(even, high, low), jnp.where(even, low, high)


def received(first, second, axis, count):
    me = lax.axis_index(axis)
    even = me % 2 == 0
    low = jnp.where(me > 0, jnp.where(even, second, first), 0.0)
    high = jnp.where(me < count - 1, jnp.where(even, first, second), 0.0)
    return low, high


def halves(x):
    high = x.astype(BF16)
    low = (x - high.astype(F32)).astype(BF16)
    return high, low


def select(mask):
    return jnp.where(mask, 1.0, 0.0).astype(BF16)


def joined(y):
    return y[:, :128] + y[:, 128:]


def route_kernel(owners, slots, rows, near, dev_hbm, tile_hbm, er_hbm, ei_hbm, sg_hbm, out_ref, slot_ref, dev_ref, tile_ref, er_ref, ei_ref, sg_ref, pair_ref, send_ref, ids_ref, rims_ref, sems, out_sems):
    count = er_ref.shape[0]
    blocks = count // 128
    copies = [
        pltpu.make_async_copy(source, target, sems.at[k])
        for k, (source, target) in enumerate(
            (
                (dev_hbm, dev_ref),
                (tile_hbm, tile_ref),
                (er_hbm, er_ref),
                (ei_hbm, ei_ref),
                (sg_hbm, sg_ref),
            )
        )
    ]
    for copy in copies:
        copy.start()
    copies[0].wait()
    copies[1].wait()
    dev = dev_ref[...]
    tile = tile_ref[...]
    tile = (tile & 3) * rows + (tile >> 2)
    hits = [jnp.broadcast_to(dev[b : b + 1], (owners, 128)) == iota((owners, 128), 0) for b in range(blocks)]
    ahead = select(iota((128, 256), 0) < iota((128, 256), 1))
    sums = jnp.dot(
        jnp.concatenate([select(h) for h in hits], axis=0), ahead, preferred_element_type=F32
    )
    carry = jnp.zeros((owners, 128), F32)
    ranks = []
    for b in range(blocks):
        part = sums[b * owners : (b + 1) * owners]
        ranks.append(
            jnp.sum(jnp.where(hits[b], part[:, :128] + carry, 0.0), axis=0, keepdims=True)
        )
        carry = carry + part[:, 128:]
    rank = jnp.concatenate(ranks, axis=0).astype(I32)
    slot_ref[...] = dev * slots + rank
    line = lambda x: jnp.concatenate([x[b : b + 1] for b in range(blocks)], axis=1)
    place = line(dev * (slots + 1) + rank)
    hit = jnp.concatenate(hits, axis=1)
    tiles = line(tile)
    upper = jnp.where(hit, jnp.broadcast_to(tiles >> 5, (owners, count)), 0)
    lower = jnp.where(hit, jnp.broadcast_to(tiles & 31, (owners, count)), 0)
    numbers = jnp.concatenate([upper, lower], axis=0).astype(F32).astype(BF16)
    which = select(jnp.broadcast_to(line(rank), (128, count)) == iota((128, count), 0))
    ids = lax.dot_general(
        numbers, which, (((1,), (1,)), ((), ())), preferred_element_type=F32
    )
    none = jnp.zeros((near, 128), F32)
    for ref in (ids_ref, rims_ref):
        ref[:near] = none
        ref[near + owners :] = none
    ids_ref[near : near + owners] = ids[:owners] * 32.0 + ids[owners:]
    for copy in copies[2:]:
        copy.wait()
    er = er_ref[...]
    ei = ei_ref[...]
    high, low = halves(sg_ref[...] * (er * er + ei * ei))
    pair_ref[:, :128] = high
    pair_ref[:, 128:] = low
    part = 2 * near
    step = part * (slots + 1)
    lane = iota((part, 128), 1)
    own_at, left_at, right_at = (4 * slots + k * slots for k in range(3))
    writes = []
    for c in range(owners // part + 1):
        if c < owners // part:
            mask = jnp.broadcast_to(place, (step, count)) == iota((step, count), 0) + c * step
            send_ref[c * step : (c + 1) * step, :] = joined(
                jnp.dot(select(mask), pair_ref[...], preferred_element_type=F32)
            )
            rims = jnp.zeros((part, 128), F32)
            for r in range(slots):
                values = send_ref[pl.ds(c * step + r, part, stride=slots + 1), :]
                rims = jnp.where(lane >> 2 == r, pltpu.roll(values, 2 + 4 * r, 1), rims)
            rims_ref[near + c * part : near + (c + 1) * part] = rims
        if c > 0:
            at = (c - 1) * part
            left, own, right = (slice(at + k * near, at + k * near + part) for k in range(3))
            info = jnp.where(lane & 3 < 2, rims_ref[left], rims_ref[right])
            info = jnp.where(lane >= own_at, pltpu.roll(ids_ref[own], own_at, 1), info)
            info = jnp.where(lane >= left_at, pltpu.roll(ids_ref[left], left_at, 1), info)
            info = jnp.where(lane >= right_at, pltpu.roll(ids_ref[right], right_at, 1), info)
            send_ref[pl.ds((c - 1) * step + slots, part, stride=slots + 1), :] = info
            span = pl.ds((c - 1) * step, step)
            write = pltpu.make_async_copy(send_ref.at[span], out_ref.at[span], out_sems.at[c - 1])
            write.start()
            writes.append(write)
    for write in writes:
        write.wait()


def route(dev, tile, er, ei, sg, owners, slots, rows, near):
    count = er.shape[0]
    return pl.pallas_call(
        functools.partial(route_kernel, owners, slots, rows, near),
        out_shape=(
            jax.ShapeDtypeStruct((owners * (slots + 1), 128), F32),
            jax.ShapeDtypeStruct((count // 128, 128), I32),
        ),
        in_specs=[pl.BlockSpec(memory_space=pltpu.HBM)] * 5,
        out_specs=(pl.BlockSpec(memory_space=pltpu.HBM), pl.BlockSpec(memory_space=pltpu.VMEM)),
        scratch_shapes=[
            pltpu.VMEM((count // 128, 128), I32),
            pltpu.VMEM((count // 128, 128), I32),
            pltpu.VMEM((count, 128), F32),
            pltpu.VMEM((count, 128), F32),
            pltpu.VMEM((count, 128), F32),
            pltpu.VMEM((count, 256), BF16),
            pltpu.VMEM((owners * (slots + 1), 128), F32),
            pltpu.VMEM((owners + 2 * near, 128), F32),
            pltpu.VMEM((owners + 2 * near, 128), F32),
            pltpu.SemaphoreType.DMA((5,)),
            pltpu.SemaphoreType.DMA((owners // (2 * near),)),
        ],
        compiler_params=pltpu.CompilerParams(vmem_limit_bytes=16 << 20),
        name="route",
    )(*pinned(dev.reshape(count // 128, 128), tile.reshape(count // 128, 128), er, ei, sg))


def source(t, a, g, heat):
    return t * (1.0 - 4.0 * a) + g * heat


def places(flat, first, slots):
    return jnp.concatenate([flat[first + r : first + r + 1] for r in range(slots)], axis=1)


def side_columns(flat, slots, row, last):
    rows = row.shape[0]
    left, right = (places(flat, k * slots, slots) for k in (5, 6))
    sums = []
    for k, ids in enumerate((left - last, left - last, right, right)):
        value = jnp.concatenate([flat[4 * r + k : 4 * r + k + 1] for r in range(slots)], axis=1)
        hit = jnp.broadcast_to(ids, row.shape) == row
        sums.append(jnp.sum(jnp.where(hit, jnp.broadcast_to(value, row.shape), 0.0), axis=1, keepdims=True))
    lane = iota((rows, 128), 1)
    out = jnp.zeros((rows, 128), F32)
    for at, x in zip((126, 127, 0, 1), sums):
        out = jnp.where(lane == at, jnp.broadcast_to(x, (rows, 128)), out)
    return out


def all_side_columns(flat, slots, rows, last):
    wide = slots * flat.shape[1]
    left, right = (places(flat, k * slots, slots).astype(I32) for k in (5, 6))
    left = left - last
    value = jnp.concatenate([flat[4 * r : 4 * r + 4] for r in range(slots)], axis=1)
    high = value.astype(BF16).astype(F32)
    value = jnp.concatenate([high, value - high], axis=0)
    pick = lambda x: jnp.broadcast_to(x, (8, wide))
    group = jnp.where(iota((8, wide), 0) & 3 < 2, pick(left >> 4), pick(right >> 4))
    spread = [jnp.where(group == k, value, 0.0) for k in range(rows // 16)]
    spread = jnp.concatenate(spread, axis=0).astype(BF16)
    pick = lambda x: jnp.broadcast_to(x & 15, (16, wide)) == iota((16, wide), 0)
    within = jnp.concatenate([select(pick(left)), select(pick(right))], axis=0)
    sums = lax.dot_general(
        within, spread, (((1,), (1,)), ((), ())), preferred_element_type=F32
    )
    sums = sums + pltpu.roll(sums, 124, 1)
    lane = iota((16, 128), 1)
    sums = jnp.where(lane & 3 < 2, sums[:16], sums[16:])
    ends = (lane >= 126) | (lane < 2)
    parts = [jnp.where(ends, pltpu.roll(sums, 126 - 8 * k, 1), 0.0) for k in range(rows // 16)]
    return jnp.concatenate(parts, axis=0)


def rims_kernel(owners, slots, got_ref, ext_ref, pair_ref, flat_ref, ids_ref, first_ref, second_ref):
    rows = ext_ref.shape[1]
    groups = ext_ref.shape[2] // 128 - 1
    info = got_ref[pl.ds(slots, owners, stride=slots + 1), :]
    ids_ref[...] = info.astype(I32)
    flat = info.T
    flat_ref[...] = flat
    for r in range(slots):
        span = slice(r * owners, (r + 1) * owners)
        high, low = halves(got_ref[pl.ds(r, owners, stride=slots + 1), :])
        pair_ref[span, :128] = high
        pair_ref[span, 128:] = low
    own = places(flat, 4 * slots, slots)
    shape = (8 * groups, owners * slots)
    line = iota(shape, 0)
    row = line & 7
    row = row + jnp.where(row < 4, 0, rows - 8)
    mask = jnp.broadcast_to(own, shape) == ((line >> 3) * rows + row).astype(F32)
    heat = joined(jnp.dot(select(mask), pair_ref[...], preferred_element_type=F32))
    side = side_columns(flat, slots, row[:8].astype(F32), (groups - 1) * rows)
    edges = []
    for at, rim in ((0, slice(0, 4)), (4, slice(rows - 4, rows))):
        loss = [heat[8 * q + at : 8 * q + at + 4] for q in range(groups)] + [side[at : at + 4]]
        t, a = ext_ref[0, rim], ext_ref[1, rim]
        edges.append((t, a, source(t, a, ext_ref[2, rim], jnp.concatenate(loss, axis=1))))
    for k in range(3):
        span = slice(4 * k, 4 * k + 4)
        first_ref[span], second_ref[span] = to_send(edges[0][k], edges[1][k], "th")


def rims(got, ext, owners, slots):
    strip = jax.ShapeDtypeStruct((12, ext.shape[2]), F32)
    return pl.pallas_call(
        functools.partial(rims_kernel, owners, slots),
        out_shape=(
            jax.ShapeDtypeStruct((owners * slots, 256), BF16),
            jax.ShapeDtypeStruct((128, owners), F32),
            jax.ShapeDtypeStruct((owners, 128), I32),
            strip,
            strip,
        ),
        compiler_params=pltpu.CompilerParams(vmem_limit_bytes=16 << 20),
        name="rims",
    )(got, ext)


def around(x):
    rows, cols = x.shape
    return (
        pltpu.roll(x, 1, 0) + pltpu.roll(x, rows - 1, 0)
    ) + (pltpu.roll(x, 1, 1) + pltpu.roll(x, cols - 1, 1))


def strips_kernel(width, t_hbm, hc_hbm, c_hbm, first_ref, second_ref, parts_ref, sems):
    cols = t_hbm.shape[1]
    copies = []
    for k, ref in enumerate((t_hbm, hc_hbm, c_hbm)):
        for side, at in enumerate((0, cols - 128)):
            copies.append(
                pltpu.make_async_copy(
                    ref.at[:, pl.ds(at, 128)], parts_ref.at[2 * k + side], sems.at[2 * k + side]
                )
            )
    for copy in copies:
        copy.start()
    for k in range(3):
        span = slice(RIM * k, RIM * k + RIM)
        copies[2 * k].wait()
        copies[2 * k + 1].wait()
        low = parts_ref[2 * k].T[:RIM]
        high = pltpu.roll(parts_ref[2 * k + 1].T[128 - RIM :], width, 0)
        first_ref[span], second_ref[span] = to_send(low, high, "em")


def strips(t, hc, c, width):
    shape = jax.ShapeDtypeStruct((3 * RIM, t.shape[0]), F32)
    return pl.pallas_call(
        functools.partial(strips_kernel, width),
        out_shape=(shape, shape),
        in_specs=[pl.BlockSpec(memory_space=pltpu.HBM)] * 3,
        scratch_shapes=[pltpu.VMEM((6, t.shape[0], 128), F32), pltpu.SemaphoreType.DMA((6,))],
        compiler_params=pltpu.CompilerParams(vmem_limit_bytes=16 << 20),
        name="strips",
    )(t, hc, c)


def sides(left, right, width, rows):
    lane = iota((rows, 128), 1)
    none = jnp.zeros((128 - RIM, rows), F32)
    left, right = (jnp.concatenate([x, none], axis=0).T for x in (left, right))
    left = pltpu.roll(left, 128 - width, 1)
    return jnp.where(lane >= 128 - width, left, jnp.where(lane < width, right, 0.0))


def prepare_kernel(width, count, t_ref, hc_ref, c_ref, first_ref, second_ref, ext_ref):
    rows, cols = t_ref.shape
    left, right = received(first_ref[...], second_ref[...], "em", count)
    for k, ref in enumerate((t_ref, hc_ref, c_ref)):
        span = slice(RIM * k, RIM * k + RIM)
        ext_ref[k, :, :cols] = ref[...]
        ext_ref[k, :, cols:] = sides(left[span], right[span], width, rows)
    hc = ext_ref[1]
    c = ext_ref[2]
    diag = hc + 4.0 * c
    g = jnp.where(diag > 0.0, 1.0 / jnp.where(diag > 0.0, diag, 1.0), 0.0)
    ext_ref[1] = c * g
    ext_ref[2] = g


def prepare(t, hc, c, first, second, width):
    rows, cols = t.shape
    return pl.pallas_call(
        functools.partial(prepare_kernel, width, lax.axis_size("em")),
        out_shape=jax.ShapeDtypeStruct((3, rows, cols + SIDE), F32),
        compiler_params=pltpu.CompilerParams(vmem_limit_bytes=16 << 20),
        name="prepare",
    )(t, hc, c, first, second)


def middle_kernel(sweeps, slots, pair_ref, flat_ref, ids_ref, ext_ref, out_ref, top_ref, bottom_ref, reply_ref, rhs_ref, temp_ref, tiles_ref, sems):
    rows, cols = out_ref.shape
    owners = ids_ref.shape[0]
    groups = cols // 128
    flat = flat_ref[...]
    own = places(flat, 4 * slots, slots)
    shape = (rows, own.shape[1])
    row = iota(shape, 0).astype(F32)
    match = lambda x, first: select(jnp.broadcast_to(x - first, shape) == row)
    for q in range(groups + 1):
        span = slice(q * 128, (q + 1) * 128)
        if q == groups:
            heat = all_side_columns(flat, slots, rows, (groups - 1) * rows)
        else:
            heat = joined(jnp.dot(match(own, q * rows), pair_ref[...], preferred_element_type=F32))
        rhs_ref[:, span] = source(ext_ref[0, :, span], ext_ref[1, :, span], ext_ref[2, :, span], heat)
    for k, ref in enumerate((ext_ref.at[0], ext_ref.at[1], rhs_ref)):
        top_ref[k] = ref[: 2 * RIM]
        bottom_ref[k] = ref[rows - 2 * RIM :]
    temp = ext_ref[0]
    for _ in range(sweeps):
        temp = rhs_ref[...] + ext_ref[1] * around(temp)
    temp_ref[...] = temp[:, :cols]
    inside = pl.ds(RIM, rows - 2 * RIM)
    write = pltpu.make_async_copy(temp_ref.at[inside], out_ref.at[inside], sems.at[0])
    write.start()
    row = iota((rows, 128), 0)
    inner = (row >= RIM) & (row < rows - RIM)
    for q in range(groups):
        high, low = halves(jnp.where(inner, temp[:, q * 128 : (q + 1) * 128], 0.0))
        tiles_ref[q * rows : (q + 1) * rows, :128] = high
        tiles_ref[q * rows : (q + 1) * rows, 128:] = low
    for r in range(0, slots, 4):
        column = slot_columns(ids_ref[...], 4 * slots + r, owners)
        mask = jnp.concatenate(
            [column == iota((4 * owners, 128), 1) + 128 * k for k in range(rows * groups // 128)], axis=1
        )
        reply_ref[r * owners : (r + 4) * owners] = joined(
            jnp.dot(select(mask), tiles_ref[...], preferred_element_type=F32)
        )
    write.wait()


def slot_columns(ids, first, owners):
    return jnp.concatenate(
        [jnp.broadcast_to(ids[:, k : k + 1], (owners, 128)) for k in range(first, first + 4)], axis=0
    )


def middle(pair, flat, ids, ext, cols, sweeps, slots):
    _, rows, wide = ext.shape
    strip = jax.ShapeDtypeStruct((3, 2 * RIM, wide), F32)
    onchip = pl.BlockSpec(memory_space=pltpu.VMEM)
    return pl.pallas_call(
        functools.partial(middle_kernel, sweeps, slots),
        out_shape=(
            jax.ShapeDtypeStruct((rows, cols), F32),
            strip,
            strip,
            jax.ShapeDtypeStruct((slots * ids.shape[0], 128), F32),
        ),
        out_specs=(pl.BlockSpec(memory_space=pltpu.HBM), onchip, onchip, onchip),
        scratch_shapes=[
            pltpu.VMEM((rows, wide), F32),
            pltpu.VMEM((rows, cols), F32),
            pltpu.VMEM((rows * cols // 128, 256), BF16),
            pltpu.SemaphoreType.DMA((1,)),
        ],
        compiler_params=pltpu.CompilerParams(vmem_limit_bytes=16 << 20),
        name="middle",
    )(pair, flat, ids, ext)


def solve_kernel(sweeps, slots, count, first_ref, second_ref, top_ref, bottom_ref, ids_ref, part_ref, inner_ref, out_ref, reply_ref, temp_ref, tiles_ref, sems):
    rows, cols = out_ref.shape
    owners = ids_ref.shape[0]
    groups = cols // 128
    none = jnp.zeros((4, top_ref.shape[2]), F32)
    above, below = received(first_ref[...], second_ref[...], "th", count)
    writes, edges = [], []
    for k, (strip, ref) in enumerate(((above, top_ref), (below, bottom_ref))):
        t, a, r = (
            jnp.concatenate(
                [none, strip[4 * j : 4 * j + 4], ref[j]] if k == 0 else [ref[j], strip[4 * j : 4 * j + 4], none],
                axis=0,
            )
            for j in range(3)
        )
        for _ in range(sweeps):
            t = r + a * around(t)
        t = t[RIM : 2 * RIM, :cols]
        edges.append(t)
        temp_ref[k] = t
        write = pltpu.make_async_copy(
            temp_ref.at[k], out_ref.at[pl.ds(k * (rows - RIM), RIM)], sems.at[k]
        )
        write.start()
        writes.append(write)
    for q in range(128 // (2 * RIM)):
        both = jnp.zeros((2 * RIM, 128), F32)
        if q < groups:
            both = jnp.concatenate([t[:, q * 128 : (q + 1) * 128] for t in edges], axis=0)
        high, low = halves(both)
        tiles_ref[2 * RIM * q : 2 * RIM * (q + 1), :128] = high
        tiles_ref[2 * RIM * q : 2 * RIM * (q + 1), 128:] = low
    ids = ids_ref[...]
    bits = rows.bit_length() - 1
    row = ids & (rows - 1)
    line = jnp.where(row < RIM, row, jnp.where(row >= rows - RIM, row - (rows - 2 * RIM), -128))
    code = (ids >> bits) * (2 * RIM) + line
    lane = iota((4 * owners, 128), 1)
    for r in range(0, slots, 4):
        mask = slot_columns(code, 4 * slots + r, owners) == lane
        got = part_ref[r * owners : (r + 4) * owners] + joined(
            jnp.dot(select(mask), tiles_ref[...], preferred_element_type=F32)
        )
        for k in range(4):
            reply_ref[pl.ds(r + k, owners, stride=slots), :] = got[k * owners : (k + 1) * owners]
    for write in writes:
        write.wait()


def solve(first, second, top, bottom, ids, part, inner, sweeps, owners, slots):
    rows, cols = inner.shape
    onchip = pl.BlockSpec(memory_space=pltpu.VMEM)
    return pl.pallas_call(
        functools.partial(solve_kernel, sweeps, slots, lax.axis_size("th")),
        out_shape=(
            jax.ShapeDtypeStruct((rows, cols), F32),
            jax.ShapeDtypeStruct((owners * slots, 128), F32),
        ),
        in_specs=[onchip] * 6 + [pl.BlockSpec(memory_space=pltpu.HBM)],
        out_specs=(pl.BlockSpec(memory_space=pltpu.HBM), onchip),
        scratch_shapes=[
            pltpu.VMEM((2, RIM, cols), F32),
            pltpu.VMEM((128, 256), BF16),
            pltpu.SemaphoreType.DMA((2,)),
        ],
        input_output_aliases={6: 0},
        compiler_params=pltpu.CompilerParams(vmem_limit_bytes=16 << 20),
        name="solve",
    )(first, second, top, bottom, ids, part, inner)


def final_kernel(slot_ref, back_ref, sg_ref, tc_ref, out_ref, pair_ref, new_ref, sems):
    total = back_ref.shape[0]
    blocks = slot_ref.shape[0]
    high, low = halves(back_ref[...])
    pair_ref[:, :128] = high
    pair_ref[:, 128:] = low
    slot = slot_ref[...].T
    writes = []
    for b in range(0, blocks, 2):
        column = jnp.concatenate(
            [jnp.broadcast_to(slot[:, k : k + 1], (128, 128)) for k in range(b, b + 2)], axis=0
        )
        mask = jnp.concatenate(
            [column == iota((256, 128), 1) + 128 * k for k in range(total // 128)], axis=1
        )
        hot = joined(jnp.dot(select(mask), pair_ref[...], preferred_element_type=F32))
        span = pl.ds(b * 128, 256)
        new_ref[span, :] = sg_ref[span, :] / (1.0 + tc_ref[span, :] * hot)
        write = pltpu.make_async_copy(new_ref.at[span], out_ref.at[span], sems.at[b // 2])
        write.start()
        writes.append(write)
    for write in writes:
        write.wait()


def final(slot, back, sg, tc):
    return pl.pallas_call(
        final_kernel,
        out_shape=jax.ShapeDtypeStruct(sg.shape, F32),
        out_specs=pl.BlockSpec(memory_space=pltpu.HBM),
        scratch_shapes=[
            pltpu.VMEM((back.shape[0], 256), BF16),
            pltpu.VMEM(sg.shape, F32),
            pltpu.SemaphoreType.DMA((slot.shape[0] // 2,)),
        ],
        compiler_params=pltpu.CompilerParams(vmem_limit_bytes=16 << 20),
        name="final",
    )(slot, back, sg, tc)


def traded(first, second, axis):
    n_em, n_th = lax.axis_size("em"), lax.axis_size("th")
    near, far = [], []
    for e in range(n_em):
        for t in range(n_th):
            if axis == "em":
                mate = (e + 1 if e % 2 else e - 1) % n_em, t
                close = e ^ 1, t
            else:
                mate = e, t + 1 if t % 2 else t - 1
                mate = mate if 0 <= mate[1] < n_th else (e ^ 1, t)
                close = e, t ^ 1
            near.append((e * n_th + t, close[0] * n_th + close[1]))
            far.append((e * n_th + t, mate[0] * n_th + mate[1]))
    return lax.ppermute(first, ("em", "th"), near), lax.ppermute(second, ("em", "th"), far)


def exchanged(x, owners):
    rows = x.shape[0]
    x = x.reshape(owners, 1, rows // owners * 128)
    x = lax.all_to_all(x, ("em", "th"), split_axis=0, concat_axis=0, tiled=True)
    return x.reshape(rows, 128)


SWEEPS = 3


def pinned(*arrays):
    return [pltpu.with_memory_space_constraint(x, pltpu.HBM) for x in arrays]


def local(e_real, e_imag, sigma_em, temp_coef, dest_dev, dest_tile, t_old, heat_cap, conduct):
    owners = lax.axis_size("em") * lax.axis_size("th")
    slots = 2 * e_real.shape[0] // owners
    rows, cols = t_old.shape
    near = lax.axis_size("th")
    send, slot = route(dest_dev, dest_tile, e_real, e_imag, sigma_em, owners, slots, rows, near)
    got = exchanged(send, owners)
    grid = pinned(*lax.optimization_barrier((t_old, heat_cap, conduct, slot))[:3])
    ext = prepare(*grid, *traded(*strips(*grid, SWEEPS), "em"), SWEEPS)
    pair, flat, ids, first, second = rims(got, ext, owners, slots)
    first, second = traded(first, second, "th")
    inner, top, bottom, part = middle(pair, flat, ids, ext, cols, SWEEPS, slots)
    (inner,) = pinned(inner)
    temp, reply = solve(first, second, top, bottom, ids, part, inner, SWEEPS, owners, slots)
    back = exchanged(reply, owners)
    return temp, final(slot, back, sigma_em, temp_coef)


def solution(mesh):
    tiles = P(("em", "th"), None)
    grid = P("th", "em")
    return jax.shard_map(
        local,
        mesh=mesh,
        in_specs=(tiles,) * 6 + (grid,) * 3,
        out_specs=(grid, tiles),
        check_vma=False,
    )
```

```python
import functools
import jax
import jax.numpy as jnp
from jax import lax
from jax.experimental import pallas as pl
from jax.experimental.pallas import tpu as pltpu
from jax.sharding import PartitionSpec as P

F32 = jnp.float32
BF16 = jnp.bfloat16
I32 = jnp.int32
RIM = 8
SIDE = 128


def iota(shape, dim):
    return lax.broadcasted_iota(I32, shape, dim)


def to_send(low, high, axis):
    even = lax.axis_index(axis) % 2 == 0
    return jnp.where(even, high, low), jnp.where(even, low, high)


def received(first, second, axis, count):
    me = lax.axis_index(axis)
    even = me % 2 == 0
    low = jnp.where(me > 0, jnp.where(even, second, first), 0.0)
    high = jnp.where(me < count - 1, jnp.where(even, first, second), 0.0)
    return low, high


def halves(x):
    high = x.astype(BF16)
    low = (x - high.astype(F32)).astype(BF16)
    return high, low


def select(mask):
    return jnp.where(mask, 1.0, 0.0).astype(BF16)


def joined(y):
    return y[:, :128] + y[:, 128:]


def route_kernel(owners, slots, rows, near, dev_hbm, tile_hbm, er_hbm, ei_hbm, sg_hbm, out_ref, slot_ref, dev_ref, tile_ref, er_ref, ei_ref, sg_ref, pair_ref, send_ref, ids_ref, rims_ref, sems, out_sems):
    count = er_ref.shape[0]
    blocks = count // 128
    copies = [
        pltpu.make_async_copy(source, target, sems.at[k])
        for k, (source, target) in enumerate(
            (
                (dev_hbm, dev_ref),
                (tile_hbm, tile_ref),
                (er_hbm, er_ref),
                (ei_hbm, ei_ref),
                (sg_hbm, sg_ref),
            )
        )
    ]
    for copy in copies:
        copy.start()
    copies[0].wait()
    copies[1].wait()
    dev = dev_ref[...]
    tile = tile_ref[...]
    tile = (tile & 3) * rows + (tile >> 2)
    hits = [jnp.broadcast_to(dev[b : b + 1], (owners, 128)) == iota((owners, 128), 0) for b in range(blocks)]
    ahead = select(iota((128, 256), 0) < iota((128, 256), 1))
    sums = jnp.dot(
        jnp.concatenate([select(h) for h in hits], axis=0), ahead, preferred_element_type=F32
    )
    carry = jnp.zeros((owners, 128), F32)
    ranks = []
    for b in range(blocks):
        part = sums[b * owners : (b + 1) * owners]
        ranks.append(
            jnp.sum(jnp.where(hits[b], part[:, :128] + carry, 0.0), axis=0, keepdims=True)
        )
        carry = carry + part[:, 128:]
    rank = jnp.concatenate(ranks, axis=0).astype(I32)
    slot_ref[...] = dev * slots + rank
    line = lambda x: jnp.concatenate([x[b : b + 1] for b in range(blocks)], axis=1)
    place = line(dev * (slots + 1) + rank)
    hit = jnp.concatenate(hits, axis=1)
    tiles = line(tile)
    upper = jnp.where(hit, jnp.broadcast_to(tiles >> 5, (owners, count)), 0)
    lower = jnp.where(hit, jnp.broadcast_to(tiles & 31, (owners, count)), 0)
    numbers = jnp.concatenate([upper, lower], axis=0).astype(F32).astype(BF16)
    which = select(jnp.broadcast_to(line(rank), (128, count)) == iota((128, count), 0))
    ids = lax.dot_general(
        numbers, which, (((1,), (1,)), ((), ())), preferred_element_type=F32
    )
    none = jnp.zeros((near, 128), F32)
    for ref in (ids_ref, rims_ref):
        ref[:near] = none
        ref[near + owners :] = none
    ids_ref[near : near + owners] = ids[:owners] * 32.0 + ids[owners:]
    for copy in copies[2:]:
        copy.wait()
    er = er_ref[...]
    ei = ei_ref[...]
    high, low = halves(sg_ref[...] * (er * er + ei * ei))
    pair_ref[:, :128] = high
    pair_ref[:, 128:] = low
    part = 2 * near
    step = part * (slots + 1)
    lane = iota((part, 128), 1)
    own_at, left_at, right_at = (4 * slots + k * slots for k in range(3))
    writes = []
    for c in range(owners // part + 1):
        if c < owners // part:
            mask = jnp.broadcast_to(place, (step, count)) == iota((step, count), 0) + c * step
            send_ref[c * step : (c + 1) * step, :] = joined(
                jnp.dot(select(mask), pair_ref[...], preferred_element_type=F32)
            )
            rims = jnp.zeros((part, 128), F32)
            for r in range(slots):
                values = send_ref[pl.ds(c * step + r, part, stride=slots + 1), :]
                rims = jnp.where(lane >> 2 == r, pltpu.roll(values, 2 + 4 * r, 1), rims)
            rims_ref[near + c * part : near + (c + 1) * part] = rims
        if c > 0:
            at = (c - 1) * part
            left, own, right = (slice(at + k * near, at + k * near + part) for k in range(3))
            info = jnp.where(lane & 3 < 2, rims_ref[left], rims_ref[right])
            info = jnp.where(lane >= own_at, pltpu.roll(ids_ref[own], own_at, 1), info)
            info = jnp.where(lane >= left_at, pltpu.roll(ids_ref[left], left_at, 1), info)
            info = jnp.where(lane >= right_at, pltpu.roll(ids_ref[right], right_at, 1), info)
            send_ref[pl.ds((c - 1) * step + slots, part, stride=slots + 1), :] = info
            span = pl.ds((c - 1) * step, step)
            write = pltpu.make_async_copy(send_ref.at[span], out_ref.at[span], out_sems.at[c - 1])
            write.start()
            writes.append(write)
    for write in writes:
        write.wait()


def route(dev, tile, er, ei, sg, owners, slots, rows, near):
    count = er.shape[0]
    return pl.pallas_call(
        functools.partial(route_kernel, owners, slots, rows, near),
        out_shape=(
            jax.ShapeDtypeStruct((owners * (slots + 1), 128), F32),
            jax.ShapeDtypeStruct((count // 128, 128), I32),
        ),
        in_specs=[pl.BlockSpec(memory_space=pltpu.HBM)] * 5,
        out_specs=(pl.BlockSpec(memory_space=pltpu.HBM), pl.BlockSpec(memory_space=pltpu.VMEM)),
        scratch_shapes=[
            pltpu.VMEM((count // 128, 128), I32),
            pltpu.VMEM((count // 128, 128), I32),
            pltpu.VMEM((count, 128), F32),
            pltpu.VMEM((count, 128), F32),
            pltpu.VMEM((count, 128), F32),
            pltpu.VMEM((count, 256), BF16),
            pltpu.VMEM((owners * (slots + 1), 128), F32),
            pltpu.VMEM((owners + 2 * near, 128), F32),
            pltpu.VMEM((owners + 2 * near, 128), F32),
            pltpu.SemaphoreType.DMA((5,)),
            pltpu.SemaphoreType.DMA((owners // (2 * near),)),
        ],
        compiler_params=pltpu.CompilerParams(vmem_limit_bytes=16 << 20),
        name="route",
    )(*pinned(dev.reshape(count // 128, 128), tile.reshape(count // 128, 128), er, ei, sg))


def source(t, a, g, heat):
    return t * (1.0 - 4.0 * a) + g * heat


def places(flat, first, slots):
    return jnp.concatenate([flat[first + r : first + r + 1] for r in range(slots)], axis=1)


def side_columns(flat, slots, row, last):
    rows = row.shape[0]
    left, right = (places(flat, k * slots, slots) for k in (5, 6))
    sums = []
    for k, ids in enumerate((left - last, left - last, right, right)):
        value = jnp.concatenate([flat[4 * r + k : 4 * r + k + 1] for r in range(slots)], axis=1)
        hit = jnp.broadcast_to(ids, row.shape) == row
        sums.append(jnp.sum(jnp.where(hit, jnp.broadcast_to(value, row.shape), 0.0), axis=1, keepdims=True))
    lane = iota((rows, 128), 1)
    out = jnp.zeros((rows, 128), F32)
    for at, x in zip((126, 127, 0, 1), sums):
        out = jnp.where(lane == at, jnp.broadcast_to(x, (rows, 128)), out)
    return out


def all_side_columns(flat, slots, rows, last):
    wide = slots * flat.shape[1]
    left, right = (places(flat, k * slots, slots).astype(I32) for k in (5, 6))
    left = left - last
    value = jnp.concatenate([flat[4 * r : 4 * r + 4] for r in range(slots)], axis=1)
    high = value.astype(BF16).astype(F32)
    value = jnp.concatenate([high, value - high], axis=0)
    pick = lambda x: jnp.broadcast_to(x, (8, wide))
    group = jnp.where(iota((8, wide), 0) & 3 < 2, pick(left >> 4), pick(right >> 4))
    spread = [jnp.where(group == k, value, 0.0) for k in range(rows // 16)]
    spread = jnp.concatenate(spread, axis=0).astype(BF16)
    pick = lambda x: jnp.broadcast_to(x & 15, (16, wide)) == iota((16, wide), 0)
    within = jnp.concatenate([select(pick(left)), select(pick(right))], axis=0)
    sums = lax.dot_general(
        within, spread, (((1,), (1,)), ((), ())), preferred_element_type=F32
    )
    sums = sums + pltpu.roll(sums, 124, 1)
    lane = iota((16, 128), 1)
    sums = jnp.where(lane & 3 < 2, sums[:16], sums[16:])
    ends = (lane >= 126) | (lane < 2)
    parts = [jnp.where(ends, pltpu.roll(sums, 126 - 8 * k, 1), 0.0) for k in range(rows // 16)]
    return jnp.concatenate(parts, axis=0)


def rims_kernel(owners, slots, got_ref, ext_ref, pair_ref, flat_ref, ids_ref, first_ref, second_ref):
    rows = ext_ref.shape[1]
    groups = ext_ref.shape[2] // 128 - 1
    info = got_ref[pl.ds(slots, owners, stride=slots + 1), :]
    ids_ref[...] = info.astype(I32)
    flat = info.T
    flat_ref[...] = flat
    for r in range(slots):
        span = slice(r * owners, (r + 1) * owners)
        high, low = halves(got_ref[pl.ds(r, owners, stride=slots + 1), :])
        pair_ref[span, :128] = high
        pair_ref[span, 128:] = low
    own = places(flat, 4 * slots, slots)
    shape = (8 * groups, owners * slots)
    line = iota(shape, 0)
    row = line & 7
    row = row + jnp.where(row < 4, 0, rows - 8)
    mask = jnp.broadcast_to(own, shape) == ((line >> 3) * rows + row).astype(F32)
    heat = joined(jnp.dot(select(mask), pair_ref[...], preferred_element_type=F32))
    side = side_columns(flat, slots, row[:8].astype(F32), (groups - 1) * rows)
    edges = []
    for at, rim in ((0, slice(0, 4)), (4, slice(rows - 4, rows))):
        loss = [heat[8 * q + at : 8 * q + at + 4] for q in range(groups)] + [side[at : at + 4]]
        t, a = ext_ref[0, rim], ext_ref[1, rim]
        edges.append((t, a, source(t, a, ext_ref[2, rim], jnp.concatenate(loss, axis=1))))
    for k in range(3):
        span = slice(4 * k, 4 * k + 4)
        first_ref[span], second_ref[span] = to_send(edges[0][k], edges[1][k], "th")


def rims(got, ext, owners, slots):
    strip = jax.ShapeDtypeStruct((12, ext.shape[2]), F32)
    return pl.pallas_call(
        functools.partial(rims_kernel, owners, slots),
        out_shape=(
            jax.ShapeDtypeStruct((owners * slots, 256), BF16),
            jax.ShapeDtypeStruct((128, owners), F32),
            jax.ShapeDtypeStruct((owners, 128), I32),
            strip,
            strip,
        ),
        compiler_params=pltpu.CompilerParams(vmem_limit_bytes=16 << 20),
        name="rims",
    )(got, ext)


def around(x):
    rows, cols = x.shape
    return (
        pltpu.roll(x, 1, 0) + pltpu.roll(x, rows - 1, 0)
    ) + (pltpu.roll(x, 1, 1) + pltpu.roll(x, cols - 1, 1))


def strips_kernel(width, t_hbm, hc_hbm, c_hbm, first_ref, second_ref, parts_ref, sems):
    cols = t_hbm.shape[1]
    copies = []
    for k, ref in enumerate((t_hbm, hc_hbm, c_hbm)):
        for side, at in enumerate((0, cols - 128)):
            copies.append(
                pltpu.make_async_copy(
                    ref.at[:, pl.ds(at, 128)], parts_ref.at[2 * k + side], sems.at[2 * k + side]
                )
            )
    for copy in copies:
        copy.start()
    for k in range(3):
        span = slice(RIM * k, RIM * k + RIM)
        copies[2 * k].wait()
        copies[2 * k + 1].wait()
        low = parts_ref[2 * k].T[:RIM]
        high = pltpu.roll(parts_ref[2 * k + 1].T[128 - RIM :], width, 0)
        first_ref[span], second_ref[span] = to_send(low, high, "em")


def strips(t, hc, c, width):
    shape = jax.ShapeDtypeStruct((3 * RIM, t.shape[0]), F32)
    return pl.pallas_call(
        functools.partial(strips_kernel, width),
        out_shape=(shape, shape),
        in_specs=[pl.BlockSpec(memory_space=pltpu.HBM)] * 3,
        scratch_shapes=[pltpu.VMEM((6, t.shape[0], 128), F32), pltpu.SemaphoreType.DMA((6,))],
        compiler_params=pltpu.CompilerParams(vmem_limit_bytes=16 << 20),
        name="strips",
    )(t, hc, c)


def sides(left, right, width, rows):
    lane = iota((rows, 128), 1)
    none = jnp.zeros((128 - RIM, rows), F32)
    left, right = (jnp.concatenate([x, none], axis=0).T for x in (left, right))
    left = pltpu.roll(left, 128 - width, 1)
    return jnp.where(lane >= 128 - width, left, jnp.where(lane < width, right, 0.0))


def prepare_kernel(width, count, t_ref, hc_ref, c_ref, first_ref, second_ref, ext_ref):
    rows, cols = t_ref.shape
    left, right = received(first_ref[...], second_ref[...], "em", count)
    for k, ref in enumerate((t_ref, hc_ref, c_ref)):
        span = slice(RIM * k, RIM * k + RIM)
        ext_ref[k, :, :cols] = ref[...]
        ext_ref[k, :, cols:] = sides(left[span], right[span], width, rows)
    hc = ext_ref[1]
    c = ext_ref[2]
    diag = hc + 4.0 * c
    g = jnp.where(diag > 0.0, 1.0 / jnp.where(diag > 0.0, diag, 1.0), 0.0)
    ext_ref[1] = c * g
    ext_ref[2] = g


def prepare(t, hc, c, first, second, width):
    rows, cols = t.shape
    return pl.pallas_call(
        functools.partial(prepare_kernel, width, lax.axis_size("em")),
        out_shape=jax.ShapeDtypeStruct((3, rows, cols + SIDE), F32),
        compiler_params=pltpu.CompilerParams(vmem_limit_bytes=16 << 20),
        name="prepare",
    )(t, hc, c, first, second)


def middle_kernel(sweeps, slots, pair_ref, flat_ref, ids_ref, ext_ref, out_ref, top_ref, bottom_ref, reply_ref, rhs_ref, temp_ref, tiles_ref, sems):
    rows, cols = out_ref.shape
    owners = ids_ref.shape[0]
    groups = cols // 128
    flat = flat_ref[...]
    own = places(flat, 4 * slots, slots)
    shape = (rows, own.shape[1])
    row = iota(shape, 0).astype(F32)
    match = lambda x, first: select(jnp.broadcast_to(x - first, shape) == row)
    for q in (groups, *range(groups)):
        span = slice(q * 128, (q + 1) * 128)
        if q == groups:
            heat = all_side_columns(flat, slots, rows, (groups - 1) * rows)
        else:
            heat = joined(jnp.dot(match(own, q * rows), pair_ref[...], preferred_element_type=F32))
        rhs_ref[:, span] = source(ext_ref[0, :, span], ext_ref[1, :, span], ext_ref[2, :, span], heat)
    for k, ref in enumerate((ext_ref.at[0], ext_ref.at[1], rhs_ref)):
        top_ref[k] = ref[: 2 * RIM]
        bottom_ref[k] = ref[rows - 2 * RIM :]
    temp = ext_ref[0]
    for _ in range(sweeps):
        temp = rhs_ref[...] + ext_ref[1] * around(temp)
    temp_ref[...] = temp[:, :cols]
    inside = pl.ds(RIM, rows - 2 * RIM)
    write = pltpu.make_async_copy(temp_ref.at[inside], out_ref.at[inside], sems.at[0])
    write.start()
    row = iota((rows, 128), 0)
    inner = (row >= RIM) & (row < rows - RIM)
    for q in range(groups):
        high, low = halves(jnp.where(inner, temp[:, q * 128 : (q + 1) * 128], 0.0))
        tiles_ref[q * rows : (q + 1) * rows, :128] = high
        tiles_ref[q * rows : (q + 1) * rows, 128:] = low
    for r in range(0, slots, 4):
        column = slot_columns(ids_ref[...], 4 * slots + r, owners)
        mask = jnp.concatenate(
            [column == iota((4 * owners, 128), 1) + 128 * k for k in range(rows * groups // 128)], axis=1
        )
        reply_ref[r * owners : (r + 4) * owners] = joined(
            jnp.dot(select(mask), tiles_ref[...], preferred_element_type=F32)
        )
    write.wait()


def slot_columns(ids, first, owners):
    return jnp.concatenate(
        [jnp.broadcast_to(ids[:, k : k + 1], (owners, 128)) for k in range(first, first + 4)], axis=0
    )


def middle(pair, flat, ids, ext, cols, sweeps, slots):
    _, rows, wide = ext.shape
    strip = jax.ShapeDtypeStruct((3, 2 * RIM, wide), F32)
    onchip = pl.BlockSpec(memory_space=pltpu.VMEM)
    return pl.pallas_call(
        functools.partial(middle_kernel, sweeps, slots),
        out_shape=(
            jax.ShapeDtypeStruct((rows, cols), F32),
            strip,
            strip,
            jax.ShapeDtypeStruct((slots * ids.shape[0], 128), F32),
        ),
        out_specs=(pl.BlockSpec(memory_space=pltpu.HBM), onchip, onchip, onchip),
        scratch_shapes=[
            pltpu.VMEM((rows, wide), F32),
            pltpu.VMEM((rows, cols), F32),
            pltpu.VMEM((rows * cols // 128, 256), BF16),
            pltpu.SemaphoreType.DMA((1,)),
        ],
        compiler_params=pltpu.CompilerParams(vmem_limit_bytes=16 << 20),
        name="middle",
    )(pair, flat, ids, ext)


def solve_kernel(sweeps, slots, count, first_ref, second_ref, top_ref, bottom_ref, ids_ref, part_ref, inner_ref, out_ref, reply_ref, temp_ref, tiles_ref, sems):
    rows, cols = out_ref.shape
    owners = ids_ref.shape[0]
    groups = cols // 128
    none = jnp.zeros((4, top_ref.shape[2]), F32)
    above, below = received(first_ref[...], second_ref[...], "th", count)
    writes, edges = [], []
    for k, (strip, ref) in enumerate(((above, top_ref), (below, bottom_ref))):
        t, a, r = (
            jnp.concatenate(
                [none, strip[4 * j : 4 * j + 4], ref[j]] if k == 0 else [ref[j], strip[4 * j : 4 * j + 4], none],
                axis=0,
            )
            for j in range(3)
        )
        for _ in range(sweeps):
            t = r + a * around(t)
        t = t[RIM : 2 * RIM, :cols]
        edges.append(t)
        temp_ref[k] = t
        write = pltpu.make_async_copy(
            temp_ref.at[k], out_ref.at[pl.ds(k * (rows - RIM), RIM)], sems.at[k]
        )
        write.start()
        writes.append(write)
    for q in range(128 // (2 * RIM)):
        both = jnp.zeros((2 * RIM, 128), F32)
        if q < groups:
            both = jnp.concatenate([t[:, q * 128 : (q + 1) * 128] for t in edges], axis=0)
        high, low = halves(both)
        tiles_ref[2 * RIM * q : 2 * RIM * (q + 1), :128] = high
        tiles_ref[2 * RIM * q : 2 * RIM * (q + 1), 128:] = low
    ids = ids_ref[...]
    bits = rows.bit_length() - 1
    row = ids & (rows - 1)
    line = jnp.where(row < RIM, row, jnp.where(row >= rows - RIM, row - (rows - 2 * RIM), -128))
    code = (ids >> bits) * (2 * RIM) + line
    lane = iota((4 * owners, 128), 1)
    for r in range(0, slots, 4):
        mask = slot_columns(code, 4 * slots + r, owners) == lane
        got = part_ref[r * owners : (r + 4) * owners] + joined(
            jnp.dot(select(mask), tiles_ref[...], preferred_element_type=F32)
        )
        for k in range(4):
            reply_ref[pl.ds(r + k, owners, stride=slots), :] = got[k * owners : (k + 1) * owners]
    for write in writes:
        write.wait()


def solve(first, second, top, bottom, ids, part, inner, sweeps, owners, slots):
    rows, cols = inner.shape
    onchip = pl.BlockSpec(memory_space=pltpu.VMEM)
    return pl.pallas_call(
        functools.partial(solve_kernel, sweeps, slots, lax.axis_size("th")),
        out_shape=(
            jax.ShapeDtypeStruct((rows, cols), F32),
            jax.ShapeDtypeStruct((owners * slots, 128), F32),
        ),
        in_specs=[onchip] * 6 + [pl.BlockSpec(memory_space=pltpu.HBM)],
        out_specs=(pl.BlockSpec(memory_space=pltpu.HBM), onchip),
        scratch_shapes=[
            pltpu.VMEM((2, RIM, cols), F32),
            pltpu.VMEM((128, 256), BF16),
            pltpu.SemaphoreType.DMA((2,)),
        ],
        input_output_aliases={6: 0},
        compiler_params=pltpu.CompilerParams(vmem_limit_bytes=16 << 20),
        name="solve",
    )(first, second, top, bottom, ids, part, inner)


def final_kernel(slot_ref, back_ref, sg_ref, tc_ref, out_ref, pair_ref, new_ref, sems):
    total = back_ref.shape[0]
    blocks = slot_ref.shape[0]
    high, low = halves(back_ref[...])
    pair_ref[:, :128] = high
    pair_ref[:, 128:] = low
    slot = slot_ref[...].T
    writes = []
    for b in range(0, blocks, 2):
        column = jnp.concatenate(
            [jnp.broadcast_to(slot[:, k : k + 1], (128, 128)) for k in range(b, b + 2)], axis=0
        )
        mask = jnp.concatenate(
            [column == iota((256, 128), 1) + 128 * k for k in range(total // 128)], axis=1
        )
        hot = joined(jnp.dot(select(mask), pair_ref[...], preferred_element_type=F32))
        span = pl.ds(b * 128, 256)
        new_ref[span, :] = sg_ref[span, :] / (1.0 + tc_ref[span, :] * hot)
        write = pltpu.make_async_copy(new_ref.at[span], out_ref.at[span], sems.at[b // 2])
        write.start()
        writes.append(write)
    for write in writes:
        write.wait()


def final(slot, back, sg, tc):
    return pl.pallas_call(
        final_kernel,
        out_shape=jax.ShapeDtypeStruct(sg.shape, F32),
        out_specs=pl.BlockSpec(memory_space=pltpu.HBM),
        scratch_shapes=[
            pltpu.VMEM((back.shape[0], 256), BF16),
            pltpu.VMEM(sg.shape, F32),
            pltpu.SemaphoreType.DMA((slot.shape[0] // 2,)),
        ],
        compiler_params=pltpu.CompilerParams(vmem_limit_bytes=16 << 20),
        name="final",
    )(slot, back, sg, tc)


def traded(first, second, axis):
    n_em, n_th = lax.axis_size("em"), lax.axis_size("th")
    near, far = [], []
    for e in range(n_em):
        for t in range(n_th):
            if axis == "em":
                mate = (e + 1 if e % 2 else e - 1) % n_em, t
                close = e ^ 1, t
            else:
                mate = e, t + 1 if t % 2 else t - 1
                mate = mate if 0 <= mate[1] < n_th else (e ^ 1, t)
                close = e, t ^ 1
            near.append((e * n_th + t, close[0] * n_th + close[1]))
            far.append((e * n_th + t, mate[0] * n_th + mate[1]))
    return lax.ppermute(first, ("em", "th"), near), lax.ppermute(second, ("em", "th"), far)


def exchanged(x, owners):
    rows = x.shape[0]
    x = x.reshape(owners, 1, rows // owners * 128)
    x = lax.all_to_all(x, ("em", "th"), split_axis=0, concat_axis=0, tiled=True)
    return x.reshape(rows, 128)


SWEEPS = 3


def pinned(*arrays):
    return [pltpu.with_memory_space_constraint(x, pltpu.HBM) for x in arrays]


def local(e_real, e_imag, sigma_em, temp_coef, dest_dev, dest_tile, t_old, heat_cap, conduct):
    owners = lax.axis_size("em") * lax.axis_size("th")
    slots = 2 * e_real.shape[0] // owners
    rows, cols = t_old.shape
    near = lax.axis_size("th")
    send, slot = route(dest_dev, dest_tile, e_real, e_imag, sigma_em, owners, slots, rows, near)
    got = exchanged(send, owners)
    grid = pinned(*lax.optimization_barrier((t_old, heat_cap, conduct, slot))[:3])
    ext = prepare(*grid, *traded(*strips(*grid, SWEEPS), "em"), SWEEPS)
    pair, flat, ids, first, second = rims(got, ext, owners, slots)
    first, second = traded(first, second, "th")
    inner, top, bottom, part = middle(pair, flat, ids, ext, cols, SWEEPS, slots)
    (inner,) = pinned(inner)
    temp, reply = solve(first, second, top, bottom, ids, part, inner, SWEEPS, owners, slots)
    back = exchanged(reply, owners)
    return temp, final(slot, back, sigma_em, temp_coef)


def solution(mesh):
    tiles = P(("em", "th"), None)
    grid = P("th", "em")
    return jax.shard_map(
        local,
        mesh=mesh,
        in_specs=(tiles,) * 6 + (grid,) * 3,
        out_specs=(grid, tiles),
        check_vma=False,
    )
```

```python
import functools
import jax
import jax.numpy as jnp
from jax import lax
from jax.experimental import pallas as pl
from jax.experimental.pallas import tpu as pltpu
from jax.sharding import PartitionSpec as P

F32 = jnp.float32
BF16 = jnp.bfloat16
I32 = jnp.int32
RIM = 8
SIDE = 128


def iota(shape, dim):
    return lax.broadcasted_iota(I32, shape, dim)


def to_send(low, high, axis):
    even = lax.axis_index(axis) % 2 == 0
    return jnp.where(even, high, low), jnp.where(even, low, high)


def received(first, second, axis, count):
    me = lax.axis_index(axis)
    even = me % 2 == 0
    low = jnp.where(me > 0, jnp.where(even, second, first), 0.0)
    high = jnp.where(me < count - 1, jnp.where(even, first, second), 0.0)
    return low, high


def halves(x):
    high = x.astype(BF16)
    low = (x - high.astype(F32)).astype(BF16)
    return high, low


def select(mask):
    return jnp.where(mask, 1.0, 0.0).astype(BF16)


def joined(y):
    return y[:, :128] + y[:, 128:]


def route_kernel(owners, slots, rows, near, dev_hbm, tile_hbm, er_hbm, ei_hbm, sg_hbm, out_ref, slot_ref, dev_ref, tile_ref, er_ref, ei_ref, sg_ref, pair_ref, send_ref, ids_ref, rims_ref, sems, out_sems):
    count = er_ref.shape[0]
    blocks = count // 128
    copies = [
        pltpu.make_async_copy(source, target, sems.at[k])
        for k, (source, target) in enumerate(
            (
                (dev_hbm, dev_ref),
                (tile_hbm, tile_ref),
                (er_hbm, er_ref),
                (ei_hbm, ei_ref),
                (sg_hbm, sg_ref),
            )
        )
    ]
    for copy in copies:
        copy.start()
    copies[0].wait()
    copies[1].wait()
    dev = dev_ref[...]
    tile = tile_ref[...]
    tile = (tile & 3) * rows + (tile >> 2)
    hits = [jnp.broadcast_to(dev[b : b + 1], (owners, 128)) == iota((owners, 128), 0) for b in range(blocks)]
    ahead = select(iota((128, 256), 0) < iota((128, 256), 1))
    sums = jnp.dot(
        jnp.concatenate([select(h) for h in hits], axis=0), ahead, preferred_element_type=F32
    )
    carry = jnp.zeros((owners, 128), F32)
    ranks = []
    for b in range(blocks):
        part = sums[b * owners : (b + 1) * owners]
        ranks.append(
            jnp.sum(jnp.where(hits[b], part[:, :128] + carry, 0.0), axis=0, keepdims=True)
        )
        carry = carry + part[:, 128:]
    rank = jnp.concatenate(ranks, axis=0).astype(I32)
    slot_ref[...] = dev * slots + rank
    line = lambda x: jnp.concatenate([x[b : b + 1] for b in range(blocks)], axis=1)
    place = line(dev * (slots + 1) + rank)
    hit = jnp.concatenate(hits, axis=1)
    tiles = line(tile)
    upper = jnp.where(hit, jnp.broadcast_to(tiles >> 5, (owners, count)), 0)
    lower = jnp.where(hit, jnp.broadcast_to(tiles & 31, (owners, count)), 0)
    numbers = jnp.concatenate([upper, lower], axis=0).astype(F32).astype(BF16)
    which = select(jnp.broadcast_to(line(rank), (128, count)) == iota((128, count), 0))
    ids = lax.dot_general(
        numbers, which, (((1,), (1,)), ((), ())), preferred_element_type=F32
    )
    none = jnp.zeros((near, 128), F32)
    for ref in (ids_ref, rims_ref):
        ref[:near] = none
        ref[near + owners :] = none
    ids_ref[near : near + owners] = ids[:owners] * 32.0 + ids[owners:]
    for copy in copies[2:]:
        copy.wait()
    er = er_ref[...]
    ei = ei_ref[...]
    high, low = halves(sg_ref[...] * (er * er + ei * ei))
    pair_ref[:, :128] = high
    pair_ref[:, 128:] = low
    part = 2 * near
    step = part * (slots + 1)
    lane = iota((part, 128), 1)
    own_at, left_at, right_at = (4 * slots + k * slots for k in range(3))
    writes = []
    for c in range(owners // part + 1):
        if c < owners // part:
            mask = jnp.broadcast_to(place, (step, count)) == iota((step, count), 0) + c * step
            send_ref[c * step : (c + 1) * step, :] = joined(
                jnp.dot(select(mask), pair_ref[...], preferred_element_type=F32)
            )
            rims = jnp.zeros((part, 128), F32)
            for r in range(slots):
                values = send_ref[pl.ds(c * step + r, part, stride=slots + 1), :]
                rims = jnp.where(lane >> 2 == r, pltpu.roll(values, 2 + 4 * r, 1), rims)
            rims_ref[near + c * part : near + (c + 1) * part] = rims
        if c > 0:
            at = (c - 1) * part
            left, own, right = (slice(at + k * near, at + k * near + part) for k in range(3))
            info = jnp.where(lane & 3 < 2, rims_ref[left], rims_ref[right])
            info = jnp.where(lane >= own_at, pltpu.roll(ids_ref[own], own_at, 1), info)
            info = jnp.where(lane >= left_at, pltpu.roll(ids_ref[left], left_at, 1), info)
            info = jnp.where(lane >= right_at, pltpu.roll(ids_ref[right], right_at, 1), info)
            send_ref[pl.ds((c - 1) * step + slots, part, stride=slots + 1), :] = info
            span = pl.ds((c - 1) * step, step)
            write = pltpu.make_async_copy(send_ref.at[span], out_ref.at[span], out_sems.at[c - 1])
            write.start()
            writes.append(write)
    for write in writes:
        write.wait()


def route(dev, tile, er, ei, sg, owners, slots, rows, near):
    count = er.shape[0]
    return pl.pallas_call(
        functools.partial(route_kernel, owners, slots, rows, near),
        out_shape=(
            jax.ShapeDtypeStruct((owners * (slots + 1), 128), F32),
            jax.ShapeDtypeStruct((count // 128, 128), I32),
        ),
        in_specs=[pl.BlockSpec(memory_space=pltpu.HBM)] * 5,
        out_specs=(pl.BlockSpec(memory_space=pltpu.HBM), pl.BlockSpec(memory_space=pltpu.VMEM)),
        scratch_shapes=[
            pltpu.VMEM((count // 128, 128), I32),
            pltpu.VMEM((count // 128, 128), I32),
            pltpu.VMEM((count, 128), F32),
            pltpu.VMEM((count, 128), F32),
            pltpu.VMEM((count, 128), F32),
            pltpu.VMEM((count, 256), BF16),
            pltpu.VMEM((owners * (slots + 1), 128), F32),
            pltpu.VMEM((owners + 2 * near, 128), F32),
            pltpu.VMEM((owners + 2 * near, 128), F32),
            pltpu.SemaphoreType.DMA((5,)),
            pltpu.SemaphoreType.DMA((owners // (2 * near),)),
        ],
        compiler_params=pltpu.CompilerParams(vmem_limit_bytes=16 << 20),
        name="route",
    )(*pinned(dev.reshape(count // 128, 128), tile.reshape(count // 128, 128), er, ei, sg))


def source(t, a, g, heat):
    return t * (1.0 - 4.0 * a) + g * heat


def places(flat, first, slots):
    return jnp.concatenate([flat[first + r : first + r + 1] for r in range(slots)], axis=1)


def side_columns(flat, slots, row, last):
    rows = row.shape[0]
    left, right = (places(flat, k * slots, slots) for k in (5, 6))
    sums = []
    for k, ids in enumerate((left - last, left - last, right, right)):
        value = jnp.concatenate([flat[4 * r + k : 4 * r + k + 1] for r in range(slots)], axis=1)
        hit = jnp.broadcast_to(ids, row.shape) == row
        sums.append(jnp.sum(jnp.where(hit, jnp.broadcast_to(value, row.shape), 0.0), axis=1, keepdims=True))
    lane = iota((rows, 128), 1)
    out = jnp.zeros((rows, 128), F32)
    for at, x in zip((126, 127, 0, 1), sums):
        out = jnp.where(lane == at, jnp.broadcast_to(x, (rows, 128)), out)
    return out


def all_side_columns(flat, slots, rows, last):
    wide = slots * flat.shape[1]
    left, right = (places(flat, k * slots, slots).astype(I32) for k in (5, 6))
    left = left - last
    value = jnp.concatenate([flat[4 * r : 4 * r + 4] for r in range(slots)], axis=1)
    high = value.astype(BF16).astype(F32)
    value = jnp.concatenate([high, value - high], axis=0)
    pick = lambda x: jnp.broadcast_to(x, (8, wide))
    group = jnp.where(iota((8, wide), 0) & 3 < 2, pick(left >> 4), pick(right >> 4))
    spread = [jnp.where(group == k, value, 0.0) for k in range(rows // 16)]
    spread = jnp.concatenate(spread, axis=0).astype(BF16)
    pick = lambda x: jnp.broadcast_to(x & 15, (16, wide)) == iota((16, wide), 0)
    within = jnp.concatenate([select(pick(left)), select(pick(right))], axis=0)
    sums = lax.dot_general(
        within, spread, (((1,), (1,)), ((), ())), preferred_element_type=F32
    )
    sums = sums + pltpu.roll(sums, 124, 1)
    lane = iota((16, 128), 1)
    sums = jnp.where(lane & 3 < 2, sums[:16], sums[16:])
    ends = (lane >= 126) | (lane < 2)
    parts = [jnp.where(ends, pltpu.roll(sums, 126 - 8 * k, 1), 0.0) for k in range(rows // 16)]
    return jnp.concatenate(parts, axis=0)


def rims_kernel(owners, slots, got_ref, ext_ref, pair_ref, flat_ref, ids_ref, first_ref, second_ref):
    rows = ext_ref.shape[1]
    groups = ext_ref.shape[2] // 128 - 1
    info = got_ref[pl.ds(slots, owners, stride=slots + 1), :]
    ids_ref[...] = info.astype(I32)
    flat = info.T
    flat_ref[...] = flat
    for r in range(slots):
        span = slice(r * owners, (r + 1) * owners)
        high, low = halves(got_ref[pl.ds(r, owners, stride=slots + 1), :])
        pair_ref[span, :128] = high
        pair_ref[span, 128:] = low
    own = places(flat, 4 * slots, slots)
    shape = (8 * groups, owners * slots)
    line = iota(shape, 0)
    row = line & 7
    row = row + jnp.where(row < 4, 0, rows - 8)
    mask = jnp.broadcast_to(own, shape) == ((line >> 3) * rows + row).astype(F32)
    heat = joined(jnp.dot(select(mask), pair_ref[...], preferred_element_type=F32))
    side = side_columns(flat, slots, row[:8].astype(F32), (groups - 1) * rows)
    edges = []
    for at, rim in ((0, slice(0, 4)), (4, slice(rows - 4, rows))):
        loss = [heat[8 * q + at : 8 * q + at + 4] for q in range(groups)] + [side[at : at + 4]]
        t, a = ext_ref[0, rim], ext_ref[1, rim]
        edges.append((t, a, source(t, a, ext_ref[2, rim], jnp.concatenate(loss, axis=1))))
    for k in range(3):
        span = slice(4 * k, 4 * k + 4)
        first_ref[span], second_ref[span] = to_send(edges[0][k], edges[1][k], "th")


def rims(got, ext, owners, slots):
    strip = jax.ShapeDtypeStruct((12, ext.shape[2]), F32)
    return pl.pallas_call(
        functools.partial(rims_kernel, owners, slots),
        out_shape=(
            jax.ShapeDtypeStruct((owners * slots, 256), BF16),
            jax.ShapeDtypeStruct((128, owners), F32),
            jax.ShapeDtypeStruct((owners, 128), I32),
            strip,
            strip,
        ),
        compiler_params=pltpu.CompilerParams(vmem_limit_bytes=16 << 20),
        name="rims",
    )(got, ext)


def around(x):
    rows, cols = x.shape
    return (
        pltpu.roll(x, 1, 0) + pltpu.roll(x, rows - 1, 0)
    ) + (pltpu.roll(x, 1, 1) + pltpu.roll(x, cols - 1, 1))


def strips_kernel(width, t_hbm, hc_hbm, c_hbm, first_ref, second_ref, parts_ref, sems):
    cols = t_hbm.shape[1]
    copies = []
    for k, ref in enumerate((t_hbm, hc_hbm, c_hbm)):
        for side, at in enumerate((0, cols - 128)):
            copies.append(
                pltpu.make_async_copy(
                    ref.at[:, pl.ds(at, 128)], parts_ref.at[2 * k + side], sems.at[2 * k + side]
                )
            )
    for copy in copies:
        copy.start()
    for k in range(3):
        span = slice(RIM * k, RIM * k + RIM)
        copies[2 * k].wait()
        copies[2 * k + 1].wait()
        low = parts_ref[2 * k].T[:RIM]
        high = pltpu.roll(parts_ref[2 * k + 1].T[128 - RIM :], width, 0)
        first_ref[span], second_ref[span] = to_send(low, high, "em")


def strips(t, hc, c, width):
    shape = jax.ShapeDtypeStruct((3 * RIM, t.shape[0]), F32)
    return pl.pallas_call(
        functools.partial(strips_kernel, width),
        out_shape=(shape, shape),
        in_specs=[pl.BlockSpec(memory_space=pltpu.HBM)] * 3,
        scratch_shapes=[pltpu.VMEM((6, t.shape[0], 128), F32), pltpu.SemaphoreType.DMA((6,))],
        compiler_params=pltpu.CompilerParams(vmem_limit_bytes=16 << 20),
        name="strips",
    )(t, hc, c)


def sides(left, right, width, rows):
    lane = iota((rows, 128), 1)
    none = jnp.zeros((128 - RIM, rows), F32)
    left, right = (jnp.concatenate([x, none], axis=0).T for x in (left, right))
    left = pltpu.roll(left, 128 - width, 1)
    return jnp.where(lane >= 128 - width, left, jnp.where(lane < width, right, 0.0))


def prepare_kernel(width, count, t_ref, hc_ref, c_ref, first_ref, second_ref, ext_ref):
    rows, cols = t_ref.shape
    left, right = received(first_ref[...], second_ref[...], "em", count)
    for k, ref in enumerate((t_ref, hc_ref, c_ref)):
        span = slice(RIM * k, RIM * k + RIM)
        ext_ref[k, :, :cols] = ref[...]
        ext_ref[k, :, cols:] = sides(left[span], right[span], width, rows)
    hc = ext_ref[1]
    c = ext_ref[2]
    diag = hc + 4.0 * c
    g = jnp.where(diag > 0.0, 1.0 / jnp.where(diag > 0.0, diag, 1.0), 0.0)
    ext_ref[1] = c * g
    ext_ref[2] = g


def prepare(t, hc, c, first, second, width):
    rows, cols = t.shape
    return pl.pallas_call(
        functools.partial(prepare_kernel, width, lax.axis_size("em")),
        out_shape=jax.ShapeDtypeStruct((3, rows, cols + SIDE), F32),
        compiler_params=pltpu.CompilerParams(vmem_limit_bytes=16 << 20),
        name="prepare",
    )(t, hc, c, first, second)


def middle_kernel(sweeps, slots, pair_ref, flat_ref, ids_ref, ext_ref, out_ref, top_ref, bottom_ref, reply_ref, rhs_ref, temp_ref, tiles_ref, sems):
    rows, cols = out_ref.shape
    owners = ids_ref.shape[0]
    groups = cols // 128
    flat = flat_ref[...]
    own = places(flat, 4 * slots, slots)
    shape = (rows, own.shape[1])
    row = iota(shape, 0).astype(F32)
    match = lambda x, first: select(jnp.broadcast_to(x - first, shape) == row)
    for q in (groups, *range(groups)):
        span = slice(q * 128, (q + 1) * 128)
        if q == groups:
            heat = all_side_columns(flat, slots, rows, (groups - 1) * rows)
        else:
            heat = joined(jnp.dot(match(own, q * rows), pair_ref[...], preferred_element_type=F32))
        rhs_ref[:, span] = source(ext_ref[0, :, span], ext_ref[1, :, span], ext_ref[2, :, span], heat)
    for k, ref in enumerate((ext_ref.at[0], ext_ref.at[1], rhs_ref)):
        top_ref[k] = ref[: 2 * RIM]
        bottom_ref[k] = ref[rows - 2 * RIM :]
    temp = ext_ref[0]
    for _ in range(sweeps):
        temp = rhs_ref[...] + ext_ref[1] * around(temp)
    temp_ref[...] = temp[:, :cols]
    inside = pl.ds(RIM, rows - 2 * RIM)
    write = pltpu.make_async_copy(temp_ref.at[inside], out_ref.at[inside], sems.at[0])
    write.start()
    row = iota((rows, 128), 0)
    inner = (row >= RIM) & (row < rows - RIM)
    for q in range(groups):
        high, low = halves(jnp.where(inner, temp[:, q * 128 : (q + 1) * 128], 0.0))
        tiles_ref[q * rows : (q + 1) * rows, :128] = high
        tiles_ref[q * rows : (q + 1) * rows, 128:] = low
    for r in range(0, slots, 4):
        column = slot_columns(ids_ref[...], 4 * slots + r, owners)
        mask = jnp.concatenate(
            [column == iota((4 * owners, 128), 1) + 128 * k for k in range(rows * groups // 128)], axis=1
        )
        reply_ref[r * owners : (r + 4) * owners] = joined(
            jnp.dot(select(mask), tiles_ref[...], preferred_element_type=F32)
        )
    write.wait()


def slot_columns(ids, first, owners):
    return jnp.concatenate(
        [jnp.broadcast_to(ids[:, k : k + 1], (owners, 128)) for k in range(first, first + 4)], axis=0
    )


def middle(pair, flat, ids, ext, cols, sweeps, slots):
    _, rows, wide = ext.shape
    strip = jax.ShapeDtypeStruct((3, 2 * RIM, wide), F32)
    onchip = pl.BlockSpec(memory_space=pltpu.VMEM)
    return pl.pallas_call(
        functools.partial(middle_kernel, sweeps, slots),
        out_shape=(
            jax.ShapeDtypeStruct((rows, cols), F32),
            strip,
            strip,
            jax.ShapeDtypeStruct((slots * ids.shape[0], 128), F32),
        ),
        out_specs=(pl.BlockSpec(memory_space=pltpu.HBM), onchip, onchip, onchip),
        scratch_shapes=[
            pltpu.VMEM((rows, wide), F32),
            pltpu.VMEM((rows, cols), F32),
            pltpu.VMEM((rows * cols // 128, 256), BF16),
            pltpu.SemaphoreType.DMA((1,)),
        ],
        compiler_params=pltpu.CompilerParams(vmem_limit_bytes=16 << 20),
        name="middle",
    )(pair, flat, ids, ext)


def solve_kernel(sweeps, slots, count, first_ref, second_ref, top_ref, bottom_ref, ids_ref, part_ref, inner_ref, out_ref, reply_ref, temp_ref, tiles_ref, sems):
    rows, cols = out_ref.shape
    owners = ids_ref.shape[0]
    groups = cols // 128
    none = jnp.zeros((4, top_ref.shape[2]), F32)
    above, below = received(first_ref[...], second_ref[...], "th", count)
    writes, edges = [], []
    for k, (strip, ref) in enumerate(((above, top_ref), (below, bottom_ref))):
        t, a, r = (
            jnp.concatenate(
                [none, strip[4 * j : 4 * j + 4], ref[j]] if k == 0 else [ref[j], strip[4 * j : 4 * j + 4], none],
                axis=0,
            )
            for j in range(3)
        )
        for _ in range(sweeps):
            t = r + a * around(t)
        t = t[RIM : 2 * RIM, :cols]
        edges.append(t)
        temp_ref[k] = t
        write = pltpu.make_async_copy(
            temp_ref.at[k], out_ref.at[pl.ds(k * (rows - RIM), RIM)], sems.at[k]
        )
        write.start()
        writes.append(write)
    for q in range(128 // (2 * RIM)):
        both = jnp.zeros((2 * RIM, 128), F32)
        if q < groups:
            both = jnp.concatenate([t[:, q * 128 : (q + 1) * 128] for t in edges], axis=0)
        high, low = halves(both)
        tiles_ref[2 * RIM * q : 2 * RIM * (q + 1), :128] = high
        tiles_ref[2 * RIM * q : 2 * RIM * (q + 1), 128:] = low
    ids = ids_ref[...]
    bits = rows.bit_length() - 1
    row = ids & (rows - 1)
    line = jnp.where(row < RIM, row, jnp.where(row >= rows - RIM, row - (rows - 2 * RIM), -128))
    code = (ids >> bits) * (2 * RIM) + line
    lane = iota((4 * owners, 128), 1)
    for r in range(0, slots, 4):
        mask = slot_columns(code, 4 * slots + r, owners) == lane
        got = part_ref[r * owners : (r + 4) * owners] + joined(
            jnp.dot(select(mask), tiles_ref[...], preferred_element_type=F32)
        )
        for k in range(4):
            reply_ref[pl.ds(r + k, owners, stride=slots), :] = got[k * owners : (k + 1) * owners]
    for write in writes:
        write.wait()


def solve(first, second, top, bottom, ids, part, inner, sweeps, owners, slots):
    rows, cols = inner.shape
    onchip = pl.BlockSpec(memory_space=pltpu.VMEM)
    return pl.pallas_call(
        functools.partial(solve_kernel, sweeps, slots, lax.axis_size("th")),
        out_shape=(
            jax.ShapeDtypeStruct((rows, cols), F32),
            jax.ShapeDtypeStruct((owners * slots, 128), F32),
        ),
        in_specs=[onchip] * 6 + [pl.BlockSpec(memory_space=pltpu.HBM)],
        out_specs=(pl.BlockSpec(memory_space=pltpu.HBM), onchip),
        scratch_shapes=[
            pltpu.VMEM((2, RIM, cols), F32),
            pltpu.VMEM((128, 256), BF16),
            pltpu.SemaphoreType.DMA((2,)),
        ],
        input_output_aliases={6: 0},
        compiler_params=pltpu.CompilerParams(vmem_limit_bytes=16 << 20),
        name="solve",
    )(first, second, top, bottom, ids, part, inner)


def final_kernel(slot_ref, back_ref, sg_ref, tc_ref, out_ref, pair_ref, new_ref, sems):
    total = back_ref.shape[0]
    blocks = slot_ref.shape[0]
    high, low = halves(back_ref[...])
    pair_ref[:, :128] = high
    pair_ref[:, 128:] = low
    slot = slot_ref[...].T
    writes = []
    for b in range(blocks):
        column = jnp.broadcast_to(slot[:, b : b + 1], (128, 128))
        mask = jnp.concatenate(
            [column == iota((128, 128), 1) + 128 * k for k in range(total // 128)], axis=1
        )
        hot = joined(jnp.dot(select(mask), pair_ref[...], preferred_element_type=F32))
        span = pl.ds(b * 128, 128)
        new_ref[span, :] = sg_ref[span, :] / (1.0 + tc_ref[span, :] * hot)
        write = pltpu.make_async_copy(new_ref.at[span], out_ref.at[span], sems.at[b])
        write.start()
        writes.append(write)
    for write in writes:
        write.wait()


def final(slot, back, sg, tc):
    return pl.pallas_call(
        final_kernel,
        out_shape=jax.ShapeDtypeStruct(sg.shape, F32),
        out_specs=pl.BlockSpec(memory_space=pltpu.HBM),
        scratch_shapes=[
            pltpu.VMEM((back.shape[0], 256), BF16),
            pltpu.VMEM(sg.shape, F32),
            pltpu.SemaphoreType.DMA((slot.shape[0],)),
        ],
        compiler_params=pltpu.CompilerParams(vmem_limit_bytes=16 << 20),
        name="final",
    )(slot, back, sg, tc)


def traded(first, second, axis):
    n_em, n_th = lax.axis_size("em"), lax.axis_size("th")
    near, far = [], []
    for e in range(n_em):
        for t in range(n_th):
            if axis == "em":
                mate = (e + 1 if e % 2 else e - 1) % n_em, t
                close = e ^ 1, t
            else:
                mate = e, t + 1 if t % 2 else t - 1
                mate = mate if 0 <= mate[1] < n_th else (e ^ 1, t)
                close = e, t ^ 1
            near.append((e * n_th + t, close[0] * n_th + close[1]))
            far.append((e * n_th + t, mate[0] * n_th + mate[1]))
    return lax.ppermute(first, ("em", "th"), near), lax.ppermute(second, ("em", "th"), far)


def exchanged(x, owners):
    rows = x.shape[0]
    x = x.reshape(owners, 1, rows // owners * 128)
    x = lax.all_to_all(x, ("em", "th"), split_axis=0, concat_axis=0, tiled=True)
    return x.reshape(rows, 128)


SWEEPS = 3


def pinned(*arrays):
    return [pltpu.with_memory_space_constraint(x, pltpu.HBM) for x in arrays]


def local(e_real, e_imag, sigma_em, temp_coef, dest_dev, dest_tile, t_old, heat_cap, conduct):
    owners = lax.axis_size("em") * lax.axis_size("th")
    slots = 2 * e_real.shape[0] // owners
    rows, cols = t_old.shape
    near = lax.axis_size("th")
    send, slot = route(dest_dev, dest_tile, e_real, e_imag, sigma_em, owners, slots, rows, near)
    got = exchanged(send, owners)
    grid = pinned(*lax.optimization_barrier((t_old, heat_cap, conduct, slot))[:3])
    ext = prepare(*grid, *traded(*strips(*grid, SWEEPS), "em"), SWEEPS)
    pair, flat, ids, first, second = rims(got, ext, owners, slots)
    first, second = traded(first, second, "th")
    inner, top, bottom, part = middle(pair, flat, ids, ext, cols, SWEEPS, slots)
    (inner,) = pinned(inner)
    temp, reply = solve(first, second, top, bottom, ids, part, inner, SWEEPS, owners, slots)
    back = exchanged(reply, owners)
    return temp, final(slot, back, sigma_em, temp_coef)


def solution(mesh):
    tiles = P(("em", "th"), None)
    grid = P("th", "em")
    return jax.shard_map(
        local,
        mesh=mesh,
        in_specs=(tiles,) * 6 + (grid,) * 3,
        out_specs=(grid, tiles),
        check_vma=False,
    )
```
